32 devices in a mesh: groups: 2 (over y), gx: 4 (over z), gy: 2 (over x), sa: 2 (over core).
Axes of the slice: x: 2, y: 2, z: 4, core: 2. Of those that a mesh axis runs over, the one named last changes fastest.
Arguments:
- initial: float32 [16, 4, 128, 256], P(('groups', 'sa'), None, 'gx', 'gy'), parts along dimension 0, may hold values from -6 to 6
- retard: float32 [16, 4, 128, 256], P(('groups', 'sa'), None, 'gx', 'gy'), parts along dimension 0, may hold values from 0.2 to 0.4
- velx: float32 [16, 4, 128, 256], P(('groups', 'sa'), None, 'gx', 'gy'), parts along dimension 0, may hold values from 0.2 to 1
- vely: float32 [16, 4, 128, 256], P(('groups', 'sa'), None, 'gx', 'gy'), parts along dimension 0, may hold values from 0.2 to 1
- monitor: float32 [8, 128, 256], P('groups', 'gx', 'gy'), parts along dimension 0, may hold values from 0.2 to 1
- controls: float32 [8192], P('groups'), parts along dimension 0, may hold values from -6 to 6
- profile: float32 [8192, 128], P('groups'), parts along dimension 0, may hold values from -4 to 4
- wells: int32 [8192], P('groups'), parts along dimension 0, may hold values from 0 to 1023
- ranking: int32 [16], P(('groups', 'sa')), parts along dimension 0, may hold values from 0 to 7, as said below
Outputs:
- final: float32 [16, 4, 128, 256], P(('groups', 'sa'), None, 'gx', 'gy'), parts along dimension 0
- gradient: float32 [8192], P('groups'), parts along dimension 0
- objective: float32 [2], P('groups'), parts along dimension 0
The draws below stay inside these ranges and needn't reach their ends.
There are 2 independent parts, one for each index of `groups`. The reference program is written for one: setup_inputs(seed, part) draws one part's arguments, and reference() takes and returns one part's arrays. A program takes and returns all parts, laid end to end along the dimension named above; each array names one. Nothing has to cross between parts.
Inputs may be any that keep to these rules, and one draw needn't show every extreme that they name: ranking holds each number from 0 to 7 once.
All inputs are finite; a program needn't handle non-finite values.
Results may differ from the reference program's by a relative error of at most 0.00009.
Values sent between devices are 32-bit elements; how exact they have to be, the bound alone decides.
No kernel may reach another device: no remote copies, remote signals or barrier semaphores. Data moves between devices by JAX's collectives and lax.ppermute only.
A program may use at most 64 MiB of HBM per device.

```python
import math
import jax
import jax.numpy as jnp
from jax import lax

NZ = 4
ITERS = 16
NC = 4096
SCREEN = 128
NX = 128
NY = 256
SAMP = 8
TAILN = 4
ROWS = 1024


def draw_ranking(key, part):
    key = jax.random.fold_in(key, 7)
    return jax.random.permutation(key, SAMP).astype(jnp.int32)


def place_ends(entries, rng, smallest, top_value):
    longest = entries.shape.index(max(entries.shape))
    spots = []
    for shift in (0, 1):
        where = [jax.random.randint(jax.random.fold_in(rng, axis), (), 0, length) for axis, length in enumerate(entries.shape)]
        where[longest] = (where[longest] + shift) % entries.shape[longest]
        spots.append(tuple(where))
    return entries.at[spots[0]].set(smallest).at[spots[1]].set(top_value)


def block_scale(stream_key, shape, shards, low, high):
    factor_of, own = 1.0, jax.random.fold_in(stream_key, 6)
    for position, parts in shards:
        draws = jnp.exp(jax.random.uniform(jax.random.fold_in(own, position), (parts,), jnp.float32, low / len(shards), high / len(shards)))
        factor_of = factor_of * jnp.repeat(draws, shape[position] // parts).reshape([-1 if axis == position else 1 for axis in range(len(shape))])
    return factor_of


def noise(stream_key, shape, spread, bound, shards=(), held_as=jnp.bfloat16):
    values = jax.random.normal(stream_key, shape, jnp.float32) * spread
    if len(shards) > 0:
        values = block_scale(stream_key, shape, shards, -0.22, 0.18) * values
    return jnp.clip(values, min=-bound, max=bound).astype(held_as)


def setup_inputs(seed: int = 0, part: int = 0) -> dict:
    seeds = jax.random.split(jax.random.key(seed), 10)
    part_splits = jax.random.split(jax.random.fold_in(seeds[9], part), 10)
    return {
        "initial": noise(part_splits[0], (SAMP, NZ, NX, NY), 1.0, 6.0, ((0, 2), (2, 4), (3, 2)), jnp.float32),
        "retard": jnp.clip(0.2 + 0.2 * jax.random.uniform(part_splits[1], (SAMP, NZ, NX, NY), jnp.float32) ** block_scale(part_splits[1], (SAMP, NZ, NX, NY), ((0, 2), (2, 4), (3, 2)), -0.2, 0.2), 0.2, 0.4),
        "velx": jnp.clip(jnp.exp(math.log(1.0) - 1.609438 * jax.random.uniform(part_splits[2], (SAMP, NZ, NX, NY), jnp.float32) ** block_scale(part_splits[2], (SAMP, NZ, NX, NY), ((0, 2), (2, 4), (3, 2)), -0.2, 0.2)), 0.2, 1.0),
        "vely": jnp.clip(jnp.exp(math.log(1.0) - 1.609438 * jax.random.uniform(part_splits[3], (SAMP, NZ, NX, NY), jnp.float32) ** block_scale(part_splits[3], (SAMP, NZ, NX, NY), ((0, 2), (2, 4), (3, 2)), -0.2, 0.2)), 0.2, 1.0),
        "monitor": jnp.clip(0.2 + 0.8 * jax.random.uniform(part_splits[4], (NZ, NX, NY), jnp.float32) ** block_scale(part_splits[4], (NZ, NX, NY), ((1, 4), (2, 2)), -0.2, 0.2), 0.2, 1.0),
        "controls": noise(part_splits[5], (NC,), 1.0, 6.0, (), jnp.float32),
        "profile": noise(part_splits[6], (NC, SCREEN), 0.5, 4.0, (), jnp.float32),
        "wells": place_ends(jax.random.randint(part_splits[7], (NC,), 0, ROWS), jax.random.fold_in(part_splits[7], 1), 0, ROWS - 1).astype(jnp.int32),
        "ranking": draw_ranking(jax.random.fold_in(jax.random.fold_in(seeds[9], part), 71), part),
    }


KAPPA = 0.1
VERT = 0.05


def neighbours(f):
    p = jnp.pad(f, ((0, 0), (1, 1), (1, 1), (1, 1)))
    return (p[:, :-2, 1:-1, 1:-1], p[:, 2:, 1:-1, 1:-1], p[:, 1:-1, :-2, 1:-1],
            p[:, 1:-1, 2:, 1:-1], p[:, 1:-1, 1:-1, :-2], p[:, 1:-1, 1:-1, 2:])


def forward_apply(c, retard, velx, vely):
    zm, zp, xm, xp, ym, yp = neighbours(c)
    flux = velx * (xm - c) + vely * (ym - c) + KAPPA * (xp + xm + yp + ym - 4.0 * c) + VERT * (zp + zm - 2.0 * c)
    return c + retard * flux


def adjoint_apply(g, retard, velx, vely):
    h = retard * g
    zm, zp, xm, xp, ym, yp = neighbours(h)
    uh_next = neighbours(velx * h)[3]
    vh_next = neighbours(vely * h)[5]
    return (g - (velx + vely + 4.0 * KAPPA + 2.0 * VERT) * h + uh_next + vh_next
            + KAPPA * (xp + xm + yp + ym) + VERT * (zp + zm))


def reference(initial, retard, velx, vely, monitor, controls, profile, wells, ranking):
    nrows = NZ * NX * NY // 128
    src_rows = jnp.zeros((nrows, 128), jnp.float32).at[wells].add(controls[:, None] * profile)
    source = src_rows.reshape(NZ, NX, NY)

    def fstep(i, c):
        return forward_apply(c + source[None], retard, velx, vely)

    final = lax.fori_loop(0, ITERS, fstep, initial)
    tail = (ranking < TAILN).astype(jnp.float32)[:, None, None, None]
    objective = jnp.sum(tail * 0.5 * monitor[None] * final * final) / (TAILN * NZ * NX * NY)
    start = tail * monitor[None] * final / (TAILN * ITERS)

    def astep(i, carry):
        g, total = carry
        g = adjoint_apply(g, retard, velx, vely)
        return (g, total + g)

    g, total = lax.fori_loop(0, ITERS, astep, (start, jnp.zeros_like(start)))
    sensitivity = jnp.sum(total, axis=0).reshape(nrows, 128)
    gradient = jnp.sum(sensitivity[wells] * profile, axis=1)
    return final, gradient, objective.reshape(1)
```

```python
import functools

import jax
import jax.numpy as jnp
from jax import lax
from jax.experimental import pallas as pl
from jax.experimental.pallas import tpu as pltpu
from jax.sharding import PartitionSpec as P

ITERS = 16
KAPPA = 0.1
VERT = 0.05
LANES = 128
SUBLANES = 8
DEPTH = ITERS
OWN = 2 * DEPTH
EXT = OWN + 2 * DEPTH
GROUPS = LANES // DEPTH
INNER = EXT // GROUPS
CHUNK = 512
PHASES = ((0, 4), (4, 8), (8, 12), (12, ITERS - 1))
VMEM_LIMIT = 48 * 1024 * 1024


def vmem():
    return pl.BlockSpec(memory_space=pltpu.VMEM)


def params():
    return pltpu.CompilerParams(vmem_limit_bytes=VMEM_LIMIT)


def sub_id():
    return lax.broadcasted_iota(jnp.int32, (SUBLANES, LANES), 0)


def lane_id():
    return lax.broadcasted_iota(jnp.int32, (SUBLANES, LANES), 1)


def wrap(shift):
    return shift % LANES if isinstance(shift, int) else lax.rem(shift, LANES)


def lane_roll(value, shift):
    if isinstance(shift, int) and shift % LANES == 0:
        return value
    return pltpu.roll(value, wrap(shift), 1)


def pick(flag, yes, no):
    if isinstance(flag, bool):
        return yes if flag else no
    return jnp.where(flag, yes, no)


def odd_tile():
    return lax.rem(lax.axis_index("gx"), 2)


def strip_kinds(count):
    return (None,) if count == 2 else (True, False)


def is_right(kind):
    return lax.axis_index("gy") == 0 if kind is None else kind


def planes(ref, row, half, rows):
    return ref[pl.ds(half * rows + row, SUBLANES, stride=2 * rows), :]


def split_kernel(initial, retard, velx, vely, out_a, out_b, sems):
    odd = odd_tile()
    copies = []
    for field, ref in enumerate((initial, retard, velx, vely)):
        for which, (out, base) in enumerate(((out_a, DEPTH * (1 - odd)), (out_b, DEPTH * odd))):
            source = ref.at[:, :, pl.ds(pl.multiple_of(base, DEPTH), DEPTH), :]
            copy = pltpu.make_async_copy(source, out.at[field], sems.at[2 * field + which])
            copy.start()
            copies.append(copy)
    for copy in copies:
        copy.wait()


def strip_pack_kernel(kinds, initial, retard, velx, vely, *outs):
    odd = odd_tile()
    group = lane_id() // DEPTH
    fields = (initial, retard, velx, vely)
    for number, kind in enumerate(kinds):
        to_y, to_a, to_b = outs[3 * number : 3 * number + 3]
        offset = DEPTH * (1 - lax.axis_index("gy")) if kind is None else (0 if kind else DEPTH)
        for i in range(INNER):
            for half in range(2):
                for pair in range(2):
                    packed = jnp.zeros((SUBLANES, LANES), jnp.float32)
                    for member in range(2):
                        for j in range(2, 6):
                            target = (j + 4 * member) % GROUPS
                            rows = planes(fields[2 * pair + member], 8 * (j - 2) + i, half, OWN)
                            moved = lane_roll(rows, DEPTH * target + offset)
                            packed = jnp.where(group == target, moved, packed)
                    to_y[pair, i, half] = packed
                for out, base in ((to_a, DEPTH * (1 - odd)), (to_b, DEPTH * odd)):
                    packed = jnp.zeros((SUBLANES, LANES), jnp.float32)
                    for field in range(4):
                        for jj in range(2):
                            target = 2 * field + jj
                            rows = planes(fields[field], base + 8 * jj + i, half, OWN)
                            moved = lane_roll(rows, DEPTH * target + offset)
                            packed = jnp.where(group == target, moved, packed)
                    out[i, half] = packed


def source_kernel(kinds, wells, controls, profile, *refs):
    outs, (acc, acc_low) = refs[:-2], refs[-2:]
    x_index, y_index = lax.axis_index("gx"), lax.axis_index("gy")
    all_x, all_blocks = OWN * lax.axis_size("gx"), lax.axis_size("gy")
    layers = 4
    per_block = EXT * layers
    r = lax.broadcasted_iota(jnp.int32, (per_block, 1), 0)
    x = x_index * OWN - DEPTH + r // layers
    ids = []
    for block in [y_index] + [
        1 - y_index if kind is None else (y_index + 1 if kind else y_index - 1) for kind in kinds
    ]:
        inside = (x >= 0) & (x < all_x) & (block >= 0) & (block < all_blocks)
        ids.append(jnp.where(inside, ((r % layers) * all_x + x) * all_blocks + block, -1))
    ids = jnp.concatenate(ids, axis=0)
    acc[...] = jnp.zeros_like(acc)
    acc_low[...] = jnp.zeros_like(acc_low)

    def chunk(c, carry):
        span = pl.ds(pl.multiple_of(c * CHUNK, CHUNK), CHUNK)
        part = profile[span, :]
        high = part.astype(jnp.bfloat16)
        low = (part - high.astype(jnp.float32)).astype(jnp.bfloat16)
        rate = controls[:, span]
        rate_high = rate.astype(jnp.bfloat16).astype(jnp.float32)
        hit = ids == wells[:, span]
        hot_high = jnp.where(hit, rate_high, 0.0).astype(jnp.bfloat16)
        hot_low = jnp.where(hit, rate - rate_high, 0.0).astype(jnp.bfloat16)
        acc[...] += jnp.dot(
            hot_high, jnp.concatenate([high, low], axis=1), preferred_element_type=jnp.float32
        )
        acc_low[...] += jnp.dot(hot_low, high, preferred_element_type=jnp.float32)
        return carry

    lax.fori_loop(0, wells.shape[1] // CHUNK, chunk, 0)
    acc_low[...] += acc[:, :LANES] + acc[:, LANES:]
    upper = sub_id() % 2 == 1
    group = lane_id() // DEPTH

    def both(first, half):
        low_layer = jnp.broadcast_to(acc_low[pl.ds(first + half, 1), :], (SUBLANES, LANES))
        high_layer = jnp.broadcast_to(acc_low[pl.ds(first + 2 + half, 1), :], (SUBLANES, LANES))
        return jnp.where(upper, high_layer, low_layer)

    for e in range(EXT):
        for half in range(2):
            outs[0][e, half] = both(e * layers, half)
    for number, kind in enumerate(kinds):
        offset = DEPTH * y_index if kind is None else (0 if kind else DEPTH)
        for i in range(INNER):
            for half in range(2):
                packed = jnp.zeros((SUBLANES, LANES), jnp.float32)
                for j in range(GROUPS):
                    rows = both((number + 1) * per_block + (j * INNER + i) * layers, half)
                    moved = lane_roll(rows, DEPTH * j + offset)
                    packed = jnp.where(group == j, moved, packed)
                outs[1 + number][i, half] = packed


def coefficients(retard, velx, vely):
    spread = KAPPA * retard
    from_x = retard * velx + spread
    from_y = retard * vely + spread
    keep = 1.0 - (from_x + from_y + (2.0 + 2.0 * VERT / KAPPA) * spread)
    return keep, from_x, from_y, spread


def places(odd):
    return DEPTH * (2 - odd), DEPTH * (1 + odd), 3 * DEPTH * (1 - odd), 3 * DEPTH * odd


def load_coefficients(odd, own, got_a, got_b, coefs, state=None):
    for x in range(OWN):
        for half in range(2):
            raw = [planes(ref, x, half, OWN) for ref in own[-3:]]
            for ref, value in zip(coefs, coefficients(*raw)):
                ref[DEPTH + x, half] = value
            if state is not None:
                state[DEPTH + x, half] = planes(own[0], x, half, OWN)
    _, _, at_a, at_b = places(odd)
    for got, at in ((got_a, at_a), (got_b, at_b)):
        for x in range(DEPTH):
            for half in range(2):
                raw = [planes(got.at[field], x, half, DEPTH) for field in (1, 2, 3)]
                for ref, value in zip(coefs, coefficients(*raw)):
                    ref[at + x, half] = value
                if state is not None:
                    state[at + x, half] = planes(got.at[0], x, half, DEPTH)


def merge_strip(odd, middle, from_a, from_b):
    quarter = lane_id() // (2 * DEPTH)
    rim = jnp.where(quarter == 3 * (1 - odd), from_a, from_b)
    return jnp.where((quarter == 1) | (quarter == 2), middle, rim)


def strip_field(odd, got_y, got_a, got_b, field, i, half):
    middle = lane_roll(got_y[field // 2, i, half], 64 * (field % 2))
    from_a = lane_roll(got_a[i, half], 96 * (1 - odd) + LANES - 32 * field)
    from_b = lane_roll(got_b[i, half], 96 * odd + LANES - 32 * field)
    return merge_strip(odd, middle, from_a, from_b)


def load_strips(odd, got, coefs, state=None):
    for i in range(INNER):
        for half in range(2):
            raw = [strip_field(odd, *got, field, i, half) for field in (1, 2, 3)]
            for ref, value in zip(coefs, coefficients(*raw)):
                ref[i, half] = value
            if state is not None:
                state[i, half] = strip_field(odd, *got, 0, i, half)


class Frame:
    def __init__(self, kinds):
        lane = lane_id()
        self.first, self.last = lane == 0, lane == LANES - 1
        self.column = lane % DEPTH
        self.strip_first, self.strip_last = self.column == 0, self.column == DEPTH - 1
        self.group = lane // DEPTH
        upper = sub_id() % 2 == 1
        self.below = jnp.where(upper, VERT / KAPPA, 0.0)
        self.above = jnp.where(upper, 0.0, VERT / KAPPA)
        self.right = [is_right(kind) for kind in kinds]
        self.to_tile = [pick(right, 127, 113) for right in self.right]
        self.to_strip = [pick(right, 1, 15) for right in self.right]
        self.edge = [self.column == pick(right, 0, DEPTH - 1) for right in self.right]

    def vertical(self, pair):
        low = (VERT / KAPPA) * pair[1] + self.below * pltpu.roll(pair[1], 1, 0)
        high = (VERT / KAPPA) * pair[0] + self.above * pltpu.roll(pair[0], SUBLANES - 1, 0)
        return low, high

    def onto_tile(self, edges, j):
        total = None
        for shift, edge in zip(self.to_tile, edges):
            moved = lane_roll(edge, shift - DEPTH * j)
            total = moved if total is None else total + moved
        return total

    def onto_strip(self, number, value, j, packed):
        moved = lane_roll(value, self.to_strip[number] + DEPTH * j)
        return jnp.where(self.group == j, moved, packed)


def forward_step(frame, tile, strips, first, last, final_step, emit):
    state, keep, from_x, from_y, spread, source = tile
    zero = jnp.zeros((SUBLANES, LANES), jnp.float32)
    count = len(strips)
    edges = [
        [[jnp.where(frame.edge[k], strips[k][0][i, h], 0.0) for h in range(2)] for i in range(INNER)]
        for k in range(count)
    ]
    gathered = [[[zero, zero] for _ in range(INNER)] for _ in range(count)]
    before = [state[first - 1, h] for h in range(2)]
    here = [state[first, h] for h in range(2)]
    for e in range(first, last + 1):
        after = [state[e + 1, h] for h in range(2)]
        j, i = divmod(e, INNER)
        upright = frame.vertical(here)
        fresh = []
        for h in range(2):
            edge = frame.onto_tile([edges[k][i][h] for k in range(count)], j)
            y_low = jnp.where(frame.first, edge, lane_roll(here[h], 1))
            y_high = jnp.where(frame.last, edge, lane_roll(here[h], LANES - 1))
            value = (
                keep[e, h] * here[h]
                + from_x[e, h] * before[h]
                + from_y[e, h] * y_low
                + spread[e, h] * (after[h] + y_high + upright[h])
            )
            fresh.append(value)
            if not final_step:
                for k in range(count):
                    gathered[k][i][h] = frame.onto_strip(k, here[h], j, gathered[k][i][h])
                state[e, h] = value + source[e, h]
        if final_step:
            emit(e, fresh)
        before, here = here, after
    if final_step:
        return
    for k in range(count):
        strip, keep, from_x, from_y, spread, source = strips[k]
        old = [[strip[i, h] for h in range(2)] for i in range(INNER)]
        for i in range(INNER):
            upright = frame.vertical(old[i])
            for h in range(2):
                x_low = old[i - 1][h] if i > 0 else lane_roll(old[INNER - 1][h], DEPTH)
                x_high = old[i + 1][h] if i < INNER - 1 else lane_roll(old[0][h], LANES - DEPTH)
                edge = gathered[k][i][h]
                y_low = jnp.where(frame.strip_first, edge, lane_roll(old[i][h], 1))
                y_high = jnp.where(frame.strip_last, edge, lane_roll(old[i][h], LANES - 1))
                strip[i, h] = (
                    keep[i, h] * old[i][h]
                    + from_x[i, h] * x_low
                    + from_y[i, h] * y_low
                    + spread[i, h] * (x_high + y_high + upright[h])
                    + source[i, h]
                )


def adjoint_step(frame, tile, strips, first, last, final_step, total):
    state, keep, from_x, from_y, spread = tile
    zero = jnp.zeros((SUBLANES, LANES), jnp.float32)
    count = len(strips)
    edges = [
        [
            [
                jnp.where(
                    frame.edge[k],
                    pick(frame.right[k], strips[k][3][i, h], strips[k][4][i, h]) * strips[k][0][i, h],
                    0.0,
                )
                for h in range(2)
            ]
            for i in range(INNER)
        ]
        for k in range(count)
    ]
    gathered = [[[zero, zero] for _ in range(INNER)] for _ in range(count)]

    def row(e):
        value = [state[e, h] for h in range(2)]
        return (
            value,
            [from_x[e, h] * value[h] for h in range(2)],
            [from_y[e, h] * value[h] for h in range(2)],
            [spread[e, h] * value[h] for h in range(2)],
        )

    before, here = row(first - 1), row(first)
    for e in range(first, last + 1):
        after = row(e + 1)
        j, i = divmod(e, INNER)
        value, _, by_y, by_spread = here
        upright = frame.vertical(by_spread)
        for h in range(2):
            edge = frame.onto_tile([edges[k][i][h] for k in range(count)], j)
            y_low = jnp.where(frame.first, edge, lane_roll(by_spread[h], 1))
            y_high = jnp.where(frame.last, edge, lane_roll(by_y[h], LANES - 1))
            fresh = (
                keep[e, h] * value[h] + (after[1][h] + before[3][h]) + (y_low + y_high) + upright[h]
            )
            if DEPTH <= e < DEPTH + OWN:
                total[e - DEPTH, h] += fresh
            if not final_step:
                state[e, h] = fresh
                for k in range(count):
                    edge = pick(frame.right[k], by_spread[h], by_y[h])
                    gathered[k][i][h] = frame.onto_strip(k, edge, j, gathered[k][i][h])
        before, here = here, after
    if final_step:
        return
    for k in range(count):
        strip, keep, from_x, from_y, spread = strips[k]
        old = [[strip[i, h] for h in range(2)] for i in range(INNER)]
        by_x = [[from_x[i, h] * old[i][h] for h in range(2)] for i in range(INNER)]
        by_spread = [[spread[i, h] * old[i][h] for h in range(2)] for i in range(INNER)]
        for i in range(INNER):
            upright = frame.vertical(by_spread[i])
            for h in range(2):
                x_low = by_spread[i - 1][h] if i > 0 else lane_roll(by_spread[INNER - 1][h], DEPTH)
                x_high = by_x[i + 1][h] if i < INNER - 1 else lane_roll(by_x[0][h], LANES - DEPTH)
                by_y = from_y[i, h] * old[i][h]
                edge = gathered[k][i][h]
                y_low = jnp.where(frame.strip_first, edge, lane_roll(by_spread[i][h], 1))
                y_high = jnp.where(frame.strip_last, edge, lane_roll(by_y, LANES - 1))
                strip[i, h] = (
                    keep[i, h] * old[i][h] + (x_low + x_high) + (y_low + y_high) + upright[h]
                )


def sweep(step):
    for begin, end in PHASES:

        def body(_, carry, begin=begin):
            step(begin + 1, EXT - 2 - begin, False)
            return carry

        lax.fori_loop(begin, end, body, 0)
    step(ITERS, EXT - 1 - ITERS, True)


def split_refs(refs, *counts):
    out = []
    for count in counts:
        out.append(refs[:count])
        refs = refs[count:]
    return out


def forward_kernel(kinds, tail_count, *refs):
    n = len(kinds)
    own, (monitor, ranking, got_a, got_b), got_strips, sources, outs, out_strips, tile, start, strips = split_refs(
        refs, 4, 4, 3 * n, 1 + n, 4, 3 * n, 5, 1, 5 * n
    )
    final, start_a, start_b, objective = outs
    start = start[0]
    odd = odd_tile()
    frame = Frame(kinds)
    state, coefs = tile[0], tile[1:]
    load_coefficients(odd, own, got_a, got_b, coefs, state)
    for e in range(EXT):
        for h in range(2):
            state[e, h] += sources[0][e, h]
    strip_refs = []
    for k in range(n):
        mine = strips[5 * k : 5 * k + 5]
        load_strips(odd, got_strips[3 * k : 3 * k + 3], mine[1:], mine[0])
        for i in range(INNER):
            for h in range(2):
                mine[0][i, h] += sources[1 + k][i, h]
        strip_refs.append((*mine, sources[1 + k]))

    sample = sub_id() // 2
    upper = sub_id() % 2 == 1
    tail = jnp.zeros((SUBLANES, LANES), jnp.float32)
    for s in range(4):
        tail = jnp.where(sample == s, jnp.where(ranking[s] < tail_count, 1.0, 0.0), tail)
    objective[...] = jnp.zeros_like(objective)

    def emit(e, fresh):
        x = e - DEPTH
        for h in range(2):
            final[pl.ds(h * OWN + x, SUBLANES, stride=2 * OWN), :] = fresh[h]
            low = jnp.broadcast_to(monitor[pl.ds(h * OWN + x, 1), :], (SUBLANES, LANES))
            high = jnp.broadcast_to(monitor[pl.ds((2 + h) * OWN + x, 1), :], (SUBLANES, LANES))
            weighted = tail * jnp.where(upper, high, low) * fresh[h]
            start[x, h] = weighted * (1.0 / (tail_count * ITERS))
            objective[...] += weighted * fresh[h]

    def step(first, last, final_step):
        forward_step(frame, (*tile, sources[0]), strip_refs, first, last, final_step, emit)

    sweep(step)
    at_a, at_b = DEPTH * (1 - odd), DEPTH * odd
    for x in range(DEPTH):
        for h in range(2):
            start_a[x, h] = start[at_a + x, h]
            start_b[x, h] = start[at_b + x, h]
    for k, kind in enumerate(kinds):
        to_y, to_a, to_b = out_strips[3 * k : 3 * k + 3]
        offset = DEPTH * (1 - lax.axis_index("gy")) if kind is None else (0 if kind else DEPTH)
        for i in range(INNER):
            packed = jnp.zeros((SUBLANES, LANES), jnp.float32)
            for h in range(2):
                for j in range(2, 6):
                    target = (j + 4 * h) % GROUPS
                    moved = lane_roll(start[8 * (j - 2) + i, h], DEPTH * target + offset)
                    packed = jnp.where(frame.group == target, moved, packed)
            to_y[i] = packed
            for out, base in ((to_a, at_a), (to_b, at_b)):
                packed = jnp.zeros((SUBLANES, LANES), jnp.float32)
                for h in range(2):
                    for jj in range(2):
                        target = 2 * h + jj
                        moved = lane_roll(start[base + 8 * jj + i, h], DEPTH * target + offset)
                        packed = jnp.where(frame.group == target, moved, packed)
                out[i] = packed


def adjoint_kernel(kinds, scale, *refs):
    n = len(kinds)
    own, got, got_strips, parts, part_strips, rest, tile, strips, scratch = split_refs(
        refs, 3, 2, 3 * n, 4, 3 * n, 4, 5, 5 * n, 2
    )
    objective, wells, profile, out = rest
    total, rows = scratch
    odd = odd_tile()
    frame = Frame(kinds)
    state, coefs = tile[0], tile[1:]
    load_coefficients(odd, own, *got, coefs)
    for part, at in zip(parts, places(odd)):
        for x in range(DEPTH):
            for h in range(2):
                state[at + x, h] = part[x, h]
    strip_refs = []
    for k in range(n):
        mine = strips[5 * k : 5 * k + 5]
        load_strips(odd, got_strips[3 * k : 3 * k + 3], mine[1:])
        got_y, got_a, got_b = part_strips[3 * k : 3 * k + 3]
        for i in range(INNER):
            for h in range(2):
                mine[0][i, h] = merge_strip(
                    odd,
                    lane_roll(got_y[i], 64 * h),
                    lane_roll(got_a[i], 96 * (1 - odd) + LANES - 32 * h),
                    lane_roll(got_b[i], 96 * odd + LANES - 32 * h),
                )
        strip_refs.append(mine)
    total[...] = jnp.zeros_like(total)

    def step(first, last, final_step):
        adjoint_step(frame, tile, strip_refs, first, last, final_step, total)

    sweep(step)
    for x in range(OWN):
        for h in range(2):
            value = total[x, h]
            value = value + pltpu.roll(value, 4, 0)
            value = value + pltpu.roll(value, 2, 0)
            rows[pl.ds((2 * x + h) * 2, 2), :] = value[:2]
    count = rows.shape[0]
    r = lax.broadcasted_iota(jnp.int32, (count, 1), 0)
    layer = (r % 2) * 2 + (r // 2) % 2
    x = lax.axis_index("gx") * OWN + r // 4
    ids = (layer * (OWN * lax.axis_size("gx")) + x) * lax.axis_size("gy") + lax.axis_index("gy")
    field = rows[...]
    high = field.astype(jnp.bfloat16)
    low = (field - high.astype(jnp.float32)).astype(jnp.bfloat16)
    both = jnp.concatenate([high, low], axis=0)
    contract = (((1,), (1,)), ((), ()))
    controls = wells.shape[1]

    def chunk(c, carry):
        span = pl.ds(pl.multiple_of(c * CHUNK, CHUNK), CHUNK)
        share = profile[span, :]
        share_high = share.astype(jnp.bfloat16)
        share_low = (share - share_high.astype(jnp.float32)).astype(jnp.bfloat16)
        first = lax.dot_general(both, share_high, contract, preferred_element_type=jnp.float32)
        second = lax.dot_general(high, share_low, contract, preferred_element_type=jnp.float32)
        product = first[:count] + first[count:] + second
        chosen = jnp.where(ids == wells[:, span], product, 0.0)
        out[:, span] = jnp.sum(chosen, axis=0, keepdims=True)
        return carry

    lax.fori_loop(0, controls // CHUNK, chunk, 0)
    whole = jnp.sum(jnp.sum(objective[...], axis=0, keepdims=True), axis=1, keepdims=True)
    out[:, controls:] = jnp.broadcast_to(whole * scale, (1, LANES))


def shape(*dims):
    return jax.ShapeDtypeStruct(dims, jnp.float32)


def partner_a(x, count):
    return x ^ 1


def partner_b(x, count):
    other = x + 1 if x % 2 else x - 1
    return other if 0 <= other < count else None


def tile_pairs(partner, count):
    return [(partner(x, count), x) for x in range(count) if partner(x, count) is not None]


def strip_pairs(kind, partner, count_x, count_y):
    pairs = []
    for x in range(count_x):
        for y in range(count_y):
            from_x = partner(x, count_x)
            from_y = 1 - y if kind is None else (y + 1 if kind else y - 1)
            if from_x is not None and 0 <= from_y < count_y:
                pairs.append((from_x * count_y + from_y, x * count_y + y))
    return pairs


def exchange(tiles, strips, kinds, count_x, count_y):
    got = [
        lax.ppermute(tile, "gx", tile_pairs(partner, count_x))
        for tile, partner in zip(tiles, (partner_a, partner_b))
    ]
    got_strips = []
    for k, kind in enumerate(kinds):
        for strip, partner in zip(
            strips[3 * k : 3 * k + 3], (lambda x, count: x, partner_a, partner_b)
        ):
            pairs = strip_pairs(kind, partner, count_x, count_y)
            got_strips.append(lax.ppermute(strip, ("gx", "gy"), pairs))
    return got, got_strips


def local(initial, retard, velx, vely, monitor, controls, profile, wells, ranking):
    samples, layers, width_x, width_y = initial.shape
    count_x, count_y = lax.axis_size("gx"), lax.axis_size("gy")
    assert (samples, layers, width_x, width_y) == (4, 4, OWN, LANES) and count_x % 2 == 0
    number = controls.shape[0]
    assert number % CHUNK == 0
    kinds = strip_kinds(count_y)
    n = len(kinds)
    fields = (initial, retard, velx, vely)
    flat = [field.reshape(-1, LANES) for field in fields]
    half_tile = shape(4, samples, layers, DEPTH, LANES)
    any_space = pl.BlockSpec(memory_space=pl.ANY)
    sent = pl.pallas_call(
        split_kernel,
        out_shape=(half_tile, half_tile),
        in_specs=[any_space] * 4,
        out_specs=(any_space, any_space),
        scratch_shapes=[pltpu.SemaphoreType.DMA((8,))],
        compiler_params=params(),
        name="split",
    )(*fields)
    strip_shape = shape(INNER, 2, SUBLANES, LANES)
    sent_strips = pl.pallas_call(
        functools.partial(strip_pack_kernel, kinds),
        out_shape=(shape(2, INNER, 2, SUBLANES, LANES), strip_shape, strip_shape) * n,
        in_specs=[vmem()] * 4,
        out_specs=(vmem(),) * (3 * n),
        compiler_params=params(),
        name="strips",
    )(*flat)
    got, got_strips = exchange(sent, sent_strips, kinds, count_x, count_y)
    wells = wells.reshape(1, -1)
    blocks = (1 + n) * EXT * layers
    sources = pl.pallas_call(
        functools.partial(source_kernel, kinds),
        out_shape=(shape(EXT, 2, SUBLANES, LANES),) + (strip_shape,) * n,
        in_specs=[vmem()] * 3,
        out_specs=(vmem(),) * (1 + n),
        scratch_shapes=[
            pltpu.VMEM((blocks, 2 * LANES), jnp.float32),
            pltpu.VMEM((blocks, LANES), jnp.float32),
        ],
        compiler_params=params(),
        name="source",
    )(wells, controls.reshape(1, -1), profile)
    got = [part.reshape(4, -1, LANES) for part in got]
    tail_count = samples * lax.axis_size("sa") // 2
    tile_scratch = [pltpu.VMEM((EXT, 2, SUBLANES, LANES), jnp.float32)] * 5
    strip_scratch = [pltpu.VMEM((INNER, 2, SUBLANES, LANES), jnp.float32)] * (5 * n)
    half_start = shape(DEPTH, 2, SUBLANES, LANES)
    packed = shape(INNER, SUBLANES, LANES)
    smem = pl.BlockSpec(memory_space=pltpu.SMEM)
    final, start_a, start_b, objective, *start_strips = pl.pallas_call(
        functools.partial(forward_kernel, kinds, tail_count),
        out_shape=(
            shape(samples * layers * OWN, LANES),
            half_start,
            half_start,
            shape(SUBLANES, LANES),
        )
        + (packed,) * (3 * n),
        in_specs=[vmem()] * 5 + [smem] + [vmem()] * (2 + 3 * n + 1 + n),
        out_specs=(vmem(),) * (4 + 3 * n),
        scratch_shapes=tile_scratch
        + [pltpu.VMEM((OWN, 2, SUBLANES, LANES), jnp.float32)]
        + strip_scratch,
        compiler_params=params(),
        name="forward",
    )(*flat, monitor.reshape(-1, LANES), ranking, *got, *got_strips, *sources)
    start = (start_a, start_b)
    got_start, got_start_strips = exchange(start, start_strips, kinds, count_x, count_y)
    cells = layers * OWN * count_x * LANES * count_y
    summed = pl.pallas_call(
        functools.partial(adjoint_kernel, kinds, 0.5 / (tail_count * cells)),
        out_shape=shape(1, number + LANES),
        in_specs=[vmem()] * (3 + 2 + 3 * n + 4 + 3 * n + 3),
        out_specs=vmem(),
        scratch_shapes=tile_scratch
        + strip_scratch
        + [
            pltpu.VMEM((OWN, 2, SUBLANES, LANES), jnp.float32),
            pltpu.VMEM((OWN * layers, LANES), jnp.float32),
        ],
        compiler_params=params(),
        name="adjoint",
    )(
        *flat[1:],
        *got,
        *got_strips,
        *start,
        *got_start,
        *got_start_strips,
        objective,
        wells,
        profile,
    )
    for axis in ("sa", "gy", "gx"):
        count = lax.axis_size(axis)
        distance = 1
        while distance < count:
            pairs = [(i, i ^ distance) for i in range(count)]
            summed = summed + lax.ppermute(summed, axis, pairs)
            distance *= 2
    return final.reshape(initial.shape), summed[0, :number], summed[0, number : number + 1]


def solution(mesh):
    in_specs = (
        P(("groups", "sa"), None, "gx", "gy"),
        P(("groups", "sa"), None, "gx", "gy"),
        P(("groups", "sa"), None, "gx", "gy"),
        P(("groups", "sa"), None, "gx", "gy"),
        P("groups", "gx", "gy"),
        P("groups"),
        P("groups", None),
        P("groups"),
        P(("groups", "sa")),
    )
    out_specs = (P(("groups", "sa"), None, "gx", "gy"), P("groups"), P("groups"))
    return jax.shard_map(local, mesh=mesh, in_specs=in_specs, out_specs=out_specs, check_vma=False)
```

```python
import functools

import jax
import jax.numpy as jnp
from jax import lax
from jax.experimental import pallas as pl
from jax.experimental.pallas import tpu as pltpu
from jax.sharding import PartitionSpec as P

ITERS = 16
KAPPA = 0.1
VERT = 0.05
LANES = 128
SUBLANES = 8
DEPTH = ITERS
OWN = 2 * DEPTH
EXT = OWN + 2 * DEPTH
WIDE = 2 * DEPTH
GROUPS = LANES // WIDE
INNER = EXT // GROUPS
JOIN = ITERS // 2
CHUNK = 512
PHASES = ((0, 4), (4, 8), (8, 12), (12, ITERS - 1))
VMEM_LIMIT = 24 * 1024 * 1024


def vmem():
    return pl.BlockSpec(memory_space=pltpu.VMEM)


def params():
    return pltpu.CompilerParams(vmem_limit_bytes=VMEM_LIMIT)


def sub_id():
    return lax.broadcasted_iota(jnp.int32, (SUBLANES, LANES), 0)


def lane_id():
    return lax.broadcasted_iota(jnp.int32, (SUBLANES, LANES), 1)


def wrap(shift):
    return shift % LANES if isinstance(shift, int) else lax.rem(shift, LANES)


def lane_roll(value, shift):
    if isinstance(shift, int) and shift % LANES == 0:
        return value
    return pltpu.roll(value, wrap(shift), 1)


def pick(flag, yes, no):
    if isinstance(flag, bool):
        return yes if flag else no
    return jnp.where(flag, yes, no)


def odd_tile():
    return lax.rem(lax.axis_index("gx"), 2)


def lacks_b():
    x = lax.axis_index("gx")
    return (x == 0) | (x == lax.axis_size("gx") - 1)


def strip_kinds(count):
    return (None,) if count == 2 else (True, False)


def is_right(kind):
    return lax.axis_index("gy") == 0 if kind is None else kind


def planes(ref, row, half, rows):
    return ref[pl.ds(half * rows + row, SUBLANES, stride=2 * rows), :]


def stage_kernel(initial, retard, velx, vely, monitor, controls, wells, *refs):
    own, out_a, out_b, out_monitor, out_controls, out_wells, sems = refs
    odd = odd_tile()
    pairs = [(monitor, out_monitor), (controls, out_controls), (wells, out_wells)]
    for field, ref in enumerate((initial, retard, velx, vely)):
        for out, base in ((out_a, DEPTH * (1 - odd)), (out_b, DEPTH * odd)):
            source = ref.at[:, :, pl.ds(pl.multiple_of(base, DEPTH), DEPTH), :]
            pairs.append((source, out.at[field]))
        pairs.append((ref, own.at[field]))
    copies = [pltpu.make_async_copy(*pair, sems.at[k]) for k, pair in enumerate(pairs)]
    for copy in copies:
        copy.start()
    for copy in copies:
        copy.wait()


def edge_offset(kind):
    return DEPTH * (1 - lax.axis_index("gy")) if kind is None else (0 if kind else DEPTH)


def strip_pack_kernel(kinds, own, *outs):
    odd = odd_tile()
    slot = lane_id() // DEPTH
    for number, kind in enumerate(kinds):
        to_y, to_a, to_b = outs[3 * number : 3 * number + 3]
        offset = edge_offset(kind)

        def put(packed, field, row, half, target):
            moved = lane_roll(planes(own.at[field], row, half, OWN), DEPTH * target + offset)
            return moved if packed is None else jnp.where(slot == target, moved, packed)

        for half in range(2):
            for i in range(INNER):
                packed = None
                for field in range(4):
                    for j in range(2):
                        target = 4 * (field // 2) + 2 * j + field % 2
                        packed = put(packed, field, INNER * j + i, half, target)
                to_y[i, half] = packed
            for out, base in ((to_a, DEPTH * (1 - odd)), (to_b, DEPTH * odd)):
                for i in range(INNER // 2):
                    packed = None
                    for field in range(4):
                        for upper in range(2):
                            row = base + INNER // 2 * upper + i
                            packed = put(packed, field, row, half, 4 * upper + field)
                    out[i, half] = packed


def coefficients(retard, velx, vely):
    spread = KAPPA * retard
    from_x = retard * velx + spread
    from_y = retard * vely + spread
    keep = 1.0 - (from_x + from_y + (2.0 + 2.0 * VERT / KAPPA) * spread)
    return keep, from_x, from_y, spread


def store_tile(refs, row, half, raw, source=None):
    state, retard, velx, vely = raw
    keep, from_x, from_y, spread = coefficients(retard, velx, vely)
    from_y = jnp.where(lane_id() == 0, 0.0, from_y)
    for ref, value in zip(refs, (state, keep, from_x, from_y, spread)):
        ref[row, half] = value


def source_kernel(kinds, wells, controls, profile, own, *refs):
    n = len(kinds)
    sources, tile, edges, (acc, acc_low) = split_refs(refs, 1 + n, 5, 1, 2)
    for x in range(OWN):
        for half in range(2):
            raw = [planes(own.at[field], x, half, OWN) for field in range(4)]
            store_tile(tile, DEPTH + x, half, raw)
    first_j = lane_id() // WIDE == 1
    for field in range(4):
        for i in range(INNER):
            for half in range(2):
                moved = [
                    lane_roll(planes(own.at[field], INNER * j + i, half, OWN), WIDE * (j + 1) + DEPTH)
                    for j in range(2)
                ]
                edges[0][field, i, half] = jnp.where(first_j, *moved)

    x_index, y_index = lax.axis_index("gx"), lax.axis_index("gy")
    all_x, all_blocks = OWN * lax.axis_size("gx"), lax.axis_size("gy")
    layers = 4
    per_block = EXT * layers
    r = lax.broadcasted_iota(jnp.int32, (per_block, 1), 0)
    x = x_index * OWN - DEPTH + r // layers
    ids = []
    for block in [y_index] + [
        1 - y_index if kind is None else (y_index + 1 if kind else y_index - 1) for kind in kinds
    ]:
        inside = (x >= 0) & (x < all_x) & (block >= 0) & (block < all_blocks)
        ids.append(jnp.where(inside, ((r % layers) * all_x + x) * all_blocks + block, -1))
    ids = jnp.concatenate(ids, axis=0)
    acc[...] = jnp.zeros_like(acc)
    acc_low[...] = jnp.zeros_like(acc_low)

    def chunk(c, carry):
        span = pl.ds(pl.multiple_of(c * CHUNK, CHUNK), CHUNK)
        part = profile[span, :]
        high = part.astype(jnp.bfloat16)
        low = (part - high.astype(jnp.float32)).astype(jnp.bfloat16)
        rate = controls[:, span]
        rate_high = rate.astype(jnp.bfloat16).astype(jnp.float32)
        hit = ids == wells[:, span]
        hot_high = jnp.where(hit, rate_high, 0.0).astype(jnp.bfloat16)
        hot_low = jnp.where(hit, rate - rate_high, 0.0).astype(jnp.bfloat16)
        acc[...] += jnp.dot(
            hot_high, jnp.concatenate([high, low], axis=1), preferred_element_type=jnp.float32
        )
        acc_low[...] += jnp.dot(hot_low, high, preferred_element_type=jnp.float32)
        return carry

    lax.fori_loop(0, wells.shape[1] // CHUNK, chunk, 0)
    acc_low[...] += acc[:, :LANES] + acc[:, LANES:]
    upper = sub_id() % 2 == 1
    group = lane_id() // WIDE

    def both(first, half):
        low_layer = jnp.broadcast_to(acc_low[pl.ds(first + half, 1), :], (SUBLANES, LANES))
        high_layer = jnp.broadcast_to(acc_low[pl.ds(first + 2 + half, 1), :], (SUBLANES, LANES))
        return jnp.where(upper, high_layer, low_layer)

    masks = Masks(kinds)
    for number in range(n):
        for i in range(INNER):
            for half in range(2):
                packed = None
                for j in range(GROUPS):
                    e = j * INNER + i
                    here = both(e * layers, half)
                    if number == 0:
                        sources[0][e, half] = here
                    beside = both((number + 1) * per_block + e * layers, half)
                    mixed = jnp.where(masks.own_edge[number], here, beside)
                    moved = lane_roll(mixed, WIDE * j + DEPTH)
                    packed = moved if packed is None else jnp.where(group == j, moved, packed)
                sources[1 + number][i, half] = packed


class Masks:
    def __init__(self, kinds):
        lane = lane_id()
        self.first, self.last = lane == 0, lane == LANES - 1
        self.group = lane // WIDE
        upper = sub_id() % 2 == 1
        self.below = jnp.where(upper, VERT / KAPPA, 0.0)
        self.above = jnp.where(upper, 0.0, VERT / KAPPA)
        self.right = [is_right(kind) for kind in kinds]
        half, eighth, sixteenth = lane % WIDE // DEPTH, lane // DEPTH, lane // JOIN
        self.rim = [half == pick(right, 1, 0) for right in self.right]
        self.not_rim = [half == pick(right, 0, 1) for right in self.right]
        self.own_edge = [eighth != pick(right, 0, LANES // DEPTH - 1) for right in self.right]
        self.outer = [sixteenth == pick(right, LANES // JOIN - 1, 0) for right in self.right]

    def vertical(self, pair):
        low = (VERT / KAPPA) * pair[1] + self.below * pltpu.roll(pair[1], 1, 0)
        high = (VERT / KAPPA) * pair[0] + self.above * pltpu.roll(pair[0], SUBLANES - 1, 0)
        return low, high

    def outer_from(self, strips, e, half, value):
        j, i = divmod(e, INNER)
        for strip, outer in zip(strips, self.outer):
            value = jnp.where(outer, lane_roll(strip[i, half], LANES - DEPTH - WIDE * j), value)
        return value

    def join(self, tile, strips, first, last):
        for e in range(first, last + 1):
            j, i = divmod(e, INNER)
            for h in range(2):
                value = self.outer_from(strips, e, h, tile[e, h])
                tile[e, h] = value
                moved = lane_roll(value, WIDE * j + DEPTH)
                for strip, own in zip(strips, self.not_rim):
                    strip[i, h] = jnp.where((self.group == j) & own, moved, strip[i, h])


def places(odd):
    return DEPTH * (2 - odd), DEPTH * (1 + odd), 3 * DEPTH * (1 - odd), 3 * DEPTH * odd


def merge_strip(masks, number, odd, middle, own_a, own_b, rim_y, rim_a, rim_b):
    inner = (masks.group == 1) | (masks.group == 2)
    at_a = masks.group == 3 * (1 - odd)
    own = jnp.where(inner, middle, jnp.where(at_a, own_a, own_b))
    rim = jnp.where(inner, rim_y, jnp.where(at_a, rim_a, rim_b))
    return jnp.where(masks.rim[number], rim, own)


def forward_step(masks, tile, strips, first, last, sourced):
    state, keep, from_x, from_y, spread, source = tile
    before = [state[first - 1, h] for h in range(2)]
    here = [state[first, h] for h in range(2)]
    for e in range(first, last + 1):
        after = [state[e + 1, h] for h in range(2)]
        upright = masks.vertical(here)
        for h in range(2):
            y_high = jnp.where(masks.last, 0.0, lane_roll(here[h], LANES - 1))
            value = (
                keep[e, h] * here[h]
                + from_x[e, h] * before[h]
                + from_y[e, h] * lane_roll(here[h], 1)
                + spread[e, h] * (after[h] + y_high + upright[h])
            )
            state[e, h] = value + source[e, h] if sourced else value
        before, here = here, after
    for strip, keep, from_x, from_y, spread, source in strips:
        old = [strip[0, h] for h in range(2)]
        here = old
        before = [lane_roll(strip[INNER - 1, h], WIDE) for h in range(2)]
        for i in range(INNER):
            if i < INNER - 1:
                after = [strip[i + 1, h] for h in range(2)]
            else:
                after = [lane_roll(value, LANES - WIDE) for value in old]
            upright = masks.vertical(here)
            for h in range(2):
                value = (
                    keep[i, h] * here[h]
                    + from_x[i, h] * before[h]
                    + from_y[i, h] * lane_roll(here[h], 1)
                    + spread[i, h] * (after[h] + lane_roll(here[h], LANES - 1) + upright[h])
                )
                strip[i, h] = value + source[i, h] if sourced else value
            before, here = here, after


def adjoint_step(masks, tile, strips, first, last):
    state, keep, from_x, from_y, spread, total = tile

    def row(refs, e):
        state, _, from_x, from_y, spread, _ = refs
        value = [state[e, h] for h in range(2)]
        return (
            value,
            [from_x[e, h] * value[h] for h in range(2)],
            [from_y[e, h] * value[h] for h in range(2)],
            [spread[e, h] * value[h] for h in range(2)],
        )

    before, here = row(tile, first - 1), row(tile, first)
    for e in range(first, last + 1):
        after = row(tile, e + 1)
        value, _, by_y, by_spread = here
        upright = masks.vertical(by_spread)
        for h in range(2):
            y_low = jnp.where(masks.first, 0.0, lane_roll(by_spread[h], 1))
            fresh = (
                keep[e, h] * value[h]
                + (after[1][h] + before[3][h])
                + (y_low + lane_roll(by_y[h], LANES - 1))
                + upright[h]
            )
            state[e, h] = fresh
            if DEPTH <= e < DEPTH + OWN:
                total[e - DEPTH, h] += fresh
        before, here = here, after
    for refs in strips:
        strip, keep, from_x, from_y, spread, total = refs
        here = row(refs, 0)
        wrapped = [lane_roll(value, LANES - WIDE) for value in here[1]]
        last_row = row(refs, INNER - 1)
        before = (None, None, None, [lane_roll(value, WIDE) for value in last_row[3]])
        for i in range(INNER):
            after = row(refs, i + 1) if i < INNER - 1 else (None, wrapped, None, None)
            value, _, by_y, by_spread = here
            upright = masks.vertical(by_spread)
            for h in range(2):
                fresh = (
                    keep[i, h] * value[h]
                    + (after[1][h] + before[3][h])
                    + (lane_roll(by_spread[h], 1) + lane_roll(by_y[h], LANES - 1))
                    + upright[h]
                )
                strip[i, h] = fresh
                total[i, h] += fresh
            before, here = here, after


def sweep(step, join):
    for begin, end in PHASES:

        def body(_, carry, begin=begin):
            step(begin + 1, EXT - 2 - begin, True)
            return carry

        if begin == JOIN:
            join(begin, EXT - 1 - begin)
        lax.fori_loop(begin, end, body, 0)
    step(ITERS, EXT - 1 - ITERS, False)


def split_refs(refs, *counts):
    out = []
    for count in counts:
        out.append(refs[:count])
        refs = refs[count:]
    return out


def forward_kernel(kinds, tail_count, *refs):
    n = len(kinds)
    ins, got_strips, sources, tile, edges, outs, strips, out_strips, (start,) = split_refs(
        refs, 4, 3 * n, 1 + n, 5, 1, 4 + 5, 5 * n, 3 * n, 1
    )
    monitor, ranking, got_a, got_b = ins
    final, start_a, start_b, objective, *tile = outs
    odd = odd_tile()
    masks = Masks(kinds)
    state = tile[0]
    _, _, at_a, at_b = places(odd)
    present = jnp.where(lacks_b(), 0.0, 1.0)
    for x in range(DEPTH):
        for h in range(2):
            raw_a = [planes(got_a.at[field], x, h, DEPTH) for field in range(4)]
            raw_b = [planes(got_b.at[field], x, h, DEPTH) for field in range(4)]
            raw_b[:2] = [value * present for value in raw_b[:2]]
            store_tile(tile, at_a + x, h, raw_a)
            store_tile(tile, at_b + x, h, raw_b)
            i = x
            upper = i // (INNER // 2)
            for k in range(n):
                got = got_strips[3 * k : 3 * k + 3]
                side = pick(masks.right[k], DEPTH, 0)
                raw = []
                for field in range(4):
                    slot = DEPTH * (4 * upper + field)
                    rim_b = got[2][i % (INNER // 2), h]
                    rim_b = lane_roll(rim_b, 2 * at_b + side + LANES - slot)
                    raw.append(
                        merge_strip(
                            masks,
                            k,
                            odd,
                            edges[0][field, i, h],
                            lane_roll(raw_a[field], 2 * at_a + DEPTH),
                            lane_roll(raw_b[field], 2 * at_b + DEPTH),
                            lane_roll(
                                got[0][i, h], LANES + WIDE + side - 64 * (field // 2) - DEPTH * (field % 2)
                            ),
                            lane_roll(
                                got[1][i % (INNER // 2), h], 2 * at_a + side + LANES - slot
                            ),
                            rim_b * present if field < 2 else rim_b,
                        )
                    )
                mine = strips[5 * k : 5 * k + 5]
                for ref, value in zip(mine, (raw[0] + sources[1 + k][i, h], *coefficients(*raw[1:]))):
                    ref[i, h] = value
    for e in range(EXT):
        for h in range(2):
            state[e, h] += sources[0][e, h]
    strip_refs = [(*strips[5 * k : 5 * k + 5], sources[1 + k]) for k in range(n)]
    strip_states = [strip[0] for strip in strip_refs]

    def step(first, last, sourced):
        forward_step(masks, (*tile, sources[0]), strip_refs, first, last, sourced)

    sweep(step, functools.partial(masks.join, state, strip_states))

    sample = sub_id() // 2
    upper = sub_id() % 2 == 1
    tail = jnp.zeros((SUBLANES, LANES), jnp.float32)
    for s in range(4):
        tail = jnp.where(sample == s, jnp.where(ranking[s] < tail_count, 1.0, 0.0), tail)
    sums = [jnp.zeros((SUBLANES, LANES), jnp.float32) for _ in range(4)]
    for x in range(OWN):
        for h in range(2):
            fresh = masks.outer_from(strip_states, DEPTH + x, h, state[DEPTH + x, h])
            final[pl.ds(h * OWN + x, SUBLANES, stride=2 * OWN), :] = fresh
            low = jnp.broadcast_to(monitor[pl.ds(h * OWN + x, 1), :], (SUBLANES, LANES))
            high = jnp.broadcast_to(monitor[pl.ds((2 + h) * OWN + x, 1), :], (SUBLANES, LANES))
            weighted = tail * jnp.where(upper, high, low) * fresh
            start[x, h] = weighted * (1.0 / (tail_count * ITERS))
            sums[x % 4] = sums[x % 4] + weighted * fresh
    objective[...] = (sums[0] + sums[1]) + (sums[2] + sums[3])

    base_a, base_b = DEPTH * (1 - odd), DEPTH * odd
    for x in range(DEPTH):
        for h in range(2):
            start_a[x, h] = start[base_a + x, h]
            start_b[x, h] = start[base_b + x, h]
    slot = lane_id() // DEPTH
    for k, kind in enumerate(kinds):
        to_y, to_a, to_b = out_strips[3 * k : 3 * k + 3]
        offset = edge_offset(kind)

        def put(packed, row, h, target):
            moved = lane_roll(start[row, h], DEPTH * target + offset)
            return moved if packed is None else jnp.where(slot == target, moved, packed)

        for i in range(INNER // 2):
            packed = None
            for upper_half in range(2):
                for j in range(2):
                    for h in range(2):
                        row = INNER * j + INNER // 2 * upper_half + i
                        packed = put(packed, row, h, 4 * upper_half + 2 * j + h)
            to_y[i] = packed
        for out, base in ((to_a, base_a), (to_b, base_b)):
            for i in range(INNER // 4):
                packed = None
                for quarter in range(4):
                    for h in range(2):
                        packed = put(packed, base + INNER // 4 * quarter + i, h, 2 * quarter + h)
                out[i] = packed


def adjoint_kernel(kinds, scale, *refs):
    n = len(kinds)
    parts, part_strips, coefs, strip_coefs, rest, (state, total), strips, (rows,) = split_refs(
        refs, 4, 3 * n, 4, 4 * n, 4, 2, 2 * n, 1
    )
    objective, wells, profile, out = rest
    odd = odd_tile()
    masks = Masks(kinds)
    at = places(odd)
    for part, first in zip(parts, at):
        for x in range(DEPTH):
            for h in range(2):
                state[first + x, h] = part[x, h]
    strip_refs = []
    for k in range(n):
        strip, strip_total = strips[2 * k : 2 * k + 2]
        got_y, got_a, got_b = part_strips[3 * k : 3 * k + 3]
        side = pick(masks.right[k], DEPTH, 0)
        for i in range(INNER):
            eighth, quarter = divmod(i, INNER // 2)[0], divmod(i, INNER // 4)[0]
            for h in range(2):
                moved = [
                    lane_roll(part[i, h], 2 * first + DEPTH) for part, first in zip(parts, at)
                ]
                slot = DEPTH * (2 * quarter + h)
                strip[i, h] = merge_strip(
                    masks,
                    k,
                    odd,
                    jnp.where(masks.group == 2 - odd, moved[0], moved[1]),
                    moved[2],
                    moved[3],
                    lane_roll(got_y[i % (INNER // 2)], LANES + WIDE + side - 64 * eighth - DEPTH * h),
                    lane_roll(got_a[i % (INNER // 4)], 2 * at[2] + side + LANES - slot),
                    lane_roll(got_b[i % (INNER // 4)], 2 * at[3] + side + LANES - slot),
                )
        strip_refs.append((strip, *strip_coefs[4 * k : 4 * k + 4], strip_total))
        strip_total[...] = jnp.zeros_like(strip_total)
    total[...] = jnp.zeros_like(total)
    tile = (state, *coefs, total)

    def step(first, last, _):
        adjoint_step(masks, tile, strip_refs, first, last)

    sweep(step, functools.partial(masks.join, state, [refs[0] for refs in strip_refs]))
    totals = [refs[-1] for refs in strip_refs]
    for x in range(OWN):
        for h in range(2):
            value = masks.outer_from(totals, DEPTH + x, h, total[x, h])
            value = value + pltpu.roll(value, 4, 0)
            value = value + pltpu.roll(value, 2, 0)
            rows[pl.ds((2 * x + h) * 2, 2), :] = value[:2]
    count = rows.shape[0]
    r = lax.broadcasted_iota(jnp.int32, (count, 1), 0)
    layer = (r % 2) * 2 + (r // 2) % 2
    x = lax.axis_index("gx") * OWN + r // 4
    ids = (layer * (OWN * lax.axis_size("gx")) + x) * lax.axis_size("gy") + lax.axis_index("gy")
    field = rows[...]
    high = field.astype(jnp.bfloat16)
    low = (field - high.astype(jnp.float32)).astype(jnp.bfloat16)
    both = jnp.concatenate([high, low], axis=0)
    contract = (((1,), (1,)), ((), ()))
    controls = wells.shape[1]

    def chunk(c, carry):
        span = pl.ds(pl.multiple_of(c * CHUNK, CHUNK), CHUNK)
        share = profile[span, :]
        share_high = share.astype(jnp.bfloat16)
        share_low = (share - share_high.astype(jnp.float32)).astype(jnp.bfloat16)
        first = lax.dot_general(both, share_high, contract, preferred_element_type=jnp.float32)
        second = lax.dot_general(high, share_low, contract, preferred_element_type=jnp.float32)
        product = first[:count] + first[count:] + second
        chosen = jnp.where(ids == wells[:, span], product, 0.0)
        out[:, span] = jnp.sum(chosen, axis=0, keepdims=True)
        return carry

    lax.fori_loop(0, controls // CHUNK, chunk, 0)
    whole = jnp.sum(jnp.sum(objective[...], axis=0, keepdims=True), axis=1, keepdims=True)
    out[:, controls:] = jnp.broadcast_to(whole * scale, (1, LANES))


def shape(*dims):
    return jax.ShapeDtypeStruct(dims, jnp.float32)


def same(x, count):
    return x


def partner_a(x, count):
    return x ^ 1


def partner_b(x, count):
    other = x + 1 if x % 2 else x - 1
    return other if 0 <= other < count else None


AXES = ("gx", "gy", "sa")


def swap_pairs(partner, kind, count_x, count_y, count_s):
    pairs = []
    for x in range(count_x):
        for y in range(count_y):
            for s in range(count_s):
                from_x, from_s = partner(x, count_x), s
                from_y = y if kind == "tile" else 1 - y if kind is None else (y + 1 if kind else y - 1)
                if from_x is None:
                    from_x, from_y, from_s = x, y, s ^ 1
                if 0 <= from_y < count_y:
                    pairs.append(
                        ((from_x * count_y + from_y) * count_s + from_s, (x * count_y + y) * count_s + s)
                    )
    return pairs


def exchange(tiles, strips, kinds):
    counts = [lax.axis_size(axis) for axis in AXES]
    got = [
        lax.ppermute(tile, AXES, swap_pairs(partner, "tile", *counts))
        for tile, partner in zip(tiles, (partner_a, partner_b))
    ]
    got_strips = []
    for k, kind in enumerate(kinds):
        for strip, partner in zip(strips[3 * k : 3 * k + 3], (same, partner_a, partner_b)):
            got_strips.append(lax.ppermute(strip, AXES, swap_pairs(partner, kind, *counts)))
    return got, got_strips


def total_over(value, axes):
    count = 1
    for axis in axes:
        count *= lax.axis_size(axis)
    bit = 1
    while bit < count:
        bits = [bit] if 2 * bit >= count else [bit, 2 * bit, 3 * bit]
        got = [lax.ppermute(value, axes, [(i, i ^ b) for i in range(count)]) for b in bits]
        value = value + got[0]
        if len(got) == 3:
            value = value + (got[1] + got[2])
        bit *= 4
    return value


def local(initial, retard, velx, vely, monitor, controls, profile, wells, ranking):
    samples, layers, width_x, width_y = initial.shape
    count_x, count_y = lax.axis_size("gx"), lax.axis_size("gy")
    assert (samples, layers, width_x, width_y) == (4, 4, OWN, LANES)
    assert count_x % 2 == 0 and lax.axis_size("sa") == 2
    number = controls.shape[0]
    assert number % CHUNK == 0
    kinds = strip_kinds(count_y)
    n = len(kinds)
    half_tile = shape(4, samples, layers, DEPTH, LANES)
    hbm = pl.BlockSpec(memory_space=pltpu.HBM)
    any_space = pl.BlockSpec(memory_space=pl.ANY)
    own, *sent, monitor, controls, wells = pl.pallas_call(
        stage_kernel,
        out_shape=(
            shape(4, samples, layers, OWN, LANES),
            half_tile,
            half_tile,
            shape(*monitor.shape),
            shape(1, number),
            jax.ShapeDtypeStruct((1, number), jnp.int32),
        ),
        in_specs=[hbm] * 7,
        out_specs=(any_space,) * 6,
        scratch_shapes=[pltpu.SemaphoreType.DMA((15,))],
        compiler_params=params(),
        name="stage",
    )(initial, retard, velx, vely, monitor, controls.reshape(1, -1), wells.reshape(1, -1))
    own = own.reshape(4, -1, LANES)
    sent_strips = pl.pallas_call(
        functools.partial(strip_pack_kernel, kinds),
        out_shape=(
            shape(INNER, 2, SUBLANES, LANES),
            shape(INNER // 2, 2, SUBLANES, LANES),
            shape(INNER // 2, 2, SUBLANES, LANES),
        )
        * n,
        in_specs=[vmem()],
        out_specs=(vmem(),) * (3 * n),
        compiler_params=params(),
        name="strips",
    )(own)
    got, got_strips = exchange(sent, sent_strips, kinds)
    tile_shape = shape(EXT, 2, SUBLANES, LANES)
    strip_shape = shape(INNER, 2, SUBLANES, LANES)
    blocks = (1 + n) * EXT * layers
    prepared = pl.pallas_call(
        functools.partial(source_kernel, kinds),
        out_shape=(tile_shape,)
        + (strip_shape,) * n
        + (tile_shape,) * 5
        + (shape(4, INNER, 2, SUBLANES, LANES),),
        in_specs=[vmem()] * 4,
        out_specs=(vmem(),) * (1 + n + 5 + 1),
        scratch_shapes=[
            pltpu.VMEM((blocks, 2 * LANES), jnp.float32),
            pltpu.VMEM((blocks, LANES), jnp.float32),
        ],
        compiler_params=params(),
        name="source",
    )(wells, controls, profile, own)
    got = [part.reshape(4, -1, LANES) for part in got]
    tail_count = samples * lax.axis_size("sa") // 2
    half_start = shape(DEPTH, 2, SUBLANES, LANES)
    smem = pl.BlockSpec(memory_space=pltpu.SMEM)
    first_tile = 4 + 3 * n + 1 + n
    final, start_a, start_b, objective, *rest = pl.pallas_call(
        functools.partial(forward_kernel, kinds, tail_count),
        out_shape=(
            shape(samples * layers * OWN, LANES),
            half_start,
            half_start,
            shape(SUBLANES, LANES),
        )
        + (tile_shape,) * 5
        + (strip_shape,) * (5 * n)
        + (
            shape(INNER // 2, SUBLANES, LANES),
            shape(INNER // 4, SUBLANES, LANES),
            shape(INNER // 4, SUBLANES, LANES),
        )
        * n,
        in_specs=[vmem(), smem] + [vmem()] * (2 + 3 * n + 1 + n + 5 + 1),
        out_specs=(vmem(),) * (4 + 5 + 5 * n + 3 * n),
        scratch_shapes=[pltpu.VMEM((OWN, 2, SUBLANES, LANES), jnp.float32)],
        input_output_aliases={first_tile + k: 4 + k for k in range(5)},
        compiler_params=params(),
        name="forward",
    )(monitor.reshape(-1, LANES), ranking, *got, *got_strips, *prepared)
    tile, strips, start_strips = split_refs(rest, 5, 5 * n, 3 * n)
    start = (start_a, start_b)
    got_start, got_start_strips = exchange(start, start_strips, kinds)
    strip_coefs = [strips[5 * k + c] for k in range(n) for c in range(1, 5)]
    cells = layers * OWN * count_x * LANES * count_y
    summed = pl.pallas_call(
        functools.partial(adjoint_kernel, kinds, 0.5 / (tail_count * cells)),
        out_shape=shape(1, number + LANES),
        in_specs=[vmem()] * (4 + 3 * n + 4 + 4 * n + 3),
        out_specs=vmem(),
        scratch_shapes=[
            pltpu.VMEM((EXT, 2, SUBLANES, LANES), jnp.float32),
            pltpu.VMEM((OWN, 2, SUBLANES, LANES), jnp.float32),
        ]
        + [pltpu.VMEM((INNER, 2, SUBLANES, LANES), jnp.float32)] * (2 * n)
        + [pltpu.VMEM((OWN * layers, LANES), jnp.float32)],
        compiler_params=params(),
        name="adjoint",
    )(
        *start,
        *got_start,
        *got_start_strips,
        *tile[1:],
        *strip_coefs,
        objective,
        wells,
        profile,
    )
    summed = total_over(summed, AXES)
    return final.reshape(initial.shape), summed[0, :number], summed[0, number : number + 1]


def solution(mesh):
    in_specs = (
        P(("groups", "sa"), None, "gx", "gy"),
        P(("groups", "sa"), None, "gx", "gy"),
        P(("groups", "sa"), None, "gx", "gy"),
        P(("groups", "sa"), None, "gx", "gy"),
        P("groups", "gx", "gy"),
        P("groups"),
        P("groups", None),
        P("groups"),
        P(("groups", "sa")),
    )
    out_specs = (P(("groups", "sa"), None, "gx", "gy"), P("groups"), P("groups"))
    return jax.shard_map(local, mesh=mesh, in_specs=in_specs, out_specs=out_specs, check_vma=False)
```

```python
import functools

import jax
import jax.numpy as jnp
from jax import lax
from jax.experimental import pallas as pl
from jax.experimental.pallas import tpu as pltpu
from jax.sharding import PartitionSpec as P

ITERS = 16
KAPPA = 0.1
VERT = 0.05
LANES = 128
SUBLANES = 8
DEPTH = ITERS
OWN = 2 * DEPTH
EXT = OWN + 2 * DEPTH
WIDE = 2 * DEPTH
GROUPS = LANES // WIDE
INNER = EXT // GROUPS
JOIN = ITERS // 2
CHUNK = 512
VMEM_LIMIT = 24 * 1024 * 1024


def vmem():
    return pl.BlockSpec(memory_space=pltpu.VMEM)


def params():
    return pltpu.CompilerParams(vmem_limit_bytes=VMEM_LIMIT)


def sub_id():
    return lax.broadcasted_iota(jnp.int32, (SUBLANES, LANES), 0)


def lane_id():
    return lax.broadcasted_iota(jnp.int32, (SUBLANES, LANES), 1)


def wrap(shift):
    return shift % LANES if isinstance(shift, int) else lax.rem(shift, LANES)


def lane_roll(value, shift):
    if isinstance(shift, int) and shift % LANES == 0:
        return value
    return pltpu.roll(value, wrap(shift), 1)


def pick(flag, yes, no):
    if isinstance(flag, bool):
        return yes if flag else no
    return jnp.where(flag, yes, no)


def odd_tile():
    return lax.rem(lax.axis_index("gx"), 2)


def lacks_b():
    x = lax.axis_index("gx")
    return (x == 0) | (x == lax.axis_size("gx") - 1)


def strip_kinds(count):
    return (None,) if count == 2 else (True, False)


def is_right(kind):
    return lax.axis_index("gy") == 0 if kind is None else kind


def planes(ref, row, half, rows):
    return ref[pl.ds(half * rows + row, SUBLANES, stride=2 * rows), :]


def stage_kernel(initial, retard, velx, vely, monitor, controls, wells, *refs):
    own, out_a, out_b, out_monitor, out_controls, out_wells, sems = refs
    odd = odd_tile()
    pairs = [(monitor, out_monitor), (controls, out_controls), (wells, out_wells)]
    for field, ref in enumerate((initial, retard, velx, vely)):
        for out, base in ((out_a, DEPTH * (1 - odd)), (out_b, DEPTH * odd)):
            source = ref.at[:, :, pl.ds(pl.multiple_of(base, DEPTH), DEPTH), :]
            pairs.append((source, out.at[field]))
        pairs.append((ref, own.at[field]))
    copies = [pltpu.make_async_copy(*pair, sems.at[k]) for k, pair in enumerate(pairs)]
    for copy in copies:
        copy.start()
    for copy in copies:
        copy.wait()


def edge_offset(kind):
    return DEPTH * (1 - lax.axis_index("gy")) if kind is None else (0 if kind else DEPTH)


def strip_pack_kernel(kinds, own, *outs):
    odd = odd_tile()
    slot = lane_id() // DEPTH
    for number, kind in enumerate(kinds):
        to_y, to_a, to_b = outs[3 * number : 3 * number + 3]
        offset = edge_offset(kind)

        def put(packed, field, row, half, target):
            moved = lane_roll(planes(own.at[field], row, half, OWN), DEPTH * target + offset)
            return moved if packed is None else jnp.where(slot == target, moved, packed)

        for half in range(2):
            for i in range(INNER):
                packed = None
                for field in range(4):
                    for j in range(2):
                        target = 4 * (field // 2) + 2 * j + field % 2
                        packed = put(packed, field, INNER * j + i, half, target)
                to_y[i, half] = packed
            for out, base in ((to_a, DEPTH * (1 - odd)), (to_b, DEPTH * odd)):
                for i in range(INNER // 2):
                    packed = None
                    for field in range(4):
                        for upper in range(2):
                            row = base + INNER // 2 * upper + i
                            packed = put(packed, field, row, half, 4 * upper + field)
                    out[i, half] = packed


def coefficients(retard, velx, vely):
    spread = KAPPA * retard
    from_x = retard * velx + spread
    from_y = retard * vely + spread
    keep = 1.0 - (from_x + from_y + (2.0 + 2.0 * VERT / KAPPA) * spread)
    return keep, from_x, from_y, spread


def store_tile(refs, row, half, raw, source=None):
    state, retard, velx, vely = raw
    keep, from_x, from_y, spread = coefficients(retard, velx, vely)
    from_y = jnp.where(lane_id() == 0, 0.0, from_y)
    for ref, value in zip(refs, (state, keep, from_x, from_y, spread)):
        ref[row, half] = value


def source_kernel(kinds, wells, controls, profile, own, *refs):
    n = len(kinds)
    sources, tile, edges, (acc, acc_low) = split_refs(refs, 1 + n, 5, 1, 2)
    for x in range(OWN):
        for half in range(2):
            raw = [planes(own.at[field], x, half, OWN) for field in range(4)]
            store_tile(tile, DEPTH + x, half, raw)
    first_j = lane_id() // WIDE == 1
    for field in range(4):
        for i in range(INNER):
            for half in range(2):
                moved = [
                    lane_roll(planes(own.at[field], INNER * j + i, half, OWN), WIDE * (j + 1) + DEPTH)
                    for j in range(2)
                ]
                edges[0][field, i, half] = jnp.where(first_j, *moved)

    x_index, y_index = lax.axis_index("gx"), lax.axis_index("gy")
    all_x, all_blocks = OWN * lax.axis_size("gx"), lax.axis_size("gy")
    layers = 4
    per_block = EXT * layers
    r = lax.broadcasted_iota(jnp.int32, (per_block, 1), 0)
    x = x_index * OWN - DEPTH + r // layers
    ids = []
    for block in [y_index] + [
        1 - y_index if kind is None else (y_index + 1 if kind else y_index - 1) for kind in kinds
    ]:
        inside = (x >= 0) & (x < all_x) & (block >= 0) & (block < all_blocks)
        ids.append(jnp.where(inside, ((r % layers) * all_x + x) * all_blocks + block, -1))
    ids = jnp.concatenate(ids, axis=0)
    acc[...] = jnp.zeros_like(acc)
    acc_low[...] = jnp.zeros_like(acc_low)

    def chunk(c, carry):
        span = pl.ds(pl.multiple_of(c * CHUNK, CHUNK), CHUNK)
        part = profile[span, :]
        high = part.astype(jnp.bfloat16)
        low = (part - high.astype(jnp.float32)).astype(jnp.bfloat16)
        rate = controls[:, span]
        rate_high = rate.astype(jnp.bfloat16).astype(jnp.float32)
        hit = ids == wells[:, span]
        hot_high = jnp.where(hit, rate_high, 0.0).astype(jnp.bfloat16)
        hot_low = jnp.where(hit, rate - rate_high, 0.0).astype(jnp.bfloat16)
        acc[...] += jnp.dot(
            hot_high, jnp.concatenate([high, low], axis=1), preferred_element_type=jnp.float32
        )
        acc_low[...] += jnp.dot(hot_low, high, preferred_element_type=jnp.float32)
        return carry

    lax.fori_loop(0, wells.shape[1] // CHUNK, chunk, 0)
    acc_low[...] += acc[:, :LANES] + acc[:, LANES:]
    upper = sub_id() % 2 == 1
    group = lane_id() // WIDE

    def both(first, half):
        low_layer = jnp.broadcast_to(acc_low[pl.ds(first + half, 1), :], (SUBLANES, LANES))
        high_layer = jnp.broadcast_to(acc_low[pl.ds(first + 2 + half, 1), :], (SUBLANES, LANES))
        return jnp.where(upper, high_layer, low_layer)

    masks = Masks(kinds)
    for number in range(n):
        for i in range(INNER):
            for half in range(2):
                packed = None
                for j in range(GROUPS):
                    e = j * INNER + i
                    here = both(e * layers, half)
                    if number == 0:
                        sources[0][e, half] = here
                    beside = both((number + 1) * per_block + e * layers, half)
                    mixed = jnp.where(masks.own_edge[number], here, beside)
                    moved = lane_roll(mixed, WIDE * j + DEPTH)
                    packed = moved if packed is None else jnp.where(group == j, moved, packed)
                sources[1 + number][i, half] = packed


class Masks:
    def __init__(self, kinds):
        lane = lane_id()
        self.first, self.last = lane == 0, lane == LANES - 1
        self.group = lane // WIDE
        upper = sub_id() % 2 == 1
        self.below = jnp.where(upper, VERT / KAPPA, 0.0)
        self.above = jnp.where(upper, 0.0, VERT / KAPPA)
        self.right = [is_right(kind) for kind in kinds]
        half, eighth, sixteenth = lane % WIDE // DEPTH, lane // DEPTH, lane // JOIN
        self.rim = [half == pick(right, 1, 0) for right in self.right]
        self.not_rim = [half == pick(right, 0, 1) for right in self.right]
        self.own_edge = [eighth != pick(right, 0, LANES // DEPTH - 1) for right in self.right]
        self.outer = [sixteenth == pick(right, LANES // JOIN - 1, 0) for right in self.right]

    def vertical(self, pair):
        low = (VERT / KAPPA) * pair[1] + self.below * pltpu.roll(pair[1], 1, 0)
        high = (VERT / KAPPA) * pair[0] + self.above * pltpu.roll(pair[0], SUBLANES - 1, 0)
        return low, high

    def outer_from(self, strips, e, half, value):
        j, i = divmod(e, INNER)
        for strip, outer in zip(strips, self.outer):
            value = jnp.where(outer, lane_roll(strip[i, half], LANES - DEPTH - WIDE * j), value)
        return value

    def join(self, tile, strips, first, last):
        for e in range(first, last + 1):
            j, i = divmod(e, INNER)
            for h in range(2):
                value = self.outer_from(strips, e, h, tile[e, h])
                tile[e, h] = value
                moved = lane_roll(value, WIDE * j + DEPTH)
                for strip, own in zip(strips, self.not_rim):
                    strip[i, h] = jnp.where((self.group == j) & own, moved, strip[i, h])


def places(odd):
    return DEPTH * (2 - odd), DEPTH * (1 + odd), 3 * DEPTH * (1 - odd), 3 * DEPTH * odd


def merge_strip(masks, number, odd, middle, own_a, own_b, rim_y, rim_a, rim_b):
    inner = (masks.group == 1) | (masks.group == 2)
    at_a = masks.group == 3 * (1 - odd)
    own = jnp.where(inner, middle, jnp.where(at_a, own_a, own_b))
    rim = jnp.where(inner, rim_y, jnp.where(at_a, rim_a, rim_b))
    return jnp.where(masks.rim[number], rim, own)


def forward_step(masks, tile, strips, first, last, sourced):
    state, keep, from_x, from_y, spread, source = tile
    before = [state[first - 1, h] for h in range(2)]
    here = [state[first, h] for h in range(2)]
    for e in range(first, last + 1):
        after = [state[e + 1, h] for h in range(2)]
        upright = masks.vertical(here)
        for h in range(2):
            y_high = jnp.where(masks.last, 0.0, lane_roll(here[h], LANES - 1))
            value = (
                keep[e, h] * here[h]
                + from_x[e, h] * before[h]
                + from_y[e, h] * lane_roll(here[h], 1)
                + spread[e, h] * (after[h] + y_high + upright[h])
            )
            state[e, h] = value + source[e, h] if sourced else value
        before, here = here, after
    for strip, keep, from_x, from_y, spread, source in strips:
        old = [strip[0, h] for h in range(2)]
        here = old
        before = [lane_roll(strip[INNER - 1, h], WIDE) for h in range(2)]
        for i in range(INNER):
            if i < INNER - 1:
                after = [strip[i + 1, h] for h in range(2)]
            else:
                after = [lane_roll(value, LANES - WIDE) for value in old]
            upright = masks.vertical(here)
            for h in range(2):
                value = (
                    keep[i, h] * here[h]
                    + from_x[i, h] * before[h]
                    + from_y[i, h] * lane_roll(here[h], 1)
                    + spread[i, h] * (after[h] + lane_roll(here[h], LANES - 1) + upright[h])
                )
                strip[i, h] = value + source[i, h] if sourced else value
            before, here = here, after


def adjoint_step(masks, tile, strips, first, last):
    state, keep, from_x, from_y, spread, total = tile

    def row(refs, e):
        state, _, from_x, from_y, spread, _ = refs
        value = [state[e, h] for h in range(2)]
        return (
            value,
            [from_x[e, h] * value[h] for h in range(2)],
            [from_y[e, h] * value[h] for h in range(2)],
            [spread[e, h] * value[h] for h in range(2)],
        )

    before, here = row(tile, first - 1), row(tile, first)
    for e in range(first, last + 1):
        after = row(tile, e + 1)
        value, _, by_y, by_spread = here
        upright = masks.vertical(by_spread)
        for h in range(2):
            y_low = jnp.where(masks.first, 0.0, lane_roll(by_spread[h], 1))
            fresh = (
                keep[e, h] * value[h]
                + (after[1][h] + before[3][h])
                + (y_low + lane_roll(by_y[h], LANES - 1))
                + upright[h]
            )
            state[e, h] = fresh
            if DEPTH <= e < DEPTH + OWN:
                total[e - DEPTH, h] += fresh
        before, here = here, after
    for refs in strips:
        strip, keep, from_x, from_y, spread, total = refs
        here = row(refs, 0)
        wrapped = [lane_roll(value, LANES - WIDE) for value in here[1]]
        last_row = row(refs, INNER - 1)
        before = (None, None, None, [lane_roll(value, WIDE) for value in last_row[3]])
        for i in range(INNER):
            after = row(refs, i + 1) if i < INNER - 1 else (None, wrapped, None, None)
            value, _, by_y, by_spread = here
            upright = masks.vertical(by_spread)
            for h in range(2):
                fresh = (
                    keep[i, h] * value[h]
                    + (after[1][h] + before[3][h])
                    + (lane_roll(by_spread[h], 1) + lane_roll(by_y[h], LANES - 1))
                    + upright[h]
                )
                strip[i, h] = fresh
                total[i, h] += fresh
            before, here = here, after


def sweep(step, join):
    for t in range(ITERS):
        if t == JOIN:
            join(t, EXT - 1 - t)
        step(t + 1, EXT - 2 - t, t < ITERS - 1)


def split_refs(refs, *counts):
    out = []
    for count in counts:
        out.append(refs[:count])
        refs = refs[count:]
    return out


def forward_kernel(kinds, tail_count, *refs):
    n = len(kinds)
    ins, got_strips, sources, tile, edges, outs, strips, out_strips, (start,) = split_refs(
        refs, 4, 3 * n, 1 + n, 5, 1, 4 + 5, 5 * n, 3 * n, 1
    )
    monitor, ranking, got_a, got_b = ins
    final, start_a, start_b, objective, *tile = outs
    odd = odd_tile()
    masks = Masks(kinds)
    state = tile[0]
    _, _, at_a, at_b = places(odd)
    present = jnp.where(lacks_b(), 0.0, 1.0)
    for x in range(DEPTH):
        for h in range(2):
            raw_a = [planes(got_a.at[field], x, h, DEPTH) for field in range(4)]
            raw_b = [planes(got_b.at[field], x, h, DEPTH) for field in range(4)]
            raw_b[:2] = [value * present for value in raw_b[:2]]
            store_tile(tile, at_a + x, h, raw_a)
            store_tile(tile, at_b + x, h, raw_b)
            i = x
            upper = i // (INNER // 2)
            for k in range(n):
                got = got_strips[3 * k : 3 * k + 3]
                side = pick(masks.right[k], DEPTH, 0)
                raw = []
                for field in range(4):
                    slot = DEPTH * (4 * upper + field)
                    rim_b = got[2][i % (INNER // 2), h]
                    rim_b = lane_roll(rim_b, 2 * at_b + side + LANES - slot)
                    raw.append(
                        merge_strip(
                            masks,
                            k,
                            odd,
                            edges[0][field, i, h],
                            lane_roll(raw_a[field], 2 * at_a + DEPTH),
                            lane_roll(raw_b[field], 2 * at_b + DEPTH),
                            lane_roll(
                                got[0][i, h], LANES + WIDE + side - 64 * (field // 2) - DEPTH * (field % 2)
                            ),
                            lane_roll(
                                got[1][i % (INNER // 2), h], 2 * at_a + side + LANES - slot
                            ),
                            rim_b * present if field < 2 else rim_b,
                        )
                    )
                mine = strips[5 * k : 5 * k + 5]
                for ref, value in zip(mine, (raw[0] + sources[1 + k][i, h], *coefficients(*raw[1:]))):
                    ref[i, h] = value
    for e in range(EXT):
        for h in range(2):
            state[e, h] += sources[0][e, h]
    strip_refs = [(*strips[5 * k : 5 * k + 5], sources[1 + k]) for k in range(n)]
    strip_states = [strip[0] for strip in strip_refs]

    def step(first, last, sourced):
        forward_step(masks, (*tile, sources[0]), strip_refs, first, last, sourced)

    sweep(step, functools.partial(masks.join, state, strip_states))

    sample = sub_id() // 2
    upper = sub_id() % 2 == 1
    tail = jnp.zeros((SUBLANES, LANES), jnp.float32)
    for s in range(4):
        tail = jnp.where(sample == s, jnp.where(ranking[s] < tail_count, 1.0, 0.0), tail)
    sums = [jnp.zeros((SUBLANES, LANES), jnp.float32) for _ in range(4)]
    for x in range(OWN):
        for h in range(2):
            fresh = masks.outer_from(strip_states, DEPTH + x, h, state[DEPTH + x, h])
            final[pl.ds(h * OWN + x, SUBLANES, stride=2 * OWN), :] = fresh
            low = jnp.broadcast_to(monitor[pl.ds(h * OWN + x, 1), :], (SUBLANES, LANES))
            high = jnp.broadcast_to(monitor[pl.ds((2 + h) * OWN + x, 1), :], (SUBLANES, LANES))
            weighted = tail * jnp.where(upper, high, low) * fresh
            start[x, h] = weighted * (1.0 / (tail_count * ITERS))
            sums[x % 4] = sums[x % 4] + weighted * fresh
    objective[...] = (sums[0] + sums[1]) + (sums[2] + sums[3])

    base_a, base_b = DEPTH * (1 - odd), DEPTH * odd
    for x in range(DEPTH):
        for h in range(2):
            start_a[x, h] = start[base_a + x, h]
            start_b[x, h] = start[base_b + x, h]
    slot = lane_id() // DEPTH
    for k, kind in enumerate(kinds):
        to_y, to_a, to_b = out_strips[3 * k : 3 * k + 3]
        offset = edge_offset(kind)

        def put(packed, row, h, target):
            moved = lane_roll(start[row, h], DEPTH * target + offset)
            return moved if packed is None else jnp.where(slot == target, moved, packed)

        for i in range(INNER // 2):
            packed = None
            for upper_half in range(2):
                for j in range(2):
                    for h in range(2):
                        row = INNER * j + INNER // 2 * upper_half + i
                        packed = put(packed, row, h, 4 * upper_half + 2 * j + h)
            to_y[i] = packed
        for out, base in ((to_a, base_a), (to_b, base_b)):
            for i in range(INNER // 4):
                packed = None
                for quarter in range(4):
                    for h in range(2):
                        packed = put(packed, base + INNER // 4 * quarter + i, h, 2 * quarter + h)
                out[i] = packed


def adjoint_kernel(kinds, scale, *refs):
    n = len(kinds)
    parts, part_strips, coefs, strip_coefs, rest, (state, total), strips, (rows,) = split_refs(
        refs, 4, 3 * n, 4, 4 * n, 4, 2, 2 * n, 1
    )
    objective, wells, profile, out = rest
    odd = odd_tile()
    masks = Masks(kinds)
    at = places(odd)
    for part, first in zip(parts, at):
        for x in range(DEPTH):
            for h in range(2):
                state[first + x, h] = part[x, h]
    strip_refs = []
    for k in range(n):
        strip, strip_total = strips[2 * k : 2 * k + 2]
        got_y, got_a, got_b = part_strips[3 * k : 3 * k + 3]
        side = pick(masks.right[k], DEPTH, 0)
        for i in range(INNER):
            eighth, quarter = divmod(i, INNER // 2)[0], divmod(i, INNER // 4)[0]
            for h in range(2):
                moved = [
                    lane_roll(part[i, h], 2 * first + DEPTH) for part, first in zip(parts, at)
                ]
                slot = DEPTH * (2 * quarter + h)
                strip[i, h] = merge_strip(
                    masks,
                    k,
                    odd,
                    jnp.where(masks.group == 2 - odd, moved[0], moved[1]),
                    moved[2],
                    moved[3],
                    lane_roll(got_y[i % (INNER // 2)], LANES + WIDE + side - 64 * eighth - DEPTH * h),
                    lane_roll(got_a[i % (INNER // 4)], 2 * at[2] + side + LANES - slot),
                    lane_roll(got_b[i % (INNER // 4)], 2 * at[3] + side + LANES - slot),
                )
        strip_refs.append((strip, *strip_coefs[4 * k : 4 * k + 4], strip_total))
        strip_total[...] = jnp.zeros_like(strip_total)
    total[...] = jnp.zeros_like(total)
    tile = (state, *coefs, total)

    def step(first, last, _):
        adjoint_step(masks, tile, strip_refs, first, last)

    sweep(step, functools.partial(masks.join, state, [refs[0] for refs in strip_refs]))
    totals = [refs[-1] for refs in strip_refs]
    for x in range(OWN):
        for h in range(2):
            value = masks.outer_from(totals, DEPTH + x, h, total[x, h])
            value = value + pltpu.roll(value, 4, 0)
            value = value + pltpu.roll(value, 2, 0)
            rows[pl.ds((2 * x + h) * 2, 2), :] = value[:2]
    count = rows.shape[0]
    r = lax.broadcasted_iota(jnp.int32, (count, 1), 0)
    layer = (r % 2) * 2 + (r // 2) % 2
    x = lax.axis_index("gx") * OWN + r // 4
    ids = (layer * (OWN * lax.axis_size("gx")) + x) * lax.axis_size("gy") + lax.axis_index("gy")
    field = rows[...]
    high = field.astype(jnp.bfloat16)
    low = (field - high.astype(jnp.float32)).astype(jnp.bfloat16)
    both = jnp.concatenate([high, low], axis=0)
    contract = (((1,), (1,)), ((), ()))
    controls = wells.shape[1]

    def chunk(c, carry):
        span = pl.ds(pl.multiple_of(c * CHUNK, CHUNK), CHUNK)
        share = profile[span, :]
        share_high = share.astype(jnp.bfloat16)
        share_low = (share - share_high.astype(jnp.float32)).astype(jnp.bfloat16)
        first = lax.dot_general(both, share_high, contract, preferred_element_type=jnp.float32)
        second = lax.dot_general(high, share_low, contract, preferred_element_type=jnp.float32)
        product = first[:count] + first[count:] + second
        chosen = jnp.where(ids == wells[:, span], product, 0.0)
        out[:, span] = jnp.sum(chosen, axis=0, keepdims=True)
        return carry

    lax.fori_loop(0, controls // CHUNK, chunk, 0)
    whole = jnp.sum(jnp.sum(objective[...], axis=0, keepdims=True), axis=1, keepdims=True)
    out[:, controls:] = jnp.broadcast_to(whole * scale, (1, LANES))


def shape(*dims):
    return jax.ShapeDtypeStruct(dims, jnp.float32)


def same(x, count):
    return x


def partner_a(x, count):
    return x ^ 1


def partner_b(x, count):
    other = x + 1 if x % 2 else x - 1
    return other if 0 <= other < count else None


AXES = ("gx", "gy", "sa")


def swap_pairs(partner, kind, count_x, count_y, count_s):
    pairs = []
    for x in range(count_x):
        for y in range(count_y):
            for s in range(count_s):
                from_x, from_s = partner(x, count_x), s
                from_y = y if kind == "tile" else 1 - y if kind is None else (y + 1 if kind else y - 1)
                if from_x is None:
                    from_x, from_y, from_s = x, y, s ^ 1
                if 0 <= from_y < count_y:
                    pairs.append(
                        ((from_x * count_y + from_y) * count_s + from_s, (x * count_y + y) * count_s + s)
                    )
    return pairs


def exchange(tiles, strips, kinds):
    counts = [lax.axis_size(axis) for axis in AXES]
    got = [
        lax.ppermute(tile, AXES, swap_pairs(partner, "tile", *counts))
        for tile, partner in zip(tiles, (partner_a, partner_b))
    ]
    got_strips = []
    for k, kind in enumerate(kinds):
        for strip, partner in zip(strips[3 * k : 3 * k + 3], (same, partner_a, partner_b)):
            got_strips.append(lax.ppermute(strip, AXES, swap_pairs(partner, kind, *counts)))
    return got, got_strips


def total_over(value, axes):
    count = 1
    for axis in axes:
        count *= lax.axis_size(axis)
    bit = 1
    while bit < count:
        bits = [bit] if 2 * bit >= count else [bit, 2 * bit, 3 * bit]
        got = [lax.ppermute(value, axes, [(i, i ^ b) for i in range(count)]) for b in bits]
        value = value + got[0]
        if len(got) == 3:
            value = value + (got[1] + got[2])
        bit *= 4
    return value


def local(initial, retard, velx, vely, monitor, controls, profile, wells, ranking):
    samples, layers, width_x, width_y = initial.shape
    count_x, count_y = lax.axis_size("gx"), lax.axis_size("gy")
    assert (samples, layers, width_x, width_y) == (4, 4, OWN, LANES)
    assert count_x % 2 == 0 and lax.axis_size("sa") == 2
    number = controls.shape[0]
    assert number % CHUNK == 0
    kinds = strip_kinds(count_y)
    n = len(kinds)
    half_tile = shape(4, samples, layers, DEPTH, LANES)
    hbm = pl.BlockSpec(memory_space=pltpu.HBM)
    any_space = pl.BlockSpec(memory_space=pl.ANY)
    inputs = (initial, retard, velx, vely, monitor, controls.reshape(1, -1), wells.reshape(1, -1))
    inputs = [pltpu.with_memory_space_constraint(value, pltpu.HBM) for value in inputs]
    own, *sent, monitor, controls, wells = pl.pallas_call(
        stage_kernel,
        out_shape=(
            shape(4, samples, layers, OWN, LANES),
            half_tile,
            half_tile,
            shape(*monitor.shape),
            shape(1, number),
            jax.ShapeDtypeStruct((1, number), jnp.int32),
        ),
        in_specs=[hbm] * 7,
        out_specs=(any_space,) * 6,
        scratch_shapes=[pltpu.SemaphoreType.DMA((15,))],
        compiler_params=params(),
        name="stage",
    )(*inputs)
    own = own.reshape(4, -1, LANES)
    sent_strips = pl.pallas_call(
        functools.partial(strip_pack_kernel, kinds),
        out_shape=(
            shape(INNER, 2, SUBLANES, LANES),
            shape(INNER // 2, 2, SUBLANES, LANES),
            shape(INNER // 2, 2, SUBLANES, LANES),
        )
        * n,
        in_specs=[vmem()],
        out_specs=(vmem(),) * (3 * n),
        compiler_params=params(),
        name="strips",
    )(own)
    got, got_strips = exchange(sent, sent_strips, kinds)
    tile_shape = shape(EXT, 2, SUBLANES, LANES)
    strip_shape = shape(INNER, 2, SUBLANES, LANES)
    blocks = (1 + n) * EXT * layers
    prepared = pl.pallas_call(
        functools.partial(source_kernel, kinds),
        out_shape=(tile_shape,)
        + (strip_shape,) * n
        + (tile_shape,) * 5
        + (shape(4, INNER, 2, SUBLANES, LANES),),
        in_specs=[vmem()] * 4,
        out_specs=(vmem(),) * (1 + n + 5 + 1),
        scratch_shapes=[
            pltpu.VMEM((blocks, 2 * LANES), jnp.float32),
            pltpu.VMEM((blocks, LANES), jnp.float32),
        ],
        compiler_params=params(),
        name="source",
    )(wells, controls, profile, own)
    got = [part.reshape(4, -1, LANES) for part in got]
    tail_count = samples * lax.axis_size("sa") // 2
    half_start = shape(DEPTH, 2, SUBLANES, LANES)
    smem = pl.BlockSpec(memory_space=pltpu.SMEM)
    first_tile = 4 + 3 * n + 1 + n
    final, start_a, start_b, objective, *rest = pl.pallas_call(
        functools.partial(forward_kernel, kinds, tail_count),
        out_shape=(
            shape(samples * layers * OWN, LANES),
            half_start,
            half_start,
            shape(SUBLANES, LANES),
        )
        + (tile_shape,) * 5
        + (strip_shape,) * (5 * n)
        + (
            shape(INNER // 2, SUBLANES, LANES),
            shape(INNER // 4, SUBLANES, LANES),
            shape(INNER // 4, SUBLANES, LANES),
        )
        * n,
        in_specs=[vmem(), smem] + [vmem()] * (2 + 3 * n + 1 + n + 5 + 1),
        out_specs=(vmem(),) * (4 + 5 + 5 * n + 3 * n),
        scratch_shapes=[pltpu.VMEM((OWN, 2, SUBLANES, LANES), jnp.float32)],
        input_output_aliases={first_tile + k: 4 + k for k in range(5)},
        compiler_params=params(),
        name="forward",
    )(monitor.reshape(-1, LANES), ranking, *got, *got_strips, *prepared)
    tile, strips, start_strips = split_refs(rest, 5, 5 * n, 3 * n)
    start = (start_a, start_b)
    got_start, got_start_strips = exchange(start, start_strips, kinds)
    strip_coefs = [strips[5 * k + c] for k in range(n) for c in range(1, 5)]
    cells = layers * OWN * count_x * LANES * count_y
    summed = pl.pallas_call(
        functools.partial(adjoint_kernel, kinds, 0.5 / (tail_count * cells)),
        out_shape=shape(1, number + LANES),
        in_specs=[vmem()] * (4 + 3 * n + 4 + 4 * n + 3),
        out_specs=vmem(),
        scratch_shapes=[
            pltpu.VMEM((EXT, 2, SUBLANES, LANES), jnp.float32),
            pltpu.VMEM((OWN, 2, SUBLANES, LANES), jnp.float32),
        ]
        + [pltpu.VMEM((INNER, 2, SUBLANES, LANES), jnp.float32)] * (2 * n)
        + [pltpu.VMEM((OWN * layers, LANES), jnp.float32)],
        compiler_params=params(),
        name="adjoint",
    )(
        *start,
        *got_start,
        *got_start_strips,
        *tile[1:],
        *strip_coefs,
        objective,
        wells,
        profile,
    )
    summed = total_over(summed, AXES)
    return final.reshape(initial.shape), summed[0, :number], summed[0, number : number + 1]


def solution(mesh):
    in_specs = (
        P(("groups", "sa"), None, "gx", "gy"),
        P(("groups", "sa"), None, "gx", "gy"),
        P(("groups", "sa"), None, "gx", "gy"),
        P(("groups", "sa"), None, "gx", "gy"),
        P("groups", "gx", "gy"),
        P("groups"),
        P("groups", None),
        P("groups"),
        P(("groups", "sa")),
    )
    out_specs = (P(("groups", "sa"), None, "gx", "gy"), P("groups"), P("groups"))
    return jax.shard_map(local, mesh=mesh, in_specs=in_specs, out_specs=out_specs, check_vma=False)
```

```python
import functools

import jax
import jax.numpy as jnp
from jax import lax
from jax.experimental import pallas as pl
from jax.experimental.pallas import tpu as pltpu
from jax.sharding import PartitionSpec as P

ITERS = 16
KAPPA = 0.1
VERT = 0.05
LANES = 128
SUBLANES = 8
DEPTH = ITERS
OWN = 2 * DEPTH
EXT = OWN + 2 * DEPTH
WIDE = 2 * DEPTH
GROUPS = LANES // WIDE
INNER = EXT // GROUPS
JOIN = ITERS // 2
CHUNK = 512
VMEM_LIMIT = 24 * 1024 * 1024


def vmem():
    return pl.BlockSpec(memory_space=pltpu.VMEM)


def params():
    return pltpu.CompilerParams(vmem_limit_bytes=VMEM_LIMIT)


def sub_id():
    return lax.broadcasted_iota(jnp.int32, (SUBLANES, LANES), 0)


def lane_id():
    return lax.broadcasted_iota(jnp.int32, (SUBLANES, LANES), 1)


def wrap(shift):
    return shift % LANES if isinstance(shift, int) else lax.rem(shift, LANES)


def lane_roll(value, shift):
    if isinstance(shift, int) and shift % LANES == 0:
        return value
    return pltpu.roll(value, wrap(shift), 1)


def pick(flag, yes, no):
    if isinstance(flag, bool):
        return yes if flag else no
    return jnp.where(flag, yes, no)


def odd_tile():
    return lax.rem(lax.axis_index("gx"), 2)


def lacks_b():
    x = lax.axis_index("gx")
    return (x == 0) | (x == lax.axis_size("gx") - 1)


def strip_kinds(count):
    return (None,) if count == 2 else (True, False)


def is_right(kind):
    return lax.axis_index("gy") == 0 if kind is None else kind


def planes(ref, row, half, rows):
    return ref[pl.ds(half * rows + row, SUBLANES, stride=2 * rows), :]


def copy_all(pairs, sems):
    copies = [pltpu.make_async_copy(*pair, sems.at[k]) for k, pair in enumerate(pairs)]
    for copy in copies:
        copy.start()
    for copy in copies:
        copy.wait()


def rims_kernel(initial, retard, velx, vely, out_a, out_b, sems):
    odd = odd_tile()
    pairs = []
    for field, ref in enumerate((initial, retard, velx, vely)):
        for out, base in ((out_a, DEPTH * (1 - odd)), (out_b, DEPTH * odd)):
            source = ref.at[:, :, pl.ds(pl.multiple_of(base, DEPTH), DEPTH), :]
            pairs.append((source, out.at[field]))
    copy_all(pairs, sems)


def edge_offset(kind):
    return DEPTH * (1 - lax.axis_index("gy")) if kind is None else (0 if kind else DEPTH)


def strip_pack_kernel(kinds, *refs):
    ins, (own, *copied), outs, (sems,) = split_refs(refs, 7, 4, 3 * len(kinds), 1)
    pairs = [(ref, own.at[field]) for field, ref in enumerate(ins[:4])]
    copy_all(pairs + list(zip(ins[4:], copied)), sems)
    odd = odd_tile()
    slot = lane_id() // DEPTH
    for number, kind in enumerate(kinds):
        to_y, to_a, to_b = outs[3 * number : 3 * number + 3]
        offset = edge_offset(kind)

        def put(packed, field, row, half, target):
            moved = lane_roll(planes(own.at[field], row, half, OWN), DEPTH * target + offset)
            return moved if packed is None else jnp.where(slot == target, moved, packed)

        for half in range(2):
            for i in range(INNER):
                packed = None
                for field in range(4):
                    for j in range(2):
                        target = 4 * (field // 2) + 2 * j + field % 2
                        packed = put(packed, field, INNER * j + i, half, target)
                to_y[i, half] = packed
            for out, base in ((to_a, DEPTH * (1 - odd)), (to_b, DEPTH * odd)):
                for i in range(INNER // 2):
                    packed = None
                    for field in range(4):
                        for upper in range(2):
                            row = base + INNER // 2 * upper + i
                            packed = put(packed, field, row, half, 4 * upper + field)
                    out[i, half] = packed


def coefficients(retard, velx, vely):
    spread = KAPPA * retard
    from_x = retard * velx + spread
    from_y = retard * vely + spread
    keep = 1.0 - (from_x + from_y + (2.0 + 2.0 * VERT / KAPPA) * spread)
    return keep, from_x, from_y, spread


def store_tile(refs, row, half, raw, source=None):
    state, retard, velx, vely = raw
    keep, from_x, from_y, spread = coefficients(retard, velx, vely)
    from_y = jnp.where(lane_id() == 0, 0.0, from_y)
    for ref, value in zip(refs, (state, keep, from_x, from_y, spread)):
        ref[row, half] = value


def source_kernel(kinds, wells, controls, profile, own, *refs):
    n = len(kinds)
    sources, tile, edges, (saved, split), (acc, acc_low) = split_refs(refs, 1 + n, 5, 1, 2, 2)
    for x in range(OWN):
        for half in range(2):
            raw = [planes(own.at[field], x, half, OWN) for field in range(4)]
            store_tile(tile, DEPTH + x, half, raw)
    first_j = lane_id() // WIDE == 1
    for field in range(4):
        for i in range(INNER):
            for half in range(2):
                moved = [
                    lane_roll(planes(own.at[field], INNER * j + i, half, OWN), WIDE * (j + 1) + DEPTH)
                    for j in range(2)
                ]
                edges[0][field, i, half] = jnp.where(first_j, *moved)

    x_index, y_index = lax.axis_index("gx"), lax.axis_index("gy")
    all_x, all_blocks = OWN * lax.axis_size("gx"), lax.axis_size("gy")
    layers = 4
    per_block = EXT * layers
    r = lax.broadcasted_iota(jnp.int32, (per_block, 1), 0)
    x = x_index * OWN - DEPTH + r // layers
    ids = []
    for block in [y_index] + [
        1 - y_index if kind is None else (y_index + 1 if kind else y_index - 1) for kind in kinds
    ]:
        inside = (x >= 0) & (x < all_x) & (block >= 0) & (block < all_blocks)
        ids.append(jnp.where(inside, ((r % layers) * all_x + x) * all_blocks + block, -1))
    ids = jnp.concatenate(ids, axis=0)
    acc[...] = jnp.zeros_like(acc)
    acc_low[...] = jnp.zeros_like(acc_low)

    def chunk(c, carry):
        span = pl.ds(pl.multiple_of(c * CHUNK, CHUNK), CHUNK)
        part = profile[span, :]
        high = part.astype(jnp.bfloat16)
        low = (part - high.astype(jnp.float32)).astype(jnp.bfloat16)
        rate = controls[:, span]
        rate_high = rate.astype(jnp.bfloat16).astype(jnp.float32)
        hit = ids == wells[:, span]
        hot_high = jnp.where(hit, rate_high, 0.0).astype(jnp.bfloat16)
        hot_low = jnp.where(hit, rate - rate_high, 0.0).astype(jnp.bfloat16)
        split_part = jnp.concatenate([high, low], axis=1)
        split[span, :] = split_part
        acc[...] += jnp.dot(hot_high, split_part, preferred_element_type=jnp.float32)
        acc_low[...] += jnp.dot(hot_low, high, preferred_element_type=jnp.float32)
        return carry

    lax.fori_loop(0, wells.shape[1] // CHUNK, chunk, 0)
    acc_low[...] += acc[:, :LANES] + acc[:, LANES:]
    upper = sub_id() % 2 == 1
    group = lane_id() // WIDE

    def both(first, half):
        low_layer = jnp.broadcast_to(acc_low[pl.ds(first + half, 1), :], (SUBLANES, LANES))
        high_layer = jnp.broadcast_to(acc_low[pl.ds(first + 2 + half, 1), :], (SUBLANES, LANES))
        return jnp.where(upper, high_layer, low_layer)

    masks = Masks(kinds)
    for number in range(n):
        for i in range(INNER):
            for half in range(2):
                packed = None
                for j in range(GROUPS):
                    e = j * INNER + i
                    here = both(e * layers, half)
                    if number == 0:
                        sources[0][e, half] = here
                    beside = both((number + 1) * per_block + e * layers, half)
                    mixed = jnp.where(masks.own_edge[number], here, beside)
                    moved = lane_roll(mixed, WIDE * j + DEPTH)
                    packed = moved if packed is None else jnp.where(group == j, moved, packed)
                sources[1 + number][i, half] = packed
    for x in range(OWN):
        for half in range(2):
            tile[0][DEPTH + x, half] += sources[0][DEPTH + x, half]
    ahead(functools.partial(forward_step, masks, (*tile, sources[0]), sourced=True), tile[0], saved)


class Masks:
    def __init__(self, kinds):
        lane = lane_id()
        self.first, self.last = lane == 0, lane == LANES - 1
        self.group = lane // WIDE
        upper = sub_id() % 2 == 1
        self.below = jnp.where(upper, VERT / KAPPA, 0.0)
        self.above = jnp.where(upper, 0.0, VERT / KAPPA)
        self.right = [is_right(kind) for kind in kinds]
        half, eighth, sixteenth = lane % WIDE // DEPTH, lane // DEPTH, lane // JOIN
        self.rim = [half == pick(right, 1, 0) for right in self.right]
        self.not_rim = [half == pick(right, 0, 1) for right in self.right]
        self.own_edge = [eighth != pick(right, 0, LANES // DEPTH - 1) for right in self.right]
        self.outer = [sixteenth == pick(right, LANES // JOIN - 1, 0) for right in self.right]

    def vertical(self, pair):
        low = (VERT / KAPPA) * pair[1] + self.below * pltpu.roll(pair[1], 1, 0)
        high = (VERT / KAPPA) * pair[0] + self.above * pltpu.roll(pair[0], SUBLANES - 1, 0)
        return low, high

    def outer_from(self, strips, e, half, value):
        j, i = divmod(e, INNER)
        for strip, outer in zip(strips, self.outer):
            value = jnp.where(outer, lane_roll(strip[i, half], LANES - DEPTH - WIDE * j), value)
        return value

    def join(self, tile, strips, first, last):
        for e in range(first, last + 1):
            j, i = divmod(e, INNER)
            for h in range(2):
                value = self.outer_from(strips, e, h, tile[e, h])
                tile[e, h] = value
                moved = lane_roll(value, WIDE * j + DEPTH)
                for strip, own in zip(strips, self.not_rim):
                    strip[i, h] = jnp.where((self.group == j) & own, moved, strip[i, h])


def places(odd):
    return DEPTH * (2 - odd), DEPTH * (1 + odd), 3 * DEPTH * (1 - odd), 3 * DEPTH * odd


def merge_strip(masks, number, odd, middle, own_a, own_b, rim_y, rim_a, rim_b):
    inner = (masks.group == 1) | (masks.group == 2)
    at_a = masks.group == 3 * (1 - odd)
    own = jnp.where(inner, middle, jnp.where(at_a, own_a, own_b))
    rim = jnp.where(inner, rim_y, jnp.where(at_a, rim_a, rim_b))
    return jnp.where(masks.rim[number], rim, own)


def forward_step(masks, tile, first, last, lower=None, upper=None, sourced=True):
    state, keep, from_x, from_y, spread, source = tile
    before = lower or [state[first - 1, h] for h in range(2)]
    here = [state[first, h] for h in range(2)]
    for e in range(first, last + 1):
        after = upper if upper and e == last else [state[e + 1, h] for h in range(2)]
        upright = masks.vertical(here)
        for h in range(2):
            y_high = jnp.where(masks.last, 0.0, lane_roll(here[h], LANES - 1))
            value = (
                keep[e, h] * here[h]
                + from_x[e, h] * before[h]
                + from_y[e, h] * lane_roll(here[h], 1)
                + spread[e, h] * (after[h] + y_high + upright[h])
            )
            state[e, h] = value + source[e, h] if sourced else value
        before, here = here, after


def forward_strips(masks, strips, sourced):
    for strip, keep, from_x, from_y, spread, source in strips:
        old = [strip[0, h] for h in range(2)]
        here = old
        before = [lane_roll(strip[INNER - 1, h], WIDE) for h in range(2)]
        for i in range(INNER):
            if i < INNER - 1:
                after = [strip[i + 1, h] for h in range(2)]
            else:
                after = [lane_roll(value, LANES - WIDE) for value in old]
            upright = masks.vertical(here)
            for h in range(2):
                value = (
                    keep[i, h] * here[h]
                    + from_x[i, h] * before[h]
                    + from_y[i, h] * lane_roll(here[h], 1)
                    + spread[i, h] * (after[h] + lane_roll(here[h], LANES - 1) + upright[h])
                )
                strip[i, h] = value + source[i, h] if sourced else value
            before, here = here, after


def scaled(refs, e, value=None):
    state, _, from_x, from_y, spread, _ = refs
    value = value or [state[e, h] for h in range(2)]
    return (
        value,
        [from_x[e, h] * value[h] for h in range(2)],
        [from_y[e, h] * value[h] for h in range(2)],
        [spread[e, h] * value[h] for h in range(2)],
    )


def adjoint_step(masks, tile, first, last, lower=None, upper=None):
    state, keep, from_x, from_y, spread, total = tile
    before, here = scaled(tile, first - 1, lower), scaled(tile, first)
    for e in range(first, last + 1):
        after = scaled(tile, e + 1, upper if e == last else None)
        value, _, by_y, by_spread = here
        upright = masks.vertical(by_spread)
        for h in range(2):
            y_low = jnp.where(masks.first, 0.0, lane_roll(by_spread[h], 1))
            fresh = (
                keep[e, h] * value[h]
                + (after[1][h] + before[3][h])
                + (y_low + lane_roll(by_y[h], LANES - 1))
                + upright[h]
            )
            state[e, h] = fresh
            if DEPTH <= e < DEPTH + OWN:
                total[e - DEPTH, h] += fresh
        before, here = here, after


def adjoint_strips(masks, strips):
    for refs in strips:
        strip, keep, from_x, from_y, spread, total = refs
        here = scaled(refs, 0)
        wrapped = [lane_roll(value, LANES - WIDE) for value in here[1]]
        last_row = scaled(refs, INNER - 1)
        before = (None, None, None, [lane_roll(value, WIDE) for value in last_row[3]])
        for i in range(INNER):
            after = scaled(refs, i + 1) if i < INNER - 1 else (None, wrapped, None, None)
            value, _, by_y, by_spread = here
            upright = masks.vertical(by_spread)
            for h in range(2):
                fresh = (
                    keep[i, h] * value[h]
                    + (after[1][h] + before[3][h])
                    + (lane_roll(by_spread[h], 1) + lane_roll(by_y[h], LANES - 1))
                    + upright[h]
                )
                strip[i, h] = fresh
                total[i, h] += fresh
            before, here = here, after


def ahead(step, state, saved):
    for t in range(JOIN):
        low, high = DEPTH + 1 + t, DEPTH + OWN - 2 - t
        for h in range(2):
            saved[t, h] = state[low, h]
            saved[t, 2 + h] = state[high, h]
        step(low, high)


def sweep(step, strip_step, join, saved):
    for t in range(ITERS):
        sourced = t < ITERS - 1
        if t == JOIN:
            join(t, EXT - 1 - t)
        if t < JOIN:
            step(t + 1, DEPTH + t, sourced, upper=[saved[t, h] for h in range(2)])
            step(DEPTH + OWN - 1 - t, EXT - 2 - t, sourced, lower=[saved[t, 2 + h] for h in range(2)])
        else:
            step(t + 1, EXT - 2 - t, sourced)
        strip_step(sourced)


def split_refs(refs, *counts):
    out = []
    for count in counts:
        out.append(refs[:count])
        refs = refs[count:]
    return out


def forward_kernel(kinds, tail_count, *refs):
    n = len(kinds)
    ins, got_strips, sources, tile, (edges, saved), outs, strips, out_strips = split_refs(
        refs, 4, 3 * n, 1 + n, 5, 2, 5 + 5, 5 * n, 3 * n
    )
    monitor, ranking, got_a, got_b = ins
    final, start_a, start_b, objective, start, *tile = outs
    odd = odd_tile()
    masks = Masks(kinds)
    state = tile[0]
    _, _, at_a, at_b = places(odd)
    present = jnp.where(lacks_b(), 0.0, 1.0)
    for x in range(DEPTH):
        for h in range(2):
            raw_a = [planes(got_a.at[field], x, h, DEPTH) for field in range(4)]
            raw_b = [planes(got_b.at[field], x, h, DEPTH) for field in range(4)]
            raw_b[:2] = [value * present for value in raw_b[:2]]
            store_tile(tile, at_a + x, h, raw_a)
            store_tile(tile, at_b + x, h, raw_b)
            i = x
            upper = i // (INNER // 2)
            for k in range(n):
                got = got_strips[3 * k : 3 * k + 3]
                side = pick(masks.right[k], DEPTH, 0)
                raw = []
                for field in range(4):
                    slot = DEPTH * (4 * upper + field)
                    rim_b = got[2][i % (INNER // 2), h]
                    rim_b = lane_roll(rim_b, 2 * at_b + side + LANES - slot)
                    raw.append(
                        merge_strip(
                            masks,
                            k,
                            odd,
                            edges[field, i, h],
                            lane_roll(raw_a[field], 2 * at_a + DEPTH),
                            lane_roll(raw_b[field], 2 * at_b + DEPTH),
                            lane_roll(
                                got[0][i, h], LANES + WIDE + side - 64 * (field // 2) - DEPTH * (field % 2)
                            ),
                            lane_roll(
                                got[1][i % (INNER // 2), h], 2 * at_a + side + LANES - slot
                            ),
                            rim_b * present if field < 2 else rim_b,
                        )
                    )
                mine = strips[5 * k : 5 * k + 5]
                for ref, value in zip(mine, (raw[0] + sources[1 + k][i, h], *coefficients(*raw[1:]))):
                    ref[i, h] = value
    for e in (*range(DEPTH), *range(DEPTH + OWN, EXT)):
        for h in range(2):
            state[e, h] += sources[0][e, h]
    strip_refs = [(*strips[5 * k : 5 * k + 5], sources[1 + k]) for k in range(n)]
    strip_states = [strip[0] for strip in strip_refs]

    def step(first, last, sourced, **beside):
        forward_step(masks, (*tile, sources[0]), first, last, sourced=sourced, **beside)

    sweep(
        step,
        functools.partial(forward_strips, masks, strip_refs),
        functools.partial(masks.join, state, strip_states),
        saved,
    )

    sample = sub_id() // 2
    upper = sub_id() % 2 == 1
    tail = jnp.zeros((SUBLANES, LANES), jnp.float32)
    for s in range(4):
        tail = jnp.where(sample == s, jnp.where(ranking[s] < tail_count, 1.0, 0.0), tail)
    sums = [jnp.zeros((SUBLANES, LANES), jnp.float32) for _ in range(4)]
    for x in range(OWN):
        for h in range(2):
            fresh = masks.outer_from(strip_states, DEPTH + x, h, state[DEPTH + x, h])
            final[pl.ds(h * OWN + x, SUBLANES, stride=2 * OWN), :] = fresh
            low = jnp.broadcast_to(monitor[pl.ds(h * OWN + x, 1), :], (SUBLANES, LANES))
            high = jnp.broadcast_to(monitor[pl.ds((2 + h) * OWN + x, 1), :], (SUBLANES, LANES))
            weighted = tail * jnp.where(upper, high, low) * fresh
            start[DEPTH + x, h] = weighted * (1.0 / (tail_count * ITERS))
            sums[x % 4] = sums[x % 4] + weighted * fresh
    objective[...] = (sums[0] + sums[1]) + (sums[2] + sums[3])

    base_a, base_b, _, _ = places(odd)
    for x in range(DEPTH):
        for h in range(2):
            start_a[x, h] = start[base_a + x, h]
            start_b[x, h] = start[base_b + x, h]
    slot = lane_id() // DEPTH
    for k, kind in enumerate(kinds):
        to_y, to_a, to_b = out_strips[3 * k : 3 * k + 3]
        offset = edge_offset(kind)

        def put(packed, row, h, target):
            moved = lane_roll(start[row, h], DEPTH * target + offset)
            return moved if packed is None else jnp.where(slot == target, moved, packed)

        for i in range(INNER // 2):
            packed = None
            for upper_half in range(2):
                for j in range(2):
                    for h in range(2):
                        row = DEPTH + INNER * j + INNER // 2 * upper_half + i
                        packed = put(packed, row, h, 4 * upper_half + 2 * j + h)
            to_y[i] = packed
        for out, base in ((to_a, base_a), (to_b, base_b)):
            for i in range(INNER // 4):
                packed = None
                for quarter in range(4):
                    for h in range(2):
                        packed = put(packed, base + INNER // 4 * quarter + i, h, 2 * quarter + h)
                out[i] = packed


def adjoint_ahead_kernel(*refs):
    coefs, (state, total, saved, edges) = refs[1:5], refs[5:]
    masks = Masks(())
    total[...] = jnp.zeros_like(total)
    first_j = masks.group == 1
    for i in range(INNER):
        for h in range(2):
            moved = [
                lane_roll(state[DEPTH + INNER * j + i, h], WIDE * (j + 1) + DEPTH) for j in range(2)
            ]
            edges[i, h] = jnp.where(first_j, *moved)
    ahead(functools.partial(adjoint_step, masks, (state, *coefs, total)), state, saved)


def adjoint_kernel(kinds, scale, *refs):
    n = len(kinds)
    parts, part_strips, (state, total, saved, edges), coefs, strip_coefs, rest, tile, strips, (rows,) = split_refs(
        refs, 2, 3 * n, 4, 4, 4 * n, 4, 2, 2 * n, 1
    )
    objective, wells, profile, out = rest
    state, total = tile
    odd = odd_tile()
    masks = Masks(kinds)
    at = places(odd)[2:]
    for part, first in zip(parts, at):
        for x in range(DEPTH):
            for h in range(2):
                state[first + x, h] = part[x, h]
    strip_refs = []
    for k in range(n):
        strip, strip_total = strips[2 * k : 2 * k + 2]
        got_y, got_a, got_b = part_strips[3 * k : 3 * k + 3]
        side = pick(masks.right[k], DEPTH, 0)
        for i in range(INNER):
            eighth, quarter = divmod(i, INNER // 2)[0], divmod(i, INNER // 4)[0]
            for h in range(2):
                moved = [
                    lane_roll(part[i, h], 2 * first + DEPTH) for part, first in zip(parts, at)
                ]
                slot = DEPTH * (2 * quarter + h)
                strip[i, h] = merge_strip(
                    masks,
                    k,
                    odd,
                    edges[i, h],
                    moved[0],
                    moved[1],
                    lane_roll(got_y[i % (INNER // 2)], LANES + WIDE + side - 64 * eighth - DEPTH * h),
                    lane_roll(got_a[i % (INNER // 4)], 2 * at[0] + side + LANES - slot),
                    lane_roll(got_b[i % (INNER // 4)], 2 * at[1] + side + LANES - slot),
                )
        strip_refs.append((strip, *strip_coefs[4 * k : 4 * k + 4], strip_total))
        strip_total[...] = jnp.zeros_like(strip_total)

    def step(first, last, _, **beside):
        adjoint_step(masks, (state, *coefs, total), first, last, **beside)

    sweep(
        step,
        lambda _: adjoint_strips(masks, strip_refs),
        functools.partial(masks.join, state, [refs[0] for refs in strip_refs]),
        saved,
    )
    totals = [refs[-1] for refs in strip_refs]
    for x in range(OWN):
        for h in range(2):
            value = masks.outer_from(totals, DEPTH + x, h, total[x, h])
            value = value + pltpu.roll(value, 4, 0)
            value = value + pltpu.roll(value, 2, 0)
            rows[pl.ds((2 * x + h) * 2, 2), :] = value[:2]
    count = rows.shape[0]
    r = lax.broadcasted_iota(jnp.int32, (count, 1), 0)
    layer = (r % 2) * 2 + (r // 2) % 2
    x = lax.axis_index("gx") * OWN + r // 4
    ids = (layer * (OWN * lax.axis_size("gx")) + x) * lax.axis_size("gy") + lax.axis_index("gy")
    field = rows[...]
    high = field.astype(jnp.bfloat16)
    low = (field - high.astype(jnp.float32)).astype(jnp.bfloat16)
    both = jnp.concatenate([high, low], axis=0)
    contract = (((1,), (1,)), ((), ()))
    controls = wells.shape[1]

    def chunk(c, carry):
        span = pl.ds(pl.multiple_of(c * CHUNK, CHUNK), CHUNK)
        share_high, share_low = profile[span, :LANES], profile[span, LANES:]
        first = lax.dot_general(both, share_high, contract, preferred_element_type=jnp.float32)
        second = lax.dot_general(high, share_low, contract, preferred_element_type=jnp.float32)
        product = first[:count] + first[count:] + second
        chosen = jnp.where(ids == wells[:, span], product, 0.0)
        out[:, span] = jnp.sum(chosen, axis=0, keepdims=True)
        return carry

    lax.fori_loop(0, controls // CHUNK, chunk, 0)
    whole = jnp.sum(jnp.sum(objective[...], axis=0, keepdims=True), axis=1, keepdims=True)
    out[:, controls:] = jnp.broadcast_to(whole * scale, (1, LANES))


def shape(*dims):
    return jax.ShapeDtypeStruct(dims, jnp.float32)


def same(x, count):
    return x


def partner_a(x, count):
    return x ^ 1


def partner_b(x, count):
    other = x + 1 if x % 2 else x - 1
    return other if 0 <= other < count else None


AXES = ("gx", "gy", "sa")


def swap_pairs(partner, kind, count_x, count_y, count_s):
    pairs = []
    for x in range(count_x):
        for y in range(count_y):
            for s in range(count_s):
                from_x, from_s = partner(x, count_x), s
                from_y = y if kind == "tile" else 1 - y if kind is None else (y + 1 if kind else y - 1)
                if from_x is None:
                    from_x, from_y, from_s = x, y, s ^ 1
                if 0 <= from_y < count_y:
                    pairs.append(
                        ((from_x * count_y + from_y) * count_s + from_s, (x * count_y + y) * count_s + s)
                    )
    return pairs


def exchange(tiles, strips, kinds):
    counts = [lax.axis_size(axis) for axis in AXES]
    got = [
        lax.ppermute(tile, AXES, swap_pairs(partner, "tile", *counts))
        for tile, partner in zip(tiles, (partner_a, partner_b))
    ]
    got_strips = []
    for k, kind in enumerate(kinds):
        for strip, partner in zip(strips[3 * k : 3 * k + 3], (same, partner_a, partner_b)):
            got_strips.append(lax.ppermute(strip, AXES, swap_pairs(partner, kind, *counts)))
    return got, got_strips


def add_kernel(value, *refs):
    got, (gradient, objective) = refs[:-2], refs[-2:]
    total = value[...] + got[0][...]
    if len(got) == 3:
        total = total + (got[1][...] + got[2][...])
    number = gradient.shape[1]
    gradient[...] = total[:, :number]
    objective[...] = total[:, number : number + 1]


def total_over(value, axes):
    count = 1
    for axis in axes:
        count *= lax.axis_size(axis)
    bit = 1
    while bit < count:
        bits = [bit] if 2 * bit >= count else [bit, 2 * bit, 3 * bit]
        got = [lax.ppermute(value, axes, [(i, i ^ b) for i in range(count)]) for b in bits]
        bit *= 4
        if bit >= count:
            break
        value = value + got[0]
        if len(got) == 3:
            value = value + (got[1] + got[2])
    return pl.pallas_call(
        add_kernel,
        out_shape=(shape(1, value.shape[1] - LANES), shape(1, 1)),
        in_specs=[vmem()] * (1 + len(got)),
        out_specs=(vmem(), vmem()),
        compiler_params=params(),
        name="total",
    )(value, *got)


def local(initial, retard, velx, vely, monitor, controls, profile, wells, ranking):
    samples, layers, width_x, width_y = initial.shape
    count_x, count_y = lax.axis_size("gx"), lax.axis_size("gy")
    assert (samples, layers, width_x, width_y) == (4, 4, OWN, LANES)
    assert count_x % 2 == 0 and lax.axis_size("sa") == 2
    number = controls.shape[0]
    assert number % CHUNK == 0
    kinds = strip_kinds(count_y)
    n = len(kinds)
    half_tile = shape(4, samples, layers, DEPTH, LANES)
    hbm = pl.BlockSpec(memory_space=pltpu.HBM)
    any_space = pl.BlockSpec(memory_space=pl.ANY)
    fields = (initial, retard, velx, vely)

    def in_hbm(values):
        return [pltpu.with_memory_space_constraint(value, pltpu.HBM) for value in values]

    sent = pl.pallas_call(
        rims_kernel,
        out_shape=(half_tile, half_tile),
        in_specs=[hbm] * 4,
        out_specs=(any_space, any_space),
        scratch_shapes=[pltpu.SemaphoreType.DMA((8,))],
        compiler_params=params(),
        name="rims",
    )(*in_hbm(fields))
    own, monitor, controls, wells, *sent_strips = pl.pallas_call(
        functools.partial(strip_pack_kernel, kinds),
        out_shape=(
            shape(4, samples * layers * OWN, LANES),
            shape(layers * OWN, LANES),
            shape(1, number),
            jax.ShapeDtypeStruct((1, number), jnp.int32),
        )
        + (
            shape(INNER, 2, SUBLANES, LANES),
            shape(INNER // 2, 2, SUBLANES, LANES),
            shape(INNER // 2, 2, SUBLANES, LANES),
        )
        * n,
        in_specs=[hbm] * 7,
        out_specs=(vmem(),) * (4 + 3 * n),
        scratch_shapes=[pltpu.SemaphoreType.DMA((7,))],
        compiler_params=params(),
        name="strips",
    )(
        *in_hbm(value.reshape(-1, LANES) for value in (*fields, monitor)),
        *in_hbm(value.reshape(1, -1) for value in (controls, wells)),
    )
    got, got_strips = exchange(sent, sent_strips, kinds)
    tile_shape = shape(EXT, 2, SUBLANES, LANES)
    strip_shape = shape(INNER, 2, SUBLANES, LANES)
    saved_shape = shape(JOIN, 4, SUBLANES, LANES)
    blocks = (1 + n) * EXT * layers
    *prepared, split = pl.pallas_call(
        functools.partial(source_kernel, kinds),
        out_shape=(tile_shape,)
        + (strip_shape,) * n
        + (tile_shape,) * 5
        + (
            shape(4, INNER, 2, SUBLANES, LANES),
            saved_shape,
            jax.ShapeDtypeStruct((number, 2 * LANES), jnp.bfloat16),
        ),
        in_specs=[vmem()] * 4,
        out_specs=(vmem(),) * (1 + n + 5 + 3),
        scratch_shapes=[
            pltpu.VMEM((blocks, 2 * LANES), jnp.float32),
            pltpu.VMEM((blocks, LANES), jnp.float32),
        ],
        compiler_params=params(),
        name="source",
    )(wells, controls, profile, own)
    got = [part.reshape(4, -1, LANES) for part in got]
    tail_count = samples * lax.axis_size("sa") // 2
    half_start = shape(DEPTH, 2, SUBLANES, LANES)
    smem = pl.BlockSpec(memory_space=pltpu.SMEM)
    first_tile = 4 + 3 * n + 1 + n
    final, start_a, start_b, objective, start, *rest = pl.pallas_call(
        functools.partial(forward_kernel, kinds, tail_count),
        out_shape=(
            shape(samples * layers * OWN, LANES),
            half_start,
            half_start,
            shape(SUBLANES, LANES),
            tile_shape,
        )
        + (tile_shape,) * 5
        + (strip_shape,) * (5 * n)
        + (
            shape(INNER // 2, SUBLANES, LANES),
            shape(INNER // 4, SUBLANES, LANES),
            shape(INNER // 4, SUBLANES, LANES),
        )
        * n,
        in_specs=[vmem(), smem] + [vmem()] * (2 + 3 * n + 1 + n + 5 + 2),
        out_specs=(vmem(),) * (5 + 5 + 5 * n + 3 * n),
        input_output_aliases={first_tile + k: 5 + k for k in range(5)},
        compiler_params=params(),
        name="forward",
    )(monitor, ranking, *got, *got_strips, *prepared)
    tile, strips, start_strips = split_refs(rest, 5, 5 * n, 3 * n)
    got_start, got_start_strips = exchange((start_a, start_b), start_strips, kinds)
    strip_coefs = [strips[5 * k + c] for k in range(n) for c in range(1, 5)]
    begun = pl.pallas_call(
        adjoint_ahead_kernel,
        out_shape=(tile_shape, shape(OWN, 2, SUBLANES, LANES), saved_shape, strip_shape),
        in_specs=[vmem()] * 5,
        out_specs=(vmem(),) * 4,
        input_output_aliases={0: 0},
        compiler_params=params(),
        name="ahead",
    )(start, *tile[1:])
    cells = layers * OWN * count_x * LANES * count_y
    summed, _, _ = pl.pallas_call(
        functools.partial(adjoint_kernel, kinds, 0.5 / (tail_count * cells)),
        out_shape=(shape(1, number + LANES), tile_shape, shape(OWN, 2, SUBLANES, LANES)),
        in_specs=[vmem()] * (2 + 3 * n + 4 + 4 + 4 * n + 3),
        out_specs=(vmem(),) * 3,
        input_output_aliases={2 + 3 * n: 1, 3 + 3 * n: 2},
        scratch_shapes=[pltpu.VMEM((INNER, 2, SUBLANES, LANES), jnp.float32)] * (2 * n)
        + [pltpu.VMEM((OWN * layers, LANES), jnp.float32)],
        compiler_params=params(),
        name="adjoint",
    )(
        *got_start,
        *got_start_strips,
        *begun,
        *tile[1:],
        *strip_coefs,
        objective,
        wells,
        split,
    )
    gradient, objective = total_over(summed, AXES)
    return final.reshape(initial.shape), gradient.reshape(-1), objective.reshape(-1)


def solution(mesh):
    in_specs = (
        P(("groups", "sa"), None, "gx", "gy"),
        P(("groups", "sa"), None, "gx", "gy"),
        P(("groups", "sa"), None, "gx", "gy"),
        P(("groups", "sa"), None, "gx", "gy"),
        P("groups", "gx", "gy"),
        P("groups"),
        P("groups", None),
        P("groups"),
        P(("groups", "sa")),
    )
    out_specs = (P(("groups", "sa"), None, "gx", "gy"), P("groups"), P("groups"))
    return jax.shard_map(local, mesh=mesh, in_specs=in_specs, out_specs=out_specs, check_vma=False)
```

```python
import functools

import jax
import jax.numpy as jnp
from jax import lax
from jax.experimental import pallas as pl
from jax.experimental.pallas import tpu as pltpu
from jax.sharding import PartitionSpec as P

ITERS = 16
KAPPA = 0.1
VERT = 0.05
LANES = 128
SUBLANES = 8
DEPTH = ITERS
OWN = 2 * DEPTH
EXT = OWN + 2 * DEPTH
WIDE = 2 * DEPTH
GROUPS = LANES // WIDE
INNER = EXT // GROUPS
JOIN = ITERS // 2
CHUNK = 2048
VMEM_LIMIT = 24 * 1024 * 1024


def vmem():
    return pl.BlockSpec(memory_space=pltpu.VMEM)


def params():
    return pltpu.CompilerParams(vmem_limit_bytes=VMEM_LIMIT)


def sub_id():
    return lax.broadcasted_iota(jnp.int32, (SUBLANES, LANES), 0)


def lane_id():
    return lax.broadcasted_iota(jnp.int32, (SUBLANES, LANES), 1)


def wrap(shift):
    return shift % LANES if isinstance(shift, int) else lax.rem(shift, LANES)


def lane_roll(value, shift):
    if isinstance(shift, int) and shift % LANES == 0:
        return value
    return pltpu.roll(value, wrap(shift), 1)


def pick(flag, yes, no):
    if isinstance(flag, bool):
        return yes if flag else no
    return jnp.where(flag, yes, no)


def odd_tile():
    return lax.rem(lax.axis_index("gx"), 2)


def lacks_b():
    x = lax.axis_index("gx")
    return (x == 0) | (x == lax.axis_size("gx") - 1)


def strip_kinds(count):
    return (None,) if count == 2 else (True, False)


def is_right(kind):
    return lax.axis_index("gy") == 0 if kind is None else kind


def planes(ref, row, half, rows):
    return ref[pl.ds(half * rows + row, SUBLANES, stride=2 * rows), :]


def copy_all(pairs, sems):
    copies = [pltpu.make_async_copy(*pair, sems.at[k]) for k, pair in enumerate(pairs)]
    for copy in copies:
        copy.start()
    for copy in copies:
        copy.wait()


def rims_kernel(initial, retard, velx, vely, out_a, out_b, sems):
    odd = odd_tile()
    pairs = []
    for field, ref in enumerate((initial, retard, velx, vely)):
        for out, base in ((out_a, DEPTH * (1 - odd)), (out_b, DEPTH * odd)):
            source = ref.at[:, :, pl.ds(pl.multiple_of(base, DEPTH), DEPTH), :]
            pairs.append((source, out.at[field]))
    copy_all(pairs, sems)


def edge_offset(kind):
    return DEPTH * (1 - lax.axis_index("gy")) if kind is None else (0 if kind else DEPTH)


def strip_pack_kernel(kinds, *refs):
    ins, (own, *copied), outs, (sems,) = split_refs(refs, 7, 4, 3 * len(kinds), 1)
    pairs = [(ref, own.at[field]) for field, ref in enumerate(ins[:4])]
    copy_all(pairs + list(zip(ins[4:], copied)), sems)
    odd = odd_tile()
    slot = lane_id() // DEPTH
    for number, kind in enumerate(kinds):
        to_y, to_a, to_b = outs[3 * number : 3 * number + 3]
        offset = edge_offset(kind)

        def put(packed, field, row, half, target):
            moved = lane_roll(planes(own.at[field], row, half, OWN), DEPTH * target + offset)
            return moved if packed is None else jnp.where(slot == target, moved, packed)

        for half in range(2):
            for i in range(INNER):
                packed = None
                for field in range(4):
                    for j in range(2):
                        target = 4 * (field // 2) + 2 * j + field % 2
                        packed = put(packed, field, INNER * j + i, half, target)
                to_y[i, half] = packed
            for out, base in ((to_a, DEPTH * (1 - odd)), (to_b, DEPTH * odd)):
                for i in range(INNER // 2):
                    packed = None
                    for field in range(4):
                        for upper in range(2):
                            row = base + INNER // 2 * upper + i
                            target = 4 * upper + field
                            target = slot_b(odd, target) if out is to_b else target
                            packed = put(packed, field, row, half, target)
                    out[i, half] = packed


def coefficients(retard, velx, vely):
    spread = KAPPA * retard
    from_x = retard * velx + spread
    from_y = retard * vely + spread
    keep = 1.0 - (from_x + from_y + (2.0 + 2.0 * VERT / KAPPA) * spread)
    return keep, from_x, from_y, spread


def store_tile(refs, row, half, raw, source=None):
    state, retard, velx, vely = raw
    keep, from_x, from_y, spread = coefficients(retard, velx, vely)
    from_y = jnp.where(lane_id() == 0, 0.0, from_y)
    for ref, value in zip(refs, (state, keep, from_x, from_y, spread)):
        ref[row, half] = value


def source_kernel(kinds, wells, controls, profile, own, *refs):
    n = len(kinds)
    sources, tile, edges, (saved, split), (acc, acc_low) = split_refs(refs, 1 + n, 5, 1, 2, 2)
    for x in range(OWN):
        for half in range(2):
            raw = [planes(own.at[field], x, half, OWN) for field in range(4)]
            store_tile(tile, DEPTH + x, half, raw)
    first_j = lane_id() // WIDE == 1
    for field in range(4):
        for i in range(INNER):
            for half in range(2):
                moved = [
                    lane_roll(planes(own.at[field], INNER * j + i, half, OWN), WIDE * (j + 1) + DEPTH)
                    for j in range(2)
                ]
                edges[0][field, i, half] = jnp.where(first_j, *moved)

    x_index, y_index = lax.axis_index("gx"), lax.axis_index("gy")
    all_x, all_blocks = OWN * lax.axis_size("gx"), lax.axis_size("gy")
    layers = 4
    per_block = EXT * layers
    r = lax.broadcasted_iota(jnp.int32, (per_block, 1), 0)
    x = x_index * OWN - DEPTH + r // layers
    ids = []
    for block in [y_index] + [
        1 - y_index if kind is None else (y_index + 1 if kind else y_index - 1) for kind in kinds
    ]:
        inside = (x >= 0) & (x < all_x) & (block >= 0) & (block < all_blocks)
        ids.append(jnp.where(inside, ((r % layers) * all_x + x) * all_blocks + block, -1))
    ids = jnp.concatenate(ids, axis=0)
    acc[...] = jnp.zeros_like(acc)
    acc_low[...] = jnp.zeros_like(acc_low)

    def chunk(c, carry):
        span = pl.ds(pl.multiple_of(c * CHUNK, CHUNK), CHUNK)
        part = profile[span, :]
        high = part.astype(jnp.bfloat16)
        low = (part - high.astype(jnp.float32)).astype(jnp.bfloat16)
        rate = controls[:, span]
        rate_high = rate.astype(jnp.bfloat16).astype(jnp.float32)
        hit = ids == wells[:, span]
        hot_high = jnp.where(hit, rate_high, 0.0).astype(jnp.bfloat16)
        hot_low = jnp.where(hit, rate - rate_high, 0.0).astype(jnp.bfloat16)
        split_part = jnp.concatenate([high, low], axis=1)
        split[span, :] = split_part
        acc[...] += jnp.dot(hot_high, split_part, preferred_element_type=jnp.float32)
        acc_low[...] += jnp.dot(hot_low, high, preferred_element_type=jnp.float32)
        return carry

    lax.fori_loop(0, wells.shape[1] // CHUNK, chunk, 0)
    acc_low[...] += acc[:, :LANES] + acc[:, LANES:]
    upper = sub_id() % 2 == 1
    group = lane_id() // WIDE

    def both(first, half):
        low_layer = jnp.broadcast_to(acc_low[pl.ds(first + half, 1), :], (SUBLANES, LANES))
        high_layer = jnp.broadcast_to(acc_low[pl.ds(first + 2 + half, 1), :], (SUBLANES, LANES))
        return jnp.where(upper, high_layer, low_layer)

    masks = Masks(kinds)
    for number in range(n):
        for i in range(INNER):
            for half in range(2):
                packed = None
                for j in range(GROUPS):
                    e = j * INNER + i
                    here = both(e * layers, half)
                    if number == 0:
                        sources[0][e, half] = here
                    beside = both((number + 1) * per_block + e * layers, half)
                    mixed = jnp.where(masks.own_edge[number], here, beside)
                    moved = lane_roll(mixed, WIDE * j + DEPTH)
                    packed = moved if packed is None else jnp.where(group == j, moved, packed)
                sources[1 + number][i, half] = packed
    for x in range(OWN):
        for half in range(2):
            tile[0][DEPTH + x, half] += sources[0][DEPTH + x, half]
    ahead(functools.partial(forward_step, masks, (*tile, sources[0]), sourced=True), tile[0], saved)


class Masks:
    def __init__(self, kinds):
        lane = lane_id()
        self.first, self.last = lane == 0, lane == LANES - 1
        self.group = lane // WIDE
        upper = sub_id() % 2 == 1
        self.below = jnp.where(upper, VERT / KAPPA, 0.0)
        self.above = jnp.where(upper, 0.0, VERT / KAPPA)
        self.right = [is_right(kind) for kind in kinds]
        half, eighth, sixteenth = lane % WIDE // DEPTH, lane // DEPTH, lane // JOIN
        self.rim = [half == pick(right, 1, 0) for right in self.right]
        self.not_rim = [half == pick(right, 0, 1) for right in self.right]
        self.own_edge = [eighth != pick(right, 0, LANES // DEPTH - 1) for right in self.right]
        self.outer = [sixteenth == pick(right, LANES // JOIN - 1, 0) for right in self.right]

    def vertical(self, pair):
        low = (VERT / KAPPA) * pair[1] + self.below * pltpu.roll(pair[1], 1, 0)
        high = (VERT / KAPPA) * pair[0] + self.above * pltpu.roll(pair[0], SUBLANES - 1, 0)
        return low, high

    def outer_from(self, strips, e, half, value):
        j, i = divmod(e, INNER)
        for strip, outer in zip(strips, self.outer):
            value = jnp.where(outer, lane_roll(strip[i, half], LANES - DEPTH - WIDE * j), value)
        return value

    def join(self, tile, strips, first, last):
        for e in range(first, last + 1):
            j, i = divmod(e, INNER)
            for h in range(2):
                value = self.outer_from(strips, e, h, tile[e, h])
                tile[e, h] = value
                moved = lane_roll(value, WIDE * j + DEPTH)
                for strip, own in zip(strips, self.not_rim):
                    strip[i, h] = jnp.where((self.group == j) & own, moved, strip[i, h])


def slot_b(odd, slot):
    return lax.rem(slot + 6 - 4 * odd, LANES // DEPTH)


def places(odd):
    return DEPTH * (2 - odd), DEPTH * (1 + odd), 3 * DEPTH * (1 - odd), 3 * DEPTH * odd


def merge_strip(masks, number, odd, slot, middle, own_a, own_b, rim_y, rim_a, rim_b):
    first_a = places(odd)[2]
    inner = (masks.group == 1) | (masks.group == 2)
    own = jnp.where(masks.group == 3 * (1 - odd), own_a, own_b)
    own = jnp.where(inner, middle, own)
    rim = jnp.where(lane_id() // DEPTH == slot, rim_a, rim_b)
    rim = lane_roll(rim, 2 * first_a + pick(masks.right[number], DEPTH, 0) + LANES - DEPTH * slot)
    return jnp.where(masks.rim[number], jnp.where(inner, rim_y, rim), own)


def forward_step(masks, tile, first, last, lower=None, upper=None, sourced=True):
    state, keep, from_x, from_y, spread, source = tile
    before = lower or [state[first - 1, h] for h in range(2)]
    here = [state[first, h] for h in range(2)]
    for e in range(first, last + 1):
        after = upper if upper and e == last else [state[e + 1, h] for h in range(2)]
        upright = masks.vertical(here)
        for h in range(2):
            y_high = jnp.where(masks.last, 0.0, lane_roll(here[h], LANES - 1))
            value = (
                keep[e, h] * here[h]
                + from_x[e, h] * before[h]
                + from_y[e, h] * lane_roll(here[h], 1)
                + spread[e, h] * (after[h] + y_high + upright[h])
            )
            state[e, h] = value + source[e, h] if sourced else value
        before, here = here, after


def forward_strips(masks, strips, sourced):
    for strip, keep, from_x, from_y, spread, source in strips:
        old = [strip[0, h] for h in range(2)]
        here = old
        before = [lane_roll(strip[INNER - 1, h], WIDE) for h in range(2)]
        for i in range(INNER):
            if i < INNER - 1:
                after = [strip[i + 1, h] for h in range(2)]
            else:
                after = [lane_roll(value, LANES - WIDE) for value in old]
            upright = masks.vertical(here)
            for h in range(2):
                value = (
                    keep[i, h] * here[h]
                    + from_x[i, h] * before[h]
                    + from_y[i, h] * lane_roll(here[h], 1)
                    + spread[i, h] * (after[h] + lane_roll(here[h], LANES - 1) + upright[h])
                )
                strip[i, h] = value + source[i, h] if sourced else value
            before, here = here, after


def scaled(refs, e, value=None):
    state, _, from_x, from_y, spread, _ = refs
    value = value or [state[e, h] for h in range(2)]
    return (
        value,
        [from_x[e, h] * value[h] for h in range(2)],
        [from_y[e, h] * value[h] for h in range(2)],
        [spread[e, h] * value[h] for h in range(2)],
    )


def adjoint_step(masks, tile, first, last, lower=None, upper=None):
    state, keep, from_x, from_y, spread, total = tile
    before, here = scaled(tile, first - 1, lower), scaled(tile, first)
    for e in range(first, last + 1):
        after = scaled(tile, e + 1, upper if e == last else None)
        value, _, by_y, by_spread = here
        upright = masks.vertical(by_spread)
        for h in range(2):
            y_low = jnp.where(masks.first, 0.0, lane_roll(by_spread[h], 1))
            fresh = (
                keep[e, h] * value[h]
                + (after[1][h] + before[3][h])
                + (y_low + lane_roll(by_y[h], LANES - 1))
                + upright[h]
            )
            state[e, h] = fresh
            if DEPTH <= e < DEPTH + OWN:
                total[e - DEPTH, h] += fresh
        before, here = here, after


def adjoint_strips(masks, strips):
    for refs in strips:
        strip, keep, from_x, from_y, spread, total = refs
        here = scaled(refs, 0)
        wrapped = [lane_roll(value, LANES - WIDE) for value in here[1]]
        last_row = scaled(refs, INNER - 1)
        before = (None, None, None, [lane_roll(value, WIDE) for value in last_row[3]])
        for i in range(INNER):
            after = scaled(refs, i + 1) if i < INNER - 1 else (None, wrapped, None, None)
            value, _, by_y, by_spread = here
            upright = masks.vertical(by_spread)
            for h in range(2):
                fresh = (
                    keep[i, h] * value[h]
                    + (after[1][h] + before[3][h])
                    + (lane_roll(by_spread[h], 1) + lane_roll(by_y[h], LANES - 1))
                    + upright[h]
                )
                strip[i, h] = fresh
                total[i, h] += fresh
            before, here = here, after


def ahead(step, state, saved):
    for t in range(JOIN):
        low, high = DEPTH + 1 + t, DEPTH + OWN - 2 - t
        for h in range(2):
            saved[t, h] = state[low, h]
            saved[t, 2 + h] = state[high, h]
        step(low, high)


def sweep(step, strip_step, join, saved):
    for t in range(ITERS):
        sourced = t < ITERS - 1
        if t == JOIN:
            join(t, EXT - 1 - t)
        if t < JOIN:
            step(t + 1, DEPTH + t, sourced, upper=[saved[t, h] for h in range(2)])
            step(DEPTH + OWN - 1 - t, EXT - 2 - t, sourced, lower=[saved[t, 2 + h] for h in range(2)])
        else:
            step(t + 1, EXT - 2 - t, sourced)
        strip_step(sourced)


def split_refs(refs, *counts):
    out = []
    for count in counts:
        out.append(refs[:count])
        refs = refs[count:]
    return out


def forward_kernel(kinds, tail_count, *refs):
    n = len(kinds)
    ins, got_strips, sources, tile, (edges, saved), outs, strips, out_strips = split_refs(
        refs, 4, 3 * n, 1 + n, 5, 2, 5 + 5, 5 * n, 3 * n
    )
    monitor, ranking, got_a, got_b = ins
    final, start_a, start_b, objective, start, *tile = outs
    odd = odd_tile()
    masks = Masks(kinds)
    state = tile[0]
    _, _, at_a, at_b = places(odd)
    present = jnp.where(lacks_b(), 0.0, 1.0)
    present_lanes = jnp.where(masks.group == 3 * odd, present, 1.0)
    for x in range(DEPTH):
        for h in range(2):
            raw_a = [planes(got_a.at[field], x, h, DEPTH) for field in range(4)]
            raw_b = [planes(got_b.at[field], x, h, DEPTH) for field in range(4)]
            raw_b[:2] = [value * present for value in raw_b[:2]]
            store_tile(tile, at_a + x, h, raw_a)
            store_tile(tile, at_b + x, h, raw_b)
            i = x
            upper = i // (INNER // 2)
            for k in range(n):
                got = got_strips[3 * k : 3 * k + 3]
                side = pick(masks.right[k], DEPTH, 0)
                raw = [
                    merge_strip(
                        masks,
                        k,
                        odd,
                        4 * upper + field,
                        edges[field, i, h],
                        lane_roll(raw_a[field], 2 * at_a + DEPTH),
                        lane_roll(raw_b[field], 2 * at_b + DEPTH),
                        lane_roll(
                            got[0][i, h], LANES + WIDE + side - 64 * (field // 2) - DEPTH * (field % 2)
                        ),
                        got[1][i % (INNER // 2), h],
                        got[2][i % (INNER // 2), h],
                    )
                    for field in range(4)
                ]
                raw[:2] = [value * present_lanes for value in raw[:2]]
                mine = strips[5 * k : 5 * k + 5]
                for ref, value in zip(mine, (raw[0] + sources[1 + k][i, h], *coefficients(*raw[1:]))):
                    ref[i, h] = value
    for e in (*range(DEPTH), *range(DEPTH + OWN, EXT)):
        for h in range(2):
            state[e, h] += sources[0][e, h]
    strip_refs = [(*strips[5 * k : 5 * k + 5], sources[1 + k]) for k in range(n)]
    strip_states = [strip[0] for strip in strip_refs]

    def step(first, last, sourced, **beside):
        forward_step(masks, (*tile, sources[0]), first, last, sourced=sourced, **beside)

    sweep(
        step,
        functools.partial(forward_strips, masks, strip_refs),
        functools.partial(masks.join, state, strip_states),
        saved,
    )

    sample = sub_id() // 2
    upper = sub_id() % 2 == 1
    tail = jnp.zeros((SUBLANES, LANES), jnp.float32)
    for s in range(4):
        tail = jnp.where(sample == s, jnp.where(ranking[s] < tail_count, 1.0, 0.0), tail)
    sums = [jnp.zeros((SUBLANES, LANES), jnp.float32) for _ in range(4)]
    for x in range(OWN):
        for h in range(2):
            fresh = masks.outer_from(strip_states, DEPTH + x, h, state[DEPTH + x, h])
            final[pl.ds(h * OWN + x, SUBLANES, stride=2 * OWN), :] = fresh
            low = jnp.broadcast_to(monitor[pl.ds(h * OWN + x, 1), :], (SUBLANES, LANES))
            high = jnp.broadcast_to(monitor[pl.ds((2 + h) * OWN + x, 1), :], (SUBLANES, LANES))
            weighted = tail * jnp.where(upper, high, low) * fresh
            start[DEPTH + x, h] = weighted * (1.0 / (tail_count * ITERS))
            sums[x % 4] = sums[x % 4] + weighted * fresh
    objective[...] = (sums[0] + sums[1]) + (sums[2] + sums[3])

    base_a, base_b, _, _ = places(odd)
    for x in range(DEPTH):
        for h in range(2):
            start_a[x, h] = start[base_a + x, h]
            start_b[x, h] = start[base_b + x, h]
    slot = lane_id() // DEPTH
    for k, kind in enumerate(kinds):
        to_y, to_a, to_b = out_strips[3 * k : 3 * k + 3]
        offset = edge_offset(kind)

        def put(packed, row, h, target):
            moved = lane_roll(start[row, h], DEPTH * target + offset)
            return moved if packed is None else jnp.where(slot == target, moved, packed)

        for i in range(INNER // 2):
            packed = None
            for upper_half in range(2):
                for j in range(2):
                    for h in range(2):
                        row = DEPTH + INNER * j + INNER // 2 * upper_half + i
                        packed = put(packed, row, h, 4 * upper_half + 2 * j + h)
            to_y[i] = packed
        for out, base in ((to_a, base_a), (to_b, base_b)):
            for i in range(INNER // 4):
                packed = None
                for quarter in range(4):
                    for h in range(2):
                        target = 2 * quarter + h
                        target = slot_b(odd, target) if out is to_b else target
                        packed = put(packed, base + INNER // 4 * quarter + i, h, target)
                out[i] = packed


def adjoint_ahead_kernel(*refs):
    coefs, (state, total, saved, edges) = refs[1:5], refs[5:]
    masks = Masks(())
    total[...] = jnp.zeros_like(total)
    first_j = masks.group == 1
    for i in range(INNER):
        for h in range(2):
            moved = [
                lane_roll(state[DEPTH + INNER * j + i, h], WIDE * (j + 1) + DEPTH) for j in range(2)
            ]
            edges[i, h] = jnp.where(first_j, *moved)
    ahead(functools.partial(adjoint_step, masks, (state, *coefs, total)), state, saved)


def adjoint_kernel(kinds, scale, *refs):
    n = len(kinds)
    parts, part_strips, (state, total, saved, edges), coefs, strip_coefs, rest, tile, strips, (rows,) = split_refs(
        refs, 2, 3 * n, 4, 4, 4 * n, 4, 2, 2 * n, 1
    )
    objective, wells, profile, out = rest
    state, total = tile
    odd = odd_tile()
    masks = Masks(kinds)
    at = places(odd)[2:]
    for part, first in zip(parts, at):
        for x in range(DEPTH):
            for h in range(2):
                state[first + x, h] = part[x, h]
    strip_refs = []
    for k in range(n):
        strip, strip_total = strips[2 * k : 2 * k + 2]
        got_y, got_a, got_b = part_strips[3 * k : 3 * k + 3]
        side = pick(masks.right[k], DEPTH, 0)
        for i in range(INNER):
            eighth, quarter = divmod(i, INNER // 2)[0], divmod(i, INNER // 4)[0]
            for h in range(2):
                moved = [
                    lane_roll(part[i, h], 2 * first + DEPTH) for part, first in zip(parts, at)
                ]
                beside = merge_strip(
                    masks,
                    k,
                    odd,
                    2 * quarter + h,
                    edges[i, h],
                    moved[0],
                    moved[1],
                    lane_roll(got_y[i % (INNER // 2)], LANES + WIDE + side - 64 * eighth - DEPTH * h),
                    got_a[i % (INNER // 4)],
                    got_b[i % (INNER // 4)],
                )
                strip[i, h] = beside
        strip_refs.append((strip, *strip_coefs[4 * k : 4 * k + 4], strip_total))
        strip_total[...] = jnp.zeros_like(strip_total)

    def step(first, last, _, **beside):
        adjoint_step(masks, (state, *coefs, total), first, last, **beside)

    sweep(
        step,
        lambda _: adjoint_strips(masks, strip_refs),
        functools.partial(masks.join, state, [refs[0] for refs in strip_refs]),
        saved,
    )
    totals = [refs[-1] for refs in strip_refs]
    for x in range(OWN):
        for h in range(2):
            value = masks.outer_from(totals, DEPTH + x, h, total[x, h])
            value = value + pltpu.roll(value, 4, 0)
            value = value + pltpu.roll(value, 2, 0)
            rows[pl.ds((2 * x + h) * 2, 2), :] = value[:2]
    count = rows.shape[0]
    r = lax.broadcasted_iota(jnp.int32, (count, 1), 0)
    layer = (r % 2) * 2 + (r // 2) % 2
    x = lax.axis_index("gx") * OWN + r // 4
    ids = (layer * (OWN * lax.axis_size("gx")) + x) * lax.axis_size("gy") + lax.axis_index("gy")
    field = rows[...]
    high = field.astype(jnp.bfloat16)
    low = (field - high.astype(jnp.float32)).astype(jnp.bfloat16)
    both = jnp.concatenate([high, low], axis=0)
    contract = (((1,), (1,)), ((), ()))
    controls = wells.shape[1]

    def chunk(c, carry):
        span = pl.ds(pl.multiple_of(c * CHUNK, CHUNK), CHUNK)
        share_high, share_low = profile[span, :LANES], profile[span, LANES:]
        first = lax.dot_general(both, share_high, contract, preferred_element_type=jnp.float32)
        second = lax.dot_general(high, share_low, contract, preferred_element_type=jnp.float32)
        product = first[:count] + first[count:] + second
        chosen = jnp.where(ids == wells[:, span], product, 0.0)
        out[:, span] = jnp.sum(chosen, axis=0, keepdims=True)
        return carry

    lax.fori_loop(0, controls // CHUNK, chunk, 0)
    whole = jnp.sum(jnp.sum(objective[...], axis=0, keepdims=True), axis=1, keepdims=True)
    out[:, controls:] = jnp.broadcast_to(whole * scale, (1, LANES))


def shape(*dims):
    return jax.ShapeDtypeStruct(dims, jnp.float32)


def same(x, count):
    return x


def partner_a(x, count):
    return x ^ 1


def partner_b(x, count):
    other = x + 1 if x % 2 else x - 1
    return other if 0 <= other < count else None


AXES = ("gx", "gy", "sa")


def swap_pairs(partner, kind, count_x, count_y, count_s):
    pairs = []
    for x in range(count_x):
        for y in range(count_y):
            for s in range(count_s):
                from_x, from_s = partner(x, count_x), s
                from_y = y if kind == "tile" else 1 - y if kind is None else (y + 1 if kind else y - 1)
                if from_x is None:
                    from_x, from_y, from_s = x, y, s ^ 1
                if 0 <= from_y < count_y:
                    pairs.append(
                        ((from_x * count_y + from_y) * count_s + from_s, (x * count_y + y) * count_s + s)
                    )
    return pairs


def exchange(tiles, strips, kinds):
    counts = [lax.axis_size(axis) for axis in AXES]
    got = [
        lax.ppermute(tile, AXES, swap_pairs(partner, "tile", *counts))
        for tile, partner in zip(tiles, (partner_a, partner_b))
    ]
    got_strips = []
    for k, kind in enumerate(kinds):
        for strip, partner in zip(strips[3 * k : 3 * k + 3], (same, partner_a, partner_b)):
            got_strips.append(lax.ppermute(strip, AXES, swap_pairs(partner, kind, *counts)))
    return got, got_strips


def add_kernel(value, *refs):
    got, (gradient, objective) = refs[:-2], refs[-2:]
    total = value[...] + got[0][...]
    if len(got) == 3:
        total = total + (got[1][...] + got[2][...])
    number = gradient.shape[1]
    gradient[...] = total[:, :number]
    objective[...] = total[:, number : number + 1]


def total_over(value, axes):
    count = 1
    for axis in axes:
        count *= lax.axis_size(axis)
    bit = 1
    while bit < count:
        bits = [bit] if 2 * bit >= count else [bit, 2 * bit, 3 * bit]
        got = [lax.ppermute(value, axes, [(i, i ^ b) for i in range(count)]) for b in bits]
        bit *= 4
        if bit >= count:
            break
        value = value + got[0]
        if len(got) == 3:
            value = value + (got[1] + got[2])
    return pl.pallas_call(
        add_kernel,
        out_shape=(shape(1, value.shape[1] - LANES), shape(1, 1)),
        in_specs=[vmem()] * (1 + len(got)),
        out_specs=(vmem(), vmem()),
        compiler_params=params(),
        name="total",
    )(value, *got)


def local(initial, retard, velx, vely, monitor, controls, profile, wells, ranking):
    samples, layers, width_x, width_y = initial.shape
    count_x, count_y = lax.axis_size("gx"), lax.axis_size("gy")
    assert (samples, layers, width_x, width_y) == (4, 4, OWN, LANES)
    assert count_x % 2 == 0 and lax.axis_size("sa") == 2
    number = controls.shape[0]
    assert number % CHUNK == 0
    kinds = strip_kinds(count_y)
    n = len(kinds)
    half_tile = shape(4, samples, layers, DEPTH, LANES)
    hbm = pl.BlockSpec(memory_space=pltpu.HBM)
    any_space = pl.BlockSpec(memory_space=pl.ANY)
    fields = (initial, retard, velx, vely)

    def in_hbm(values):
        return [pltpu.with_memory_space_constraint(value, pltpu.HBM) for value in values]

    sent = pl.pallas_call(
        rims_kernel,
        out_shape=(half_tile, half_tile),
        in_specs=[hbm] * 4,
        out_specs=(any_space, any_space),
        scratch_shapes=[pltpu.SemaphoreType.DMA((8,))],
        compiler_params=params(),
        name="rims",
    )(*in_hbm(fields))
    own, monitor, controls, wells, *sent_strips = pl.pallas_call(
        functools.partial(strip_pack_kernel, kinds),
        out_shape=(
            shape(4, samples * layers * OWN, LANES),
            shape(layers * OWN, LANES),
            shape(1, number),
            jax.ShapeDtypeStruct((1, number), jnp.int32),
        )
        + (
            shape(INNER, 2, SUBLANES, LANES),
            shape(INNER // 2, 2, SUBLANES, LANES),
            shape(INNER // 2, 2, SUBLANES, LANES),
        )
        * n,
        in_specs=[hbm] * 7,
        out_specs=(vmem(),) * (4 + 3 * n),
        scratch_shapes=[pltpu.SemaphoreType.DMA((7,))],
        compiler_params=params(),
        name="strips",
    )(
        *in_hbm(value.reshape(-1, LANES) for value in (*fields, monitor)),
        *in_hbm(value.reshape(1, -1) for value in (controls, wells)),
    )
    got, got_strips = exchange(sent, sent_strips, kinds)
    tile_shape = shape(EXT, 2, SUBLANES, LANES)
    strip_shape = shape(INNER, 2, SUBLANES, LANES)
    saved_shape = shape(JOIN, 4, SUBLANES, LANES)
    blocks = (1 + n) * EXT * layers
    *prepared, split = pl.pallas_call(
        functools.partial(source_kernel, kinds),
        out_shape=(tile_shape,)
        + (strip_shape,) * n
        + (tile_shape,) * 5
        + (
            shape(4, INNER, 2, SUBLANES, LANES),
            saved_shape,
            jax.ShapeDtypeStruct((number, 2 * LANES), jnp.bfloat16),
        ),
        in_specs=[vmem()] * 4,
        out_specs=(vmem(),) * (1 + n + 5 + 3),
        scratch_shapes=[
            pltpu.VMEM((blocks, 2 * LANES), jnp.float32),
            pltpu.VMEM((blocks, LANES), jnp.float32),
        ],
        compiler_params=params(),
        name="source",
    )(wells, controls, profile, own)
    got = [part.reshape(4, -1, LANES) for part in got]
    tail_count = samples * lax.axis_size("sa") // 2
    half_start = shape(DEPTH, 2, SUBLANES, LANES)
    smem = pl.BlockSpec(memory_space=pltpu.SMEM)
    first_tile = 4 + 3 * n + 1 + n
    final, start_a, start_b, objective, start, *rest = pl.pallas_call(
        functools.partial(forward_kernel, kinds, tail_count),
        out_shape=(
            shape(samples * layers * OWN, LANES),
            half_start,
            half_start,
            shape(SUBLANES, LANES),
            tile_shape,
        )
        + (tile_shape,) * 5
        + (strip_shape,) * (5 * n)
        + (
            shape(INNER // 2, SUBLANES, LANES),
            shape(INNER // 4, SUBLANES, LANES),
            shape(INNER // 4, SUBLANES, LANES),
        )
        * n,
        in_specs=[vmem(), smem] + [vmem()] * (2 + 3 * n + 1 + n + 5 + 2),
        out_specs=(vmem(),) * (5 + 5 + 5 * n + 3 * n),
        input_output_aliases={first_tile + k: 5 + k for k in range(5)},
        compiler_params=params(),
        name="forward",
    )(monitor, ranking, *got, *got_strips, *prepared)
    tile, strips, start_strips = split_refs(rest, 5, 5 * n, 3 * n)
    got_start, got_start_strips = exchange((start_a, start_b), start_strips, kinds)
    strip_coefs = [strips[5 * k + c] for k in range(n) for c in range(1, 5)]
    begun = pl.pallas_call(
        adjoint_ahead_kernel,
        out_shape=(tile_shape, shape(OWN, 2, SUBLANES, LANES), saved_shape, strip_shape),
        in_specs=[vmem()] * 5,
        out_specs=(vmem(),) * 4,
        input_output_aliases={0: 0},
        compiler_params=params(),
        name="ahead",
    )(start, *tile[1:])
    cells = layers * OWN * count_x * LANES * count_y
    summed, _, _ = pl.pallas_call(
        functools.partial(adjoint_kernel, kinds, 0.5 / (tail_count * cells)),
        out_shape=(shape(1, number + LANES), tile_shape, shape(OWN, 2, SUBLANES, LANES)),
        in_specs=[vmem()] * (2 + 3 * n + 4 + 4 + 4 * n + 3),
        out_specs=(vmem(),) * 3,
        input_output_aliases={2 + 3 * n: 1, 3 + 3 * n: 2},
        scratch_shapes=[pltpu.VMEM((INNER, 2, SUBLANES, LANES), jnp.float32)] * (2 * n)
        + [pltpu.VMEM((OWN * layers, LANES), jnp.float32)],
        compiler_params=params(),
        name="adjoint",
    )(
        *got_start,
        *got_start_strips,
        *begun,
        *tile[1:],
        *strip_coefs,
        objective,
        wells,
        split,
    )
    gradient, objective = total_over(summed, AXES)
    return final.reshape(initial.shape), gradient.reshape(-1), objective.reshape(-1)


def solution(mesh):
    in_specs = (
        P(("groups", "sa"), None, "gx", "gy"),
        P(("groups", "sa"), None, "gx", "gy"),
        P(("groups", "sa"), None, "gx", "gy"),
        P(("groups", "sa"), None, "gx", "gy"),
        P("groups", "gx", "gy"),
        P("groups"),
        P("groups", None),
        P("groups"),
        P(("groups", "sa")),
    )
    out_specs = (P(("groups", "sa"), None, "gx", "gy"), P("groups"), P("groups"))
    return jax.shard_map(local, mesh=mesh, in_specs=in_specs, out_specs=out_specs, check_vma=False)
```

```python
import functools

import jax
import jax.numpy as jnp
from jax import lax
from jax.experimental import pallas as pl
from jax.experimental.pallas import tpu as pltpu
from jax.sharding import PartitionSpec as P

ITERS = 16
KAPPA = 0.1
VERT = 0.05
LANES = 128
SUBLANES = 8
DEPTH = ITERS
OWN = 2 * DEPTH
EXT = OWN + 2 * DEPTH
WIDE = 2 * DEPTH
GROUPS = LANES // WIDE
INNER = EXT // GROUPS
JOIN = ITERS // 2
CHUNK = 2048
VMEM_LIMIT = 24 * 1024 * 1024


def vmem():
    return pl.BlockSpec(memory_space=pltpu.VMEM)


def params():
    return pltpu.CompilerParams(vmem_limit_bytes=VMEM_LIMIT)


def sub_id():
    return lax.broadcasted_iota(jnp.int32, (SUBLANES, LANES), 0)


def lane_id():
    return lax.broadcasted_iota(jnp.int32, (SUBLANES, LANES), 1)


def wrap(shift):
    return shift % LANES if isinstance(shift, int) else lax.rem(shift, LANES)


def lane_roll(value, shift):
    if isinstance(shift, int) and shift % LANES == 0:
        return value
    return pltpu.roll(value, wrap(shift), 1)


def pick(flag, yes, no):
    if isinstance(flag, bool):
        return yes if flag else no
    return jnp.where(flag, yes, no)


def odd_tile():
    return lax.rem(lax.axis_index("gx"), 2)


def lacks_b():
    x = lax.axis_index("gx")
    return (x == 0) | (x == lax.axis_size("gx") - 1)


def strip_kinds(count):
    return (None,) if count == 2 else (True, False)


def is_right(kind):
    return lax.axis_index("gy") == 0 if kind is None else kind


def planes(ref, row, half, rows):
    return ref[pl.ds(half * rows + row, SUBLANES, stride=2 * rows), :]


def copy_all(pairs, sems):
    copies = [pltpu.make_async_copy(*pair, sems.at[k]) for k, pair in enumerate(pairs)]
    for copy in copies:
        copy.start()
    for copy in copies:
        copy.wait()


def rims_kernel(initial, retard, velx, vely, out_a, out_b, sems):
    odd = odd_tile()
    pairs = []
    for field, ref in enumerate((initial, retard, velx, vely)):
        for out, base in ((out_a, DEPTH * (1 - odd)), (out_b, DEPTH * odd)):
            source = ref.at[:, :, pl.ds(pl.multiple_of(base, DEPTH), DEPTH), :]
            pairs.append((source, out.at[field]))
    copy_all(pairs, sems)


def edge_offset(kind):
    return DEPTH * (1 - lax.axis_index("gy")) if kind is None else (0 if kind else DEPTH)


def strip_pack_kernel(kinds, *refs):
    ins, (own, *copied), outs, (sems,) = split_refs(refs, 7, 4, 3 * len(kinds), 1)
    pairs = [(ref, own.at[field]) for field, ref in enumerate(ins[:4])]
    copy_all(pairs + list(zip(ins[4:], copied)), sems)
    odd = odd_tile()
    slot = lane_id() // DEPTH
    for number, kind in enumerate(kinds):
        to_y, to_a, to_b = outs[3 * number : 3 * number + 3]
        offset = edge_offset(kind)

        def put(packed, field, row, half, target):
            moved = lane_roll(planes(own.at[field], row, half, OWN), DEPTH * target + offset)
            return moved if packed is None else jnp.where(slot == target, moved, packed)

        for half in range(2):
            for i in range(INNER):
                packed = None
                for field in range(4):
                    for j in range(2):
                        target = 4 * (field // 2) + 2 * j + field % 2
                        packed = put(packed, field, INNER * j + i, half, target)
                to_y[i, half] = packed
            for out, base in ((to_a, DEPTH * (1 - odd)), (to_b, DEPTH * odd)):
                for i in range(INNER // 2):
                    packed = None
                    for field in range(4):
                        for upper in range(2):
                            row = base + INNER // 2 * upper + i
                            target = 4 * upper + field
                            target = slot_b(odd, target) if out is to_b else target
                            packed = put(packed, field, row, half, target)
                    out[i, half] = packed


def coefficients(retard, velx, vely):
    spread = KAPPA * retard
    from_x = retard * velx + spread
    from_y = retard * vely + spread
    keep = 1.0 - (from_x + from_y + (2.0 + 2.0 * VERT / KAPPA) * spread)
    return keep, from_x, from_y, spread


def store_tile(refs, row, half, raw, source=None):
    state, retard, velx, vely = raw
    keep, from_x, from_y, spread = coefficients(retard, velx, vely)
    from_y = jnp.where(lane_id() == 0, 0.0, from_y)
    for ref, value in zip(refs, (state, keep, from_x, from_y, spread)):
        ref[row, half] = value


def source_kernel(kinds, tail_count, wells, controls, profile, own, monitor, ranking, *refs):
    n = len(kinds)
    sources, tile, edges, (saved, weights, split), (acc, acc_low) = split_refs(refs, 1 + n, 5, 1, 3, 2)
    for x in range(OWN):
        for half in range(2):
            raw = [planes(own.at[field], x, half, OWN) for field in range(4)]
            store_tile(tile, DEPTH + x, half, raw)
    first_j = lane_id() // WIDE == 1
    for field in range(4):
        for i in range(INNER):
            for half in range(2):
                moved = [
                    lane_roll(planes(own.at[field], INNER * j + i, half, OWN), WIDE * (j + 1) + DEPTH)
                    for j in range(2)
                ]
                edges[0][field, i, half] = jnp.where(first_j, *moved)

    x_index, y_index = lax.axis_index("gx"), lax.axis_index("gy")
    all_x, all_blocks = OWN * lax.axis_size("gx"), lax.axis_size("gy")
    layers = 4
    per_block = EXT * layers
    r = lax.broadcasted_iota(jnp.int32, (per_block, 1), 0)
    x = x_index * OWN - DEPTH + r // layers
    ids = []
    for block in [y_index] + [
        1 - y_index if kind is None else (y_index + 1 if kind else y_index - 1) for kind in kinds
    ]:
        inside = (x >= 0) & (x < all_x) & (block >= 0) & (block < all_blocks)
        ids.append(jnp.where(inside, ((r % layers) * all_x + x) * all_blocks + block, -1))
    ids = jnp.concatenate(ids, axis=0)
    acc[...] = jnp.zeros_like(acc)
    acc_low[...] = jnp.zeros_like(acc_low)

    def chunk(c, carry):
        span = pl.ds(pl.multiple_of(c * CHUNK, CHUNK), CHUNK)
        part = profile[span, :]
        high = part.astype(jnp.bfloat16)
        low = (part - high.astype(jnp.float32)).astype(jnp.bfloat16)
        rate = controls[:, span]
        rate_high = rate.astype(jnp.bfloat16).astype(jnp.float32)
        hit = ids == wells[:, span]
        hot_high = jnp.where(hit, rate_high, 0.0).astype(jnp.bfloat16)
        hot_low = jnp.where(hit, rate - rate_high, 0.0).astype(jnp.bfloat16)
        split_part = jnp.concatenate([high, low], axis=1)
        split[span, :] = split_part
        acc[...] += jnp.dot(hot_high, split_part, preferred_element_type=jnp.float32)
        acc_low[...] += jnp.dot(hot_low, high, preferred_element_type=jnp.float32)
        return carry

    lax.fori_loop(0, wells.shape[1] // CHUNK, chunk, 0)
    acc_low[...] += acc[:, :LANES] + acc[:, LANES:]
    upper = sub_id() % 2 == 1
    group = lane_id() // WIDE

    def both(first, half):
        low_layer = jnp.broadcast_to(acc_low[pl.ds(first + half, 1), :], (SUBLANES, LANES))
        high_layer = jnp.broadcast_to(acc_low[pl.ds(first + 2 + half, 1), :], (SUBLANES, LANES))
        return jnp.where(upper, high_layer, low_layer)

    masks = Masks(kinds)
    for number in range(n):
        for i in range(INNER):
            for half in range(2):
                packed = None
                for j in range(GROUPS):
                    e = j * INNER + i
                    here = both(e * layers, half)
                    if number == 0:
                        sources[0][e, half] = here
                    beside = both((number + 1) * per_block + e * layers, half)
                    mixed = jnp.where(masks.own_edge[number], here, beside)
                    moved = lane_roll(mixed, WIDE * j + DEPTH)
                    packed = moved if packed is None else jnp.where(group == j, moved, packed)
                sources[1 + number][i, half] = packed
    sample = sub_id() // 2
    tail = jnp.zeros((SUBLANES, LANES), jnp.float32)
    for s in range(4):
        tail = jnp.where(sample == s, jnp.where(ranking[s] < tail_count, 1.0, 0.0), tail)
    for x in range(OWN):
        for half in range(2):
            tile[0][DEPTH + x, half] += sources[0][DEPTH + x, half]
            low = jnp.broadcast_to(monitor[pl.ds(half * OWN + x, 1), :], (SUBLANES, LANES))
            high = jnp.broadcast_to(monitor[pl.ds((2 + half) * OWN + x, 1), :], (SUBLANES, LANES))
            weights[x, half] = tail * jnp.where(upper, high, low)
    ahead(functools.partial(forward_step, masks, (*tile, sources[0]), sourced=True), tile[0], saved)


class Masks:
    def __init__(self, kinds):
        lane = lane_id()
        self.first, self.last = lane == 0, lane == LANES - 1
        self.group = lane // WIDE
        upper = sub_id() % 2 == 1
        self.below = jnp.where(upper, VERT / KAPPA, 0.0)
        self.above = jnp.where(upper, 0.0, VERT / KAPPA)
        self.right = [is_right(kind) for kind in kinds]
        half, eighth, sixteenth = lane % WIDE // DEPTH, lane // DEPTH, lane // JOIN
        self.rim = [half == pick(right, 1, 0) for right in self.right]
        self.not_rim = [half == pick(right, 0, 1) for right in self.right]
        self.own_edge = [eighth != pick(right, 0, LANES // DEPTH - 1) for right in self.right]
        self.outer = [sixteenth == pick(right, LANES // JOIN - 1, 0) for right in self.right]

    def vertical(self, pair):
        low = (VERT / KAPPA) * pair[1] + self.below * pltpu.roll(pair[1], 1, 0)
        high = (VERT / KAPPA) * pair[0] + self.above * pltpu.roll(pair[0], SUBLANES - 1, 0)
        return low, high

    def outer_from(self, strips, e, half, value):
        j, i = divmod(e, INNER)
        for strip, outer in zip(strips, self.outer):
            value = jnp.where(outer, lane_roll(strip[i, half], LANES - DEPTH - WIDE * j), value)
        return value

    def join(self, tile, strips, first, last):
        for e in range(first, last + 1):
            j, i = divmod(e, INNER)
            for h in range(2):
                value = self.outer_from(strips, e, h, tile[e, h])
                tile[e, h] = value
                moved = lane_roll(value, WIDE * j + DEPTH)
                for strip, own in zip(strips, self.not_rim):
                    strip[i, h] = jnp.where((self.group == j) & own, moved, strip[i, h])


def slot_b(odd, slot):
    return lax.rem(slot + 6 - 4 * odd, LANES // DEPTH)


def places(odd):
    return DEPTH * (2 - odd), DEPTH * (1 + odd), 3 * DEPTH * (1 - odd), 3 * DEPTH * odd


def merge_strip(masks, number, odd, slot, middle, own_a, own_b, rim_y, rim_a, rim_b):
    first_a = places(odd)[2]
    inner = (masks.group == 1) | (masks.group == 2)
    own = jnp.where(masks.group == 3 * (1 - odd), own_a, own_b)
    own = jnp.where(inner, middle, own)
    rim = jnp.where(lane_id() // DEPTH == slot, rim_a, rim_b)
    rim = lane_roll(rim, 2 * first_a + pick(masks.right[number], DEPTH, 0) + LANES - DEPTH * slot)
    return jnp.where(masks.rim[number], jnp.where(inner, rim_y, rim), own)


def forward_step(masks, tile, first, last, lower=None, upper=None, sourced=True):
    state, keep, from_x, from_y, spread, source = tile
    before = lower or [state[first - 1, h] for h in range(2)]
    here = [state[first, h] for h in range(2)]
    for e in range(first, last + 1):
        after = upper if upper and e == last else [state[e + 1, h] for h in range(2)]
        upright = masks.vertical(here)
        for h in range(2):
            y_high = jnp.where(masks.last, 0.0, lane_roll(here[h], LANES - 1))
            value = (
                keep[e, h] * here[h]
                + from_x[e, h] * before[h]
                + from_y[e, h] * lane_roll(here[h], 1)
                + spread[e, h] * (after[h] + y_high + upright[h])
            )
            state[e, h] = value + source[e, h] if sourced else value
        before, here = here, after


def forward_strips(masks, strips, sourced):
    for strip, keep, from_x, from_y, spread, source in strips:
        old = [strip[0, h] for h in range(2)]
        here = old
        before = [lane_roll(strip[INNER - 1, h], WIDE) for h in range(2)]
        for i in range(INNER):
            if i < INNER - 1:
                after = [strip[i + 1, h] for h in range(2)]
            else:
                after = [lane_roll(value, LANES - WIDE) for value in old]
            upright = masks.vertical(here)
            for h in range(2):
                value = (
                    keep[i, h] * here[h]
                    + from_x[i, h] * before[h]
                    + from_y[i, h] * lane_roll(here[h], 1)
                    + spread[i, h] * (after[h] + lane_roll(here[h], LANES - 1) + upright[h])
                )
                strip[i, h] = value + source[i, h] if sourced else value
            before, here = here, after


def scaled(refs, e, value=None):
    state, _, from_x, from_y, spread, _ = refs
    value = value or [state[e, h] for h in range(2)]
    return (
        value,
        [from_x[e, h] * value[h] for h in range(2)],
        [from_y[e, h] * value[h] for h in range(2)],
        [spread[e, h] * value[h] for h in range(2)],
    )


def adjoint_step(masks, tile, first, last, lower=None, upper=None):
    state, keep, from_x, from_y, spread, total = tile
    before, here = scaled(tile, first - 1, lower), scaled(tile, first)
    for e in range(first, last + 1):
        after = scaled(tile, e + 1, upper if e == last else None)
        value, _, by_y, by_spread = here
        upright = masks.vertical(by_spread)
        for h in range(2):
            y_low = jnp.where(masks.first, 0.0, lane_roll(by_spread[h], 1))
            fresh = (
                keep[e, h] * value[h]
                + (after[1][h] + before[3][h])
                + (y_low + lane_roll(by_y[h], LANES - 1))
                + upright[h]
            )
            state[e, h] = fresh
            if DEPTH <= e < DEPTH + OWN:
                total[e - DEPTH, h] += fresh
        before, here = here, after


def adjoint_strips(masks, strips):
    for refs in strips:
        strip, keep, from_x, from_y, spread, total = refs
        here = scaled(refs, 0)
        wrapped = [lane_roll(value, LANES - WIDE) for value in here[1]]
        last_row = scaled(refs, INNER - 1)
        before = (None, None, None, [lane_roll(value, WIDE) for value in last_row[3]])
        for i in range(INNER):
            after = scaled(refs, i + 1) if i < INNER - 1 else (None, wrapped, None, None)
            value, _, by_y, by_spread = here
            upright = masks.vertical(by_spread)
            for h in range(2):
                fresh = (
                    keep[i, h] * value[h]
                    + (after[1][h] + before[3][h])
                    + (lane_roll(by_spread[h], 1) + lane_roll(by_y[h], LANES - 1))
                    + upright[h]
                )
                strip[i, h] = fresh
                total[i, h] += fresh
            before, here = here, after


def ahead(step, state, saved):
    for t in range(JOIN):
        low, high = DEPTH + 1 + t, DEPTH + OWN - 2 - t
        for h in range(2):
            saved[t, h] = state[low, h]
            saved[t, 2 + h] = state[high, h]
        step(low, high)


def sweep(step, strip_step, join, saved):
    for t in range(ITERS):
        sourced = t < ITERS - 1
        if t == JOIN:
            join(t, EXT - 1 - t)
        if t < JOIN:
            step(t + 1, DEPTH + t, sourced, upper=[saved[t, h] for h in range(2)])
            step(DEPTH + OWN - 1 - t, EXT - 2 - t, sourced, lower=[saved[t, 2 + h] for h in range(2)])
        else:
            step(t + 1, EXT - 2 - t, sourced)
        strip_step(sourced)


def split_refs(refs, *counts):
    out = []
    for count in counts:
        out.append(refs[:count])
        refs = refs[count:]
    return out


def forward_kernel(kinds, tail_count, *refs):
    n = len(kinds)
    ins, got_strips, sources, tile, (edges, saved, weights), outs, strips, out_strips, states = split_refs(
        refs, 2, 3 * n, 1 + n, 5, 3, 5 + 5, 4 * n, 3 * n, n
    )
    got_a, got_b = ins
    final, start_a, start_b, objective, start, *tile = outs
    odd = odd_tile()
    masks = Masks(kinds)
    state = tile[0]
    _, _, at_a, at_b = places(odd)
    present = jnp.where(lacks_b(), 0.0, 1.0)
    present_lanes = jnp.where(masks.group == 3 * odd, present, 1.0)
    for x in range(DEPTH):
        for h in range(2):
            raw_a = [planes(got_a.at[field], x, h, DEPTH) for field in range(4)]
            raw_b = [planes(got_b.at[field], x, h, DEPTH) for field in range(4)]
            raw_b[:2] = [value * present for value in raw_b[:2]]
            store_tile(tile, at_a + x, h, raw_a)
            store_tile(tile, at_b + x, h, raw_b)
            i = x
            upper = i // (INNER // 2)
            for k in range(n):
                got = got_strips[3 * k : 3 * k + 3]
                side = pick(masks.right[k], DEPTH, 0)
                raw = [
                    merge_strip(
                        masks,
                        k,
                        odd,
                        4 * upper + field,
                        edges[field, i, h],
                        lane_roll(raw_a[field], 2 * at_a + DEPTH),
                        lane_roll(raw_b[field], 2 * at_b + DEPTH),
                        lane_roll(
                            got[0][i, h], LANES + WIDE + side - 64 * (field // 2) - DEPTH * (field % 2)
                        ),
                        got[1][i % (INNER // 2), h],
                        got[2][i % (INNER // 2), h],
                    )
                    for field in range(4)
                ]
                raw[:2] = [value * present_lanes for value in raw[:2]]
                mine = (states[k], *strips[4 * k : 4 * k + 4])
                for ref, value in zip(mine, (raw[0] + sources[1 + k][i, h], *coefficients(*raw[1:]))):
                    ref[i, h] = value
    for e in (*range(DEPTH), *range(DEPTH + OWN, EXT)):
        for h in range(2):
            state[e, h] += sources[0][e, h]
    strip_refs = [(states[k], *strips[4 * k : 4 * k + 4], sources[1 + k]) for k in range(n)]
    strip_states = [strip[0] for strip in strip_refs]

    def step(first, last, sourced, **beside):
        forward_step(masks, (*tile, sources[0]), first, last, sourced=sourced, **beside)

    sweep(
        step,
        functools.partial(forward_strips, masks, strip_refs),
        functools.partial(masks.join, state, strip_states),
        saved,
    )

    sums = [jnp.zeros((SUBLANES, LANES), jnp.float32) for _ in range(4)]
    for x in range(OWN):
        for h in range(2):
            fresh = masks.outer_from(strip_states, DEPTH + x, h, state[DEPTH + x, h])
            final[pl.ds(h * OWN + x, SUBLANES, stride=2 * OWN), :] = fresh
            weighted = weights[x, h] * fresh
            start[DEPTH + x, h] = weighted * (1.0 / (tail_count * ITERS))
            sums[x % 4] = sums[x % 4] + weighted * fresh
    objective[...] = (sums[0] + sums[1]) + (sums[2] + sums[3])

    base_a, base_b, _, _ = places(odd)
    for x in range(DEPTH):
        for h in range(2):
            start_a[x, h] = start[base_a + x, h]
            start_b[x, h] = start[base_b + x, h]
    slot = lane_id() // DEPTH
    for k, kind in enumerate(kinds):
        to_y, to_a, to_b = out_strips[3 * k : 3 * k + 3]
        offset = edge_offset(kind)

        def put(packed, row, h, target):
            moved = lane_roll(start[row, h], DEPTH * target + offset)
            return moved if packed is None else jnp.where(slot == target, moved, packed)

        for i in range(INNER // 2):
            packed = None
            for upper_half in range(2):
                for j in range(2):
                    for h in range(2):
                        row = DEPTH + INNER * j + INNER // 2 * upper_half + i
                        packed = put(packed, row, h, 4 * upper_half + 2 * j + h)
            to_y[i] = packed
        for out, base in ((to_a, base_a), (to_b, base_b)):
            for i in range(INNER // 4):
                packed = None
                for quarter in range(4):
                    for h in range(2):
                        target = 2 * quarter + h
                        target = slot_b(odd, target) if out is to_b else target
                        packed = put(packed, base + INNER // 4 * quarter + i, h, target)
                out[i] = packed


def adjoint_ahead_kernel(*refs):
    coefs, (final, state, total, saved, edges, final_out, sem) = refs[1:5], refs[5:]
    leave = pltpu.make_async_copy(final, final_out, sem)
    leave.start()
    masks = Masks(())
    total[...] = jnp.zeros_like(total)
    first_j = masks.group == 1
    for i in range(INNER):
        for h in range(2):
            moved = [
                lane_roll(state[DEPTH + INNER * j + i, h], WIDE * (j + 1) + DEPTH) for j in range(2)
            ]
            edges[i, h] = jnp.where(first_j, *moved)
    ahead(functools.partial(adjoint_step, masks, (state, *coefs, total)), state, saved)
    leave.wait()


def adjoint_kernel(kinds, scale, *refs):
    n = len(kinds)
    parts, part_strips, (_, _, saved, edges), coefs, strip_coefs, rest, outs, strips, (rows,) = split_refs(
        refs, 2, 3 * n, 4, 4, 4 * n, 3, 3, 2 * n, 1
    )
    objective, wells, profile = rest
    out, state, total = outs
    odd = odd_tile()
    masks = Masks(kinds)
    at = places(odd)[2:]
    for part, first in zip(parts, at):
        for x in range(DEPTH):
            for h in range(2):
                state[first + x, h] = part[x, h]
    strip_refs = []
    for k in range(n):
        strip, strip_total = strips[2 * k : 2 * k + 2]
        got_y, got_a, got_b = part_strips[3 * k : 3 * k + 3]
        side = pick(masks.right[k], DEPTH, 0)
        for i in range(INNER):
            eighth, quarter = divmod(i, INNER // 2)[0], divmod(i, INNER // 4)[0]
            for h in range(2):
                moved = [
                    lane_roll(part[i, h], 2 * first + DEPTH) for part, first in zip(parts, at)
                ]
                beside = merge_strip(
                    masks,
                    k,
                    odd,
                    2 * quarter + h,
                    edges[i, h],
                    moved[0],
                    moved[1],
                    lane_roll(got_y[i % (INNER // 2)], LANES + WIDE + side - 64 * eighth - DEPTH * h),
                    got_a[i % (INNER // 4)],
                    got_b[i % (INNER // 4)],
                )
                strip[i, h] = beside
        strip_refs.append((strip, *strip_coefs[4 * k : 4 * k + 4], strip_total))
        strip_total[...] = jnp.zeros_like(strip_total)

    def step(first, last, _, **beside):
        adjoint_step(masks, (state, *coefs, total), first, last, **beside)

    sweep(
        step,
        lambda _: adjoint_strips(masks, strip_refs),
        functools.partial(masks.join, state, [refs[0] for refs in strip_refs]),
        saved,
    )
    totals = [refs[-1] for refs in strip_refs]
    for x in range(OWN):
        for h in range(2):
            value = masks.outer_from(totals, DEPTH + x, h, total[x, h])
            value = value + pltpu.roll(value, 4, 0)
            value = value + pltpu.roll(value, 2, 0)
            rows[pl.ds((2 * x + h) * 2, 2), :] = value[:2]
    count = rows.shape[0]
    r = lax.broadcasted_iota(jnp.int32, (count, 1), 0)
    layer = (r % 2) * 2 + (r // 2) % 2
    x = lax.axis_index("gx") * OWN + r // 4
    ids = (layer * (OWN * lax.axis_size("gx")) + x) * lax.axis_size("gy") + lax.axis_index("gy")
    field = rows[...]
    high = field.astype(jnp.bfloat16)
    low = (field - high.astype(jnp.float32)).astype(jnp.bfloat16)
    both = jnp.concatenate([high, low], axis=0)
    contract = (((1,), (1,)), ((), ()))
    controls = wells.shape[1]

    def chunk(c, carry):
        span = pl.ds(pl.multiple_of(c * CHUNK, CHUNK), CHUNK)
        share_high, share_low = profile[span, :LANES], profile[span, LANES:]
        first = lax.dot_general(both, share_high, contract, preferred_element_type=jnp.float32)
        second = lax.dot_general(high, share_low, contract, preferred_element_type=jnp.float32)
        product = first[:count] + first[count:] + second
        chosen = jnp.where(ids == wells[:, span], product, 0.0)
        out[:, span] = jnp.sum(chosen, axis=0, keepdims=True)
        return carry

    lax.fori_loop(0, controls // CHUNK, chunk, 0)
    whole = jnp.sum(jnp.sum(objective[...], axis=0, keepdims=True), axis=1, keepdims=True)
    out[:, controls:] = jnp.broadcast_to(whole * scale, (1, LANES))


def shape(*dims):
    return jax.ShapeDtypeStruct(dims, jnp.float32)


def same(x, count):
    return x


def partner_a(x, count):
    return x ^ 1


def partner_b(x, count):
    other = x + 1 if x % 2 else x - 1
    return other if 0 <= other < count else None


AXES = ("gx", "gy", "sa")


def swap_pairs(partner, kind, count_x, count_y, count_s):
    pairs = []
    for x in range(count_x):
        for y in range(count_y):
            for s in range(count_s):
                from_x, from_s = partner(x, count_x), s
                from_y = y if kind == "tile" else 1 - y if kind is None else (y + 1 if kind else y - 1)
                if from_x is None:
                    from_x, from_y, from_s = x, y, s ^ 1
                if 0 <= from_y < count_y:
                    pairs.append(
                        ((from_x * count_y + from_y) * count_s + from_s, (x * count_y + y) * count_s + s)
                    )
    return pairs


def exchange(tiles, strips, kinds):
    counts = [lax.axis_size(axis) for axis in AXES]
    got = [
        lax.ppermute(tile, AXES, swap_pairs(partner, "tile", *counts))
        for tile, partner in zip(tiles, (partner_a, partner_b))
    ]
    got_strips = []
    for k, kind in enumerate(kinds):
        for strip, partner in zip(strips[3 * k : 3 * k + 3], (same, partner_a, partner_b)):
            got_strips.append(lax.ppermute(strip, AXES, swap_pairs(partner, kind, *counts)))
    return got, got_strips


def add_kernel(value, *refs):
    got, (gradient, objective) = refs[:-2], refs[-2:]
    total = value[...] + got[0][...]
    if len(got) == 3:
        total = total + (got[1][...] + got[2][...])
    number = gradient.shape[1]
    gradient[...] = total[:, :number]
    objective[...] = total[:, number : number + 1]


def total_over(value, axes):
    count = 1
    for axis in axes:
        count *= lax.axis_size(axis)
    bit = 1
    while bit < count:
        bits = [bit] if 2 * bit >= count else [bit, 2 * bit, 3 * bit]
        got = [lax.ppermute(value, axes, [(i, i ^ b) for i in range(count)]) for b in bits]
        bit *= 4
        if bit >= count:
            break
        value = value + got[0]
        if len(got) == 3:
            value = value + (got[1] + got[2])
    return pl.pallas_call(
        add_kernel,
        out_shape=(shape(1, value.shape[1] - LANES), shape(1, 1)),
        in_specs=[vmem()] * (1 + len(got)),
        out_specs=(vmem(), vmem()),
        compiler_params=params(),
        name="total",
    )(value, *got)


def local(initial, retard, velx, vely, monitor, controls, profile, wells, ranking):
    samples, layers, width_x, width_y = initial.shape
    count_x, count_y = lax.axis_size("gx"), lax.axis_size("gy")
    assert (samples, layers, width_x, width_y) == (4, 4, OWN, LANES)
    assert count_x % 2 == 0 and lax.axis_size("sa") == 2
    number = controls.shape[0]
    assert number % CHUNK == 0
    kinds = strip_kinds(count_y)
    n = len(kinds)
    half_tile = shape(4, samples, layers, DEPTH, LANES)
    hbm = pl.BlockSpec(memory_space=pltpu.HBM)
    smem = pl.BlockSpec(memory_space=pltpu.SMEM)
    tail_count = samples * lax.axis_size("sa") // 2
    any_space = pl.BlockSpec(memory_space=pl.ANY)
    fields = (initial, retard, velx, vely)

    def in_hbm(values):
        return [pltpu.with_memory_space_constraint(value, pltpu.HBM) for value in values]

    sent = pl.pallas_call(
        rims_kernel,
        out_shape=(half_tile, half_tile),
        in_specs=[hbm] * 4,
        out_specs=(any_space, any_space),
        scratch_shapes=[pltpu.SemaphoreType.DMA((8,))],
        compiler_params=params(),
        name="rims",
    )(*in_hbm(fields))
    own, monitor, controls, wells, *sent_strips = pl.pallas_call(
        functools.partial(strip_pack_kernel, kinds),
        out_shape=(
            shape(4, samples * layers * OWN, LANES),
            shape(layers * OWN, LANES),
            shape(1, number),
            jax.ShapeDtypeStruct((1, number), jnp.int32),
        )
        + (
            shape(INNER, 2, SUBLANES, LANES),
            shape(INNER // 2, 2, SUBLANES, LANES),
            shape(INNER // 2, 2, SUBLANES, LANES),
        )
        * n,
        in_specs=[hbm] * 7,
        out_specs=(vmem(),) * (4 + 3 * n),
        scratch_shapes=[pltpu.SemaphoreType.DMA((7,))],
        compiler_params=params(),
        name="strips",
    )(
        *in_hbm(value.reshape(-1, LANES) for value in (*fields, monitor)),
        *in_hbm(value.reshape(1, -1) for value in (controls, wells)),
    )
    got, got_strips = exchange(sent, sent_strips, kinds)
    tile_shape = shape(EXT, 2, SUBLANES, LANES)
    strip_shape = shape(INNER, 2, SUBLANES, LANES)
    saved_shape = shape(JOIN, 4, SUBLANES, LANES)
    blocks = (1 + n) * EXT * layers
    *prepared, split = pl.pallas_call(
        functools.partial(source_kernel, kinds, tail_count),
        out_shape=(tile_shape,)
        + (strip_shape,) * n
        + (tile_shape,) * 5
        + (
            shape(4, INNER, 2, SUBLANES, LANES),
            saved_shape,
            shape(OWN, 2, SUBLANES, LANES),
            jax.ShapeDtypeStruct((number, 2 * LANES), jnp.bfloat16),
        ),
        in_specs=[vmem()] * 5 + [smem],
        out_specs=(vmem(),) * (1 + n + 5 + 4),
        scratch_shapes=[
            pltpu.VMEM((blocks, 2 * LANES), jnp.float32),
            pltpu.VMEM((blocks, LANES), jnp.float32),
        ],
        compiler_params=params(),
        name="source",
    )(wells, controls, profile, own, monitor, ranking)
    got = [part.reshape(4, -1, LANES) for part in got]
    half_start = shape(DEPTH, 2, SUBLANES, LANES)
    first_tile = 2 + 3 * n + 1 + n
    final, start_a, start_b, objective, start, *rest = pl.pallas_call(
        functools.partial(forward_kernel, kinds, tail_count),
        out_shape=(
            shape(samples * layers * OWN, LANES),
            half_start,
            half_start,
            shape(SUBLANES, LANES),
            tile_shape,
        )
        + (tile_shape,) * 5
        + (strip_shape,) * (4 * n)
        + (
            shape(INNER // 2, SUBLANES, LANES),
            shape(INNER // 4, SUBLANES, LANES),
            shape(INNER // 4, SUBLANES, LANES),
        )
        * n,
        in_specs=[vmem()] * (2 + 3 * n + 1 + n + 5 + 3),
        out_specs=(vmem(),) * (5 + 5 + 4 * n + 3 * n),
        scratch_shapes=[pltpu.VMEM((INNER, 2, SUBLANES, LANES), jnp.float32)] * n,
        input_output_aliases={first_tile + k: 5 + k for k in range(5)},
        compiler_params=params(),
        name="forward",
    )(*got, *got_strips, *prepared)
    tile, strip_coefs, start_strips = split_refs(rest, 5, 4 * n, 3 * n)
    got_start, got_start_strips = exchange((start_a, start_b), start_strips, kinds)
    *begun, final = pl.pallas_call(
        adjoint_ahead_kernel,
        out_shape=(
            tile_shape,
            shape(OWN, 2, SUBLANES, LANES),
            saved_shape,
            strip_shape,
            shape(*final.shape),
        ),
        in_specs=[vmem()] * 6,
        out_specs=(vmem(),) * 4 + (hbm,),
        scratch_shapes=[pltpu.SemaphoreType.DMA],
        input_output_aliases={0: 0},
        compiler_params=params(),
        name="ahead",
    )(start, *tile[1:], final)
    cells = layers * OWN * count_x * LANES * count_y
    summed, _, _ = pl.pallas_call(
        functools.partial(adjoint_kernel, kinds, 0.5 / (tail_count * cells)),
        out_shape=(
            shape(1, number + LANES),
            tile_shape,
            shape(OWN, 2, SUBLANES, LANES),
        ),
        in_specs=[vmem()] * (2 + 3 * n + 4 + 4 + 4 * n + 3),
        out_specs=(vmem(),) * 3,
        input_output_aliases={2 + 3 * n: 1, 3 + 3 * n: 2},
        scratch_shapes=[pltpu.VMEM((INNER, 2, SUBLANES, LANES), jnp.float32)] * (2 * n)
        + [pltpu.VMEM((OWN * layers, LANES), jnp.float32)],
        compiler_params=params(),
        name="adjoint",
    )(
        *got_start,
        *got_start_strips,
        *begun,
        *tile[1:],
        *strip_coefs,
        objective,
        wells,
        split,
    )
    gradient, objective = total_over(summed, AXES)
    return final.reshape(initial.shape), gradient.reshape(-1), objective.reshape(-1)


def solution(mesh):
    in_specs = (
        P(("groups", "sa"), None, "gx", "gy"),
        P(("groups", "sa"), None, "gx", "gy"),
        P(("groups", "sa"), None, "gx", "gy"),
        P(("groups", "sa"), None, "gx", "gy"),
        P("groups", "gx", "gy"),
        P("groups"),
        P("groups", None),
        P("groups"),
        P(("groups", "sa")),
    )
    out_specs = (P(("groups", "sa"), None, "gx", "gy"), P("groups"), P("groups"))
    return jax.shard_map(local, mesh=mesh, in_specs=in_specs, out_specs=out_specs, check_vma=False)
```

```python
import functools

import jax
import jax.numpy as jnp
from jax import lax
from jax.experimental import pallas as pl
from jax.experimental.pallas import tpu as pltpu
from jax.sharding import PartitionSpec as P

ITERS = 16
KAPPA = 0.1
VERT = 0.05
LANES = 128
SUBLANES = 8
DEPTH = ITERS
OWN = 2 * DEPTH
EXT = OWN + 2 * DEPTH
WIDE = 2 * DEPTH
GROUPS = LANES // WIDE
INNER = EXT // GROUPS
JOIN = ITERS // 2
CHUNK = 4096
VMEM_LIMIT = 24 * 1024 * 1024


def vmem():
    return pl.BlockSpec(memory_space=pltpu.VMEM)


def params():
    return pltpu.CompilerParams(vmem_limit_bytes=VMEM_LIMIT)


def sub_id():
    return lax.broadcasted_iota(jnp.int32, (SUBLANES, LANES), 0)


def lane_id():
    return lax.broadcasted_iota(jnp.int32, (SUBLANES, LANES), 1)


def wrap(shift):
    return shift % LANES if isinstance(shift, int) else lax.rem(shift, LANES)


def lane_roll(value, shift):
    if isinstance(shift, int) and shift % LANES == 0:
        return value
    return pltpu.roll(value, wrap(shift), 1)


def pick(flag, yes, no):
    if isinstance(flag, bool):
        return yes if flag else no
    return jnp.where(flag, yes, no)


def odd_tile():
    return lax.rem(lax.axis_index("gx"), 2)


def lacks_b():
    x = lax.axis_index("gx")
    return (x == 0) | (x == lax.axis_size("gx") - 1)


def strip_kinds(count):
    return (None,) if count == 2 else (True, False)


def is_right(kind):
    return lax.axis_index("gy") == 0 if kind is None else kind


def planes(ref, row, half, rows):
    return ref[pl.ds(half * rows + row, SUBLANES, stride=2 * rows), :]


def copy_all(pairs, sems):
    copies = [pltpu.make_async_copy(*pair, sems.at[k]) for k, pair in enumerate(pairs)]
    for copy in copies:
        copy.start()
    for copy in copies:
        copy.wait()


def rims_kernel(initial, retard, velx, vely, out_a, out_b, sems):
    odd = odd_tile()
    pairs = []
    for field, ref in enumerate((initial, retard, velx, vely)):
        for out, base in ((out_a, DEPTH * (1 - odd)), (out_b, DEPTH * odd)):
            source = ref.at[:, :, pl.ds(pl.multiple_of(base, DEPTH), DEPTH), :]
            pairs.append((source, out.at[field]))
    copy_all(pairs, sems)


def edge_offset(kind):
    return DEPTH * (1 - lax.axis_index("gy")) if kind is None else (0 if kind else DEPTH)


def strip_pack_kernel(kinds, *refs):
    ins, (own, *copied), outs, (sems,) = split_refs(refs, 7, 4, 3 * len(kinds), 1)
    pairs = [(ref, own.at[field]) for field, ref in enumerate(ins[:4])]
    copy_all(pairs + list(zip(ins[4:], copied)), sems)
    odd = odd_tile()
    slot = lane_id() // DEPTH
    for number, kind in enumerate(kinds):
        to_y, to_a, to_b = outs[3 * number : 3 * number + 3]
        offset = edge_offset(kind)

        def put(packed, field, row, half, target):
            moved = lane_roll(planes(own.at[field], row, half, OWN), DEPTH * target + offset)
            return moved if packed is None else jnp.where(slot == target, moved, packed)

        for half in range(2):
            for i in range(INNER):
                packed = None
                for field in range(4):
                    for j in range(2):
                        target = 4 * (field // 2) + 2 * j + field % 2
                        packed = put(packed, field, INNER * j + i, half, target)
                to_y[i, half] = packed
            for out, base in ((to_a, DEPTH * (1 - odd)), (to_b, DEPTH * odd)):
                for i in range(INNER // 2):
                    packed = None
                    for field in range(4):
                        for upper in range(2):
                            row = base + INNER // 2 * upper + i
                            target = 4 * upper + field
                            target = slot_b(odd, target) if out is to_b else target
                            packed = put(packed, field, row, half, target)
                    out[i, half] = packed


def coefficients(retard, velx, vely):
    spread = KAPPA * retard
    from_x = retard * velx + spread
    from_y = retard * vely + spread
    keep = 1.0 - (from_x + from_y + (2.0 + 2.0 * VERT / KAPPA) * spread)
    return keep, from_x, from_y, spread


def store_tile(refs, row, half, raw, source=None):
    state, retard, velx, vely = raw
    keep, from_x, from_y, spread = coefficients(retard, velx, vely)
    from_y = jnp.where(lane_id() == 0, 0.0, from_y)
    for ref, value in zip(refs, (state, keep, from_x, from_y, spread)):
        ref[row, half] = value


def source_kernel(kinds, wells, controls, profile, own, *refs):
    n = len(kinds)
    sources, tile, edges, (saved, split), (acc, acc_low) = split_refs(refs, 1 + n, 5, 1, 2, 2)
    for x in range(OWN):
        for half in range(2):
            raw = [planes(own.at[field], x, half, OWN) for field in range(4)]
            store_tile(tile, DEPTH + x, half, raw)
    first_j = lane_id() // WIDE == 1
    for field in range(4):
        for i in range(INNER):
            for half in range(2):
                moved = [
                    lane_roll(planes(own.at[field], INNER * j + i, half, OWN), WIDE * (j + 1) + DEPTH)
                    for j in range(2)
                ]
                edges[0][field, i, half] = jnp.where(first_j, *moved)

    x_index, y_index = lax.axis_index("gx"), lax.axis_index("gy")
    all_x, all_blocks = OWN * lax.axis_size("gx"), lax.axis_size("gy")
    layers = 4
    per_block = EXT * layers
    r = lax.broadcasted_iota(jnp.int32, (per_block, 1), 0)
    x = x_index * OWN - DEPTH + r // layers
    ids = []
    for block in [y_index] + [
        1 - y_index if kind is None else (y_index + 1 if kind else y_index - 1) for kind in kinds
    ]:
        inside = (x >= 0) & (x < all_x) & (block >= 0) & (block < all_blocks)
        ids.append(jnp.where(inside, ((r % layers) * all_x + x) * all_blocks + block, -1))
    ids = jnp.concatenate(ids, axis=0)
    acc[...] = jnp.zeros_like(acc)
    acc_low[...] = jnp.zeros_like(acc_low)

    def chunk(c, carry):
        span = pl.ds(pl.multiple_of(c * CHUNK, CHUNK), CHUNK)
        part = profile[span, :]
        high = part.astype(jnp.bfloat16)
        low = (part - high.astype(jnp.float32)).astype(jnp.bfloat16)
        rate = controls[:, span]
        rate_high = rate.astype(jnp.bfloat16).astype(jnp.float32)
        hit = ids == wells[:, span]
        hot_high = jnp.where(hit, rate_high, 0.0).astype(jnp.bfloat16)
        hot_low = jnp.where(hit, rate - rate_high, 0.0).astype(jnp.bfloat16)
        split_part = jnp.concatenate([high, low], axis=1)
        split[span, :] = split_part
        acc[...] += jnp.dot(hot_high, split_part, preferred_element_type=jnp.float32)
        acc_low[...] += jnp.dot(hot_low, high, preferred_element_type=jnp.float32)
        return carry

    lax.fori_loop(0, wells.shape[1] // CHUNK, chunk, 0)
    acc_low[...] += acc[:, :LANES] + acc[:, LANES:]
    upper = sub_id() % 2 == 1
    group = lane_id() // WIDE

    def both(first, half):
        low_layer = jnp.broadcast_to(acc_low[pl.ds(first + half, 1), :], (SUBLANES, LANES))
        high_layer = jnp.broadcast_to(acc_low[pl.ds(first + 2 + half, 1), :], (SUBLANES, LANES))
        return jnp.where(upper, high_layer, low_layer)

    masks = Masks(kinds)
    for number in range(n):
        for i in range(INNER):
            for half in range(2):
                packed = None
                for j in range(GROUPS):
                    e = j * INNER + i
                    here = both(e * layers, half)
                    if number == 0:
                        sources[0][e, half] = here
                    beside = both((number + 1) * per_block + e * layers, half)
                    mixed = jnp.where(masks.own_edge[number], here, beside)
                    moved = lane_roll(mixed, WIDE * j + DEPTH)
                    packed = moved if packed is None else jnp.where(group == j, moved, packed)
                sources[1 + number][i, half] = packed
    for x in range(OWN):
        for half in range(2):
            tile[0][DEPTH + x, half] += sources[0][DEPTH + x, half]
    ahead(functools.partial(forward_step, masks, (*tile, sources[0]), sourced=True), tile[0], saved)


class Masks:
    def __init__(self, kinds):
        lane = lane_id()
        self.first, self.last = lane == 0, lane == LANES - 1
        self.group = lane // WIDE
        upper = sub_id() % 2 == 1
        self.below = jnp.where(upper, VERT / KAPPA, 0.0)
        self.above = jnp.where(upper, 0.0, VERT / KAPPA)
        self.right = [is_right(kind) for kind in kinds]
        half, eighth, sixteenth = lane % WIDE // DEPTH, lane // DEPTH, lane // JOIN
        self.rim = [half == pick(right, 1, 0) for right in self.right]
        self.not_rim = [half == pick(right, 0, 1) for right in self.right]
        self.own_edge = [eighth != pick(right, 0, LANES // DEPTH - 1) for right in self.right]
        self.outer = [sixteenth == pick(right, LANES // JOIN - 1, 0) for right in self.right]

    def vertical(self, pair):
        low = (VERT / KAPPA) * pair[1] + self.below * pltpu.roll(pair[1], 1, 0)
        high = (VERT / KAPPA) * pair[0] + self.above * pltpu.roll(pair[0], SUBLANES - 1, 0)
        return low, high

    def outer_from(self, strips, e, half, value):
        j, i = divmod(e, INNER)
        for strip, outer in zip(strips, self.outer):
            value = jnp.where(outer, lane_roll(strip[i, half], LANES - DEPTH - WIDE * j), value)
        return value

    def join(self, tile, strips, first, last):
        for e in range(first, last + 1):
            j, i = divmod(e, INNER)
            for h in range(2):
                value = self.outer_from(strips, e, h, tile[e, h])
                tile[e, h] = value
                moved = lane_roll(value, WIDE * j + DEPTH)
                for strip, own in zip(strips, self.not_rim):
                    strip[i, h] = jnp.where((self.group == j) & own, moved, strip[i, h])


def slot_b(odd, slot):
    return lax.rem(slot + 6 - 4 * odd, LANES // DEPTH)


def places(odd):
    return DEPTH * (2 - odd), DEPTH * (1 + odd), 3 * DEPTH * (1 - odd), 3 * DEPTH * odd


def merge_strip(masks, number, odd, slot, middle, own_a, own_b, rim_y, rim_a, rim_b):
    first_a = places(odd)[2]
    inner = (masks.group == 1) | (masks.group == 2)
    own = jnp.where(masks.group == 3 * (1 - odd), own_a, own_b)
    own = jnp.where(inner, middle, own)
    rim = jnp.where(lane_id() // DEPTH == slot, rim_a, rim_b)
    rim = lane_roll(rim, 2 * first_a + pick(masks.right[number], DEPTH, 0) + LANES - DEPTH * slot)
    return jnp.where(masks.rim[number], jnp.where(inner, rim_y, rim), own)


def forward_step(masks, tile, first, last, lower=None, upper=None, sourced=True):
    state, keep, from_x, from_y, spread, source = tile
    before = lower or [state[first - 1, h] for h in range(2)]
    here = [state[first, h] for h in range(2)]
    for e in range(first, last + 1):
        after = upper if upper and e == last else [state[e + 1, h] for h in range(2)]
        upright = masks.vertical(here)
        for h in range(2):
            y_high = jnp.where(masks.last, 0.0, lane_roll(here[h], LANES - 1))
            value = (
                keep[e, h] * here[h]
                + from_x[e, h] * before[h]
                + from_y[e, h] * lane_roll(here[h], 1)
                + spread[e, h] * (after[h] + y_high + upright[h])
            )
            state[e, h] = value + source[e, h] if sourced else value
        before, here = here, after


def forward_strips(masks, strips, sourced):
    for strip, keep, from_x, from_y, spread, source in strips:
        old = [strip[0, h] for h in range(2)]
        here = old
        before = [lane_roll(strip[INNER - 1, h], WIDE) for h in range(2)]
        for i in range(INNER):
            if i < INNER - 1:
                after = [strip[i + 1, h] for h in range(2)]
            else:
                after = [lane_roll(value, LANES - WIDE) for value in old]
            upright = masks.vertical(here)
            for h in range(2):
                value = (
                    keep[i, h] * here[h]
                    + from_x[i, h] * before[h]
                    + from_y[i, h] * lane_roll(here[h], 1)
                    + spread[i, h] * (after[h] + lane_roll(here[h], LANES - 1) + upright[h])
                )
                strip[i, h] = value + source[i, h] if sourced else value
            before, here = here, after


def scaled(refs, e, value=None):
    state, _, from_x, from_y, spread, _ = refs
    value = value or [state[e, h] for h in range(2)]
    return (
        value,
        [from_x[e, h] * value[h] for h in range(2)],
        [from_y[e, h] * value[h] for h in range(2)],
        [spread[e, h] * value[h] for h in range(2)],
    )


def adjoint_step(masks, tile, first, last, lower=None, upper=None):
    state, keep, from_x, from_y, spread, total = tile
    before, here = scaled(tile, first - 1, lower), scaled(tile, first)
    for e in range(first, last + 1):
        after = scaled(tile, e + 1, upper if e == last else None)
        value, _, by_y, by_spread = here
        upright = masks.vertical(by_spread)
        for h in range(2):
            y_low = jnp.where(masks.first, 0.0, lane_roll(by_spread[h], 1))
            fresh = (
                keep[e, h] * value[h]
                + (after[1][h] + before[3][h])
                + (y_low + lane_roll(by_y[h], LANES - 1))
                + upright[h]
            )
            state[e, h] = fresh
            if DEPTH <= e < DEPTH + OWN:
                total[e - DEPTH, h] += fresh
        before, here = here, after


def adjoint_strips(masks, strips):
    for refs in strips:
        strip, keep, from_x, from_y, spread, total = refs
        here = scaled(refs, 0)
        wrapped = [lane_roll(value, LANES - WIDE) for value in here[1]]
        last_row = scaled(refs, INNER - 1)
        before = (None, None, None, [lane_roll(value, WIDE) for value in last_row[3]])
        for i in range(INNER):
            after = scaled(refs, i + 1) if i < INNER - 1 else (None, wrapped, None, None)
            value, _, by_y, by_spread = here
            upright = masks.vertical(by_spread)
            for h in range(2):
                fresh = (
                    keep[i, h] * value[h]
                    + (after[1][h] + before[3][h])
                    + (lane_roll(by_spread[h], 1) + lane_roll(by_y[h], LANES - 1))
                    + upright[h]
                )
                strip[i, h] = fresh
                total[i, h] += fresh
            before, here = here, after


def ahead(step, state, saved):
    for t in range(JOIN):
        low, high = DEPTH + 1 + t, DEPTH + OWN - 2 - t
        for h in range(2):
            saved[t, h] = state[low, h]
            saved[t, 2 + h] = state[high, h]
        step(low, high)


def sweep(step, strip_step, join, saved):
    for t in range(ITERS):
        sourced = t < ITERS - 1
        if t == JOIN:
            join(t, EXT - 1 - t)
        if t < JOIN:
            step(t + 1, DEPTH + t, sourced, upper=[saved[t, h] for h in range(2)])
            step(DEPTH + OWN - 1 - t, EXT - 2 - t, sourced, lower=[saved[t, 2 + h] for h in range(2)])
        else:
            step(t + 1, EXT - 2 - t, sourced)
        strip_step(sourced)


def split_refs(refs, *counts):
    out = []
    for count in counts:
        out.append(refs[:count])
        refs = refs[count:]
    return out


def forward_kernel(kinds, tail_count, *refs):
    n = len(kinds)
    ins, got_strips, sources, tile, (edges, saved), outs, strips, out_strips, states = split_refs(
        refs, 4, 3 * n, 1 + n, 5, 2, 5 + 5, 4 * n, 3 * n, n
    )
    monitor, ranking, got_a, got_b = ins
    final, start_a, start_b, objective, start, *tile = outs
    odd = odd_tile()
    masks = Masks(kinds)
    state = tile[0]
    _, _, at_a, at_b = places(odd)
    present = jnp.where(lacks_b(), 0.0, 1.0)
    present_lanes = jnp.where(masks.group == 3 * odd, present, 1.0)
    for x in range(DEPTH):
        for h in range(2):
            raw_a = [planes(got_a.at[field], x, h, DEPTH) for field in range(4)]
            raw_b = [planes(got_b.at[field], x, h, DEPTH) for field in range(4)]
            raw_b[:2] = [value * present for value in raw_b[:2]]
            store_tile(tile, at_a + x, h, raw_a)
            store_tile(tile, at_b + x, h, raw_b)
            i = x
            upper = i // (INNER // 2)
            for k in range(n):
                got = got_strips[3 * k : 3 * k + 3]
                side = pick(masks.right[k], DEPTH, 0)
                raw = [
                    merge_strip(
                        masks,
                        k,
                        odd,
                        4 * upper + field,
                        edges[field, i, h],
                        lane_roll(raw_a[field], 2 * at_a + DEPTH),
                        lane_roll(raw_b[field], 2 * at_b + DEPTH),
                        lane_roll(
                            got[0][i, h], LANES + WIDE + side - 64 * (field // 2) - DEPTH * (field % 2)
                        ),
                        got[1][i % (INNER // 2), h],
                        got[2][i % (INNER // 2), h],
                    )
                    for field in range(4)
                ]
                raw[:2] = [value * present_lanes for value in raw[:2]]
                mine = (states[k], *strips[4 * k : 4 * k + 4])
                for ref, value in zip(mine, (raw[0] + sources[1 + k][i, h], *coefficients(*raw[1:]))):
                    ref[i, h] = value
    for e in (*range(DEPTH), *range(DEPTH + OWN, EXT)):
        for h in range(2):
            state[e, h] += sources[0][e, h]
    strip_refs = [(states[k], *strips[4 * k : 4 * k + 4], sources[1 + k]) for k in range(n)]
    strip_states = [strip[0] for strip in strip_refs]

    def step(first, last, sourced, **beside):
        forward_step(masks, (*tile, sources[0]), first, last, sourced=sourced, **beside)

    sweep(
        step,
        functools.partial(forward_strips, masks, strip_refs),
        functools.partial(masks.join, state, strip_states),
        saved,
    )

    sample = sub_id() // 2
    tail = jnp.zeros((SUBLANES, LANES), jnp.float32)
    for s in range(4):
        tail = jnp.where(sample == s, jnp.where(ranking[s] < tail_count, 1.0, 0.0), tail)
    upper = sub_id() % 2 == 1
    sums = [jnp.zeros((SUBLANES, LANES), jnp.float32) for _ in range(4)]
    for x in range(OWN):
        for h in range(2):
            fresh = masks.outer_from(strip_states, DEPTH + x, h, state[DEPTH + x, h])
            final[pl.ds(h * OWN + x, SUBLANES, stride=2 * OWN), :] = fresh
            low = jnp.broadcast_to(monitor[pl.ds(h * OWN + x, 1), :], (SUBLANES, LANES))
            high = jnp.broadcast_to(monitor[pl.ds((2 + h) * OWN + x, 1), :], (SUBLANES, LANES))
            weighted = tail * jnp.where(upper, high, low) * fresh
            start[DEPTH + x, h] = weighted * (1.0 / (tail_count * ITERS))
            sums[x % 4] = sums[x % 4] + weighted * fresh
    objective[...] = (sums[0] + sums[1]) + (sums[2] + sums[3])

    base_a, base_b, _, _ = places(odd)
    for x in range(DEPTH):
        for h in range(2):
            start_a[x, h] = start[base_a + x, h]
            start_b[x, h] = start[base_b + x, h]
    slot = lane_id() // DEPTH
    for k, kind in enumerate(kinds):
        to_y, to_a, to_b = out_strips[3 * k : 3 * k + 3]
        offset = edge_offset(kind)

        def put(packed, row, h, target):
            moved = lane_roll(start[row, h], DEPTH * target + offset)
            return moved if packed is None else jnp.where(slot == target, moved, packed)

        for i in range(INNER // 2):
            packed = None
            for upper_half in range(2):
                for j in range(2):
                    for h in range(2):
                        row = DEPTH + INNER * j + INNER // 2 * upper_half + i
                        packed = put(packed, row, h, 4 * upper_half + 2 * j + h)
            to_y[i] = packed
        for out, base in ((to_a, base_a), (to_b, base_b)):
            for i in range(INNER // 4):
                packed = None
                for quarter in range(4):
                    for h in range(2):
                        target = 2 * quarter + h
                        target = slot_b(odd, target) if out is to_b else target
                        packed = put(packed, base + INNER // 4 * quarter + i, h, target)
                out[i] = packed


def adjoint_ahead_kernel(*refs):
    coefs, (final, state, total, saved, edges, final_out, sem) = refs[1:5], refs[5:]
    leave = pltpu.make_async_copy(final, final_out, sem)
    leave.start()
    masks = Masks(())
    total[...] = jnp.zeros_like(total)
    first_j = masks.group == 1
    for i in range(INNER):
        for h in range(2):
            moved = [
                lane_roll(state[DEPTH + INNER * j + i, h], WIDE * (j + 1) + DEPTH) for j in range(2)
            ]
            edges[i, h] = jnp.where(first_j, *moved)
    ahead(functools.partial(adjoint_step, masks, (state, *coefs, total)), state, saved)
    leave.wait()


def adjoint_kernel(kinds, scale, *refs):
    n = len(kinds)
    parts, part_strips, (_, _, saved, edges), coefs, strip_coefs, rest, outs, strips, (rows,) = split_refs(
        refs, 2, 3 * n, 4, 4, 4 * n, 3, 3, 2 * n, 1
    )
    objective, wells, profile = rest
    out, state, total = outs
    odd = odd_tile()
    masks = Masks(kinds)
    at = places(odd)[2:]
    for part, first in zip(parts, at):
        for x in range(DEPTH):
            for h in range(2):
                state[first + x, h] = part[x, h]
    strip_refs = []
    for k in range(n):
        strip, strip_total = strips[2 * k : 2 * k + 2]
        got_y, got_a, got_b = part_strips[3 * k : 3 * k + 3]
        side = pick(masks.right[k], DEPTH, 0)
        for i in range(INNER):
            eighth, quarter = divmod(i, INNER // 2)[0], divmod(i, INNER // 4)[0]
            for h in range(2):
                moved = [
                    lane_roll(part[i, h], 2 * first + DEPTH) for part, first in zip(parts, at)
                ]
                beside = merge_strip(
                    masks,
                    k,
                    odd,
                    2 * quarter + h,
                    edges[i, h],
                    moved[0],
                    moved[1],
                    lane_roll(got_y[i % (INNER // 2)], LANES + WIDE + side - 64 * eighth - DEPTH * h),
                    got_a[i % (INNER // 4)],
                    got_b[i % (INNER // 4)],
                )
                strip[i, h] = beside
        strip_refs.append((strip, *strip_coefs[4 * k : 4 * k + 4], strip_total))
        strip_total[...] = jnp.zeros_like(strip_total)

    def step(first, last, _, **beside):
        adjoint_step(masks, (state, *coefs, total), first, last, **beside)

    sweep(
        step,
        lambda _: adjoint_strips(masks, strip_refs),
        functools.partial(masks.join, state, [refs[0] for refs in strip_refs]),
        saved,
    )
    totals = [refs[-1] for refs in strip_refs]
    for x in range(OWN):
        for h in range(2):
            value = masks.outer_from(totals, DEPTH + x, h, total[x, h])
            value = value + pltpu.roll(value, 4, 0)
            value = value + pltpu.roll(value, 2, 0)
            rows[pl.ds((2 * x + h) * 2, 2), :] = value[:2]
    count = rows.shape[0]
    r = lax.broadcasted_iota(jnp.int32, (count, 1), 0)
    layer = (r % 2) * 2 + (r // 2) % 2
    x = lax.axis_index("gx") * OWN + r // 4
    ids = (layer * (OWN * lax.axis_size("gx")) + x) * lax.axis_size("gy") + lax.axis_index("gy")
    field = rows[...]
    high = field.astype(jnp.bfloat16)
    low = (field - high.astype(jnp.float32)).astype(jnp.bfloat16)
    both = jnp.concatenate([high, low], axis=0)
    contract = (((1,), (1,)), ((), ()))
    controls = wells.shape[1]

    def chunk(c, carry):
        span = pl.ds(pl.multiple_of(c * CHUNK, CHUNK), CHUNK)
        share_high, share_low = profile[span, :LANES], profile[span, LANES:]
        first = lax.dot_general(both, share_high, contract, preferred_element_type=jnp.float32)
        second = lax.dot_general(high, share_low, contract, preferred_element_type=jnp.float32)
        product = first[:count] + first[count:] + second
        chosen = jnp.where(ids == wells[:, span], product, 0.0)
        out[:, span] = jnp.sum(chosen, axis=0, keepdims=True)
        return carry

    lax.fori_loop(0, controls // CHUNK, chunk, 0)
    whole = jnp.sum(jnp.sum(objective[...], axis=0, keepdims=True), axis=1, keepdims=True)
    out[:, controls:] = jnp.broadcast_to(whole * scale, (1, LANES))


def shape(*dims):
    return jax.ShapeDtypeStruct(dims, jnp.float32)


def same(x, count):
    return x


def partner_a(x, count):
    return x ^ 1


def partner_b(x, count):
    other = x + 1 if x % 2 else x - 1
    return other if 0 <= other < count else None


AXES = ("gx", "gy", "sa")


def swap_pairs(partner, kind, count_x, count_y, count_s):
    pairs = []
    for x in range(count_x):
        for y in range(count_y):
            for s in range(count_s):
                from_x, from_s = partner(x, count_x), s
                from_y = y if kind == "tile" else 1 - y if kind is None else (y + 1 if kind else y - 1)
                if from_x is None:
                    from_x, from_y, from_s = x, y, s ^ 1
                if 0 <= from_y < count_y:
                    pairs.append(
                        ((from_x * count_y + from_y) * count_s + from_s, (x * count_y + y) * count_s + s)
                    )
    return pairs


def exchange(tiles, strips, kinds):
    counts = [lax.axis_size(axis) for axis in AXES]
    got = [
        lax.ppermute(tile, AXES, swap_pairs(partner, "tile", *counts))
        for tile, partner in zip(tiles, (partner_a, partner_b))
    ]
    got_strips = []
    for k, kind in enumerate(kinds):
        for strip, partner in zip(strips[3 * k : 3 * k + 3], (same, partner_a, partner_b)):
            got_strips.append(lax.ppermute(strip, AXES, swap_pairs(partner, kind, *counts)))
    return got, got_strips


def add_kernel(value, *refs):
    got, (gradient, objective) = refs[:-2], refs[-2:]
    total = value[...] + got[0][...]
    if len(got) == 3:
        total = total + (got[1][...] + got[2][...])
    number = gradient.shape[1]
    gradient[...] = total[:, :number]
    objective[...] = total[:, number : number + 1]


def total_over(value, axes):
    count = 1
    for axis in axes:
        count *= lax.axis_size(axis)
    bit = 1
    while bit < count:
        bits = [bit] if 2 * bit >= count else [bit, 2 * bit, 3 * bit]
        got = [lax.ppermute(value, axes, [(i, i ^ b) for i in range(count)]) for b in bits]
        bit *= 4
        if bit >= count:
            break
        value = value + got[0]
        if len(got) == 3:
            value = value + (got[1] + got[2])
    return pl.pallas_call(
        add_kernel,
        out_shape=(shape(1, value.shape[1] - LANES), shape(1, 1)),
        in_specs=[vmem()] * (1 + len(got)),
        out_specs=(vmem(), vmem()),
        compiler_params=params(),
        name="total",
    )(value, *got)


def local(initial, retard, velx, vely, monitor, controls, profile, wells, ranking):
    samples, layers, width_x, width_y = initial.shape
    count_x, count_y = lax.axis_size("gx"), lax.axis_size("gy")
    assert (samples, layers, width_x, width_y) == (4, 4, OWN, LANES)
    assert count_x % 2 == 0 and lax.axis_size("sa") == 2
    number = controls.shape[0]
    assert number % CHUNK == 0
    kinds = strip_kinds(count_y)
    n = len(kinds)
    half_tile = shape(4, samples, layers, DEPTH, LANES)
    hbm = pl.BlockSpec(memory_space=pltpu.HBM)
    smem = pl.BlockSpec(memory_space=pltpu.SMEM)
    tail_count = samples * lax.axis_size("sa") // 2
    any_space = pl.BlockSpec(memory_space=pl.ANY)
    fields = (initial, retard, velx, vely)

    def in_hbm(values):
        return [pltpu.with_memory_space_constraint(value, pltpu.HBM) for value in values]

    sent = pl.pallas_call(
        rims_kernel,
        out_shape=(half_tile, half_tile),
        in_specs=[hbm] * 4,
        out_specs=(any_space, any_space),
        scratch_shapes=[pltpu.SemaphoreType.DMA((8,))],
        compiler_params=params(),
        name="rims",
    )(*in_hbm(fields))
    own, monitor, controls, wells, *sent_strips = pl.pallas_call(
        functools.partial(strip_pack_kernel, kinds),
        out_shape=(
            shape(4, samples * layers * OWN, LANES),
            shape(layers * OWN, LANES),
            shape(1, number),
            jax.ShapeDtypeStruct((1, number), jnp.int32),
        )
        + (
            shape(INNER, 2, SUBLANES, LANES),
            shape(INNER // 2, 2, SUBLANES, LANES),
            shape(INNER // 2, 2, SUBLANES, LANES),
        )
        * n,
        in_specs=[hbm] * 7,
        out_specs=(vmem(),) * (4 + 3 * n),
        scratch_shapes=[pltpu.SemaphoreType.DMA((7,))],
        compiler_params=params(),
        name="strips",
    )(
        *in_hbm(value.reshape(-1, LANES) for value in (*fields, monitor)),
        *in_hbm(value.reshape(1, -1) for value in (controls, wells)),
    )
    got, got_strips = exchange(sent, sent_strips, kinds)
    tile_shape = shape(EXT, 2, SUBLANES, LANES)
    strip_shape = shape(INNER, 2, SUBLANES, LANES)
    saved_shape = shape(JOIN, 4, SUBLANES, LANES)
    blocks = (1 + n) * EXT * layers
    *prepared, split = pl.pallas_call(
        functools.partial(source_kernel, kinds),
        out_shape=(tile_shape,)
        + (strip_shape,) * n
        + (tile_shape,) * 5
        + (
            shape(4, INNER, 2, SUBLANES, LANES),
            saved_shape,
            jax.ShapeDtypeStruct((number, 2 * LANES), jnp.bfloat16),
        ),
        in_specs=[vmem()] * 4,
        out_specs=(vmem(),) * (1 + n + 5 + 3),
        scratch_shapes=[
            pltpu.VMEM((blocks, 2 * LANES), jnp.float32),
            pltpu.VMEM((blocks, LANES), jnp.float32),
        ],
        compiler_params=params(),
        name="source",
    )(wells, controls, profile, own)
    got = [part.reshape(4, -1, LANES) for part in got]
    half_start = shape(DEPTH, 2, SUBLANES, LANES)
    first_tile = 4 + 3 * n + 1 + n
    final, start_a, start_b, objective, start, *rest = pl.pallas_call(
        functools.partial(forward_kernel, kinds, tail_count),
        out_shape=(
            shape(samples * layers * OWN, LANES),
            half_start,
            half_start,
            shape(SUBLANES, LANES),
            tile_shape,
        )
        + (tile_shape,) * 5
        + (strip_shape,) * (4 * n)
        + (
            shape(INNER // 2, SUBLANES, LANES),
            shape(INNER // 4, SUBLANES, LANES),
            shape(INNER // 4, SUBLANES, LANES),
        )
        * n,
        in_specs=[vmem(), smem] + [vmem()] * (2 + 3 * n + 1 + n + 5 + 2),
        out_specs=(vmem(),) * (5 + 5 + 4 * n + 3 * n),
        scratch_shapes=[pltpu.VMEM((INNER, 2, SUBLANES, LANES), jnp.float32)] * n,
        input_output_aliases={first_tile + k: 5 + k for k in range(5)},
        compiler_params=params(),
        name="forward",
    )(monitor, ranking, *got, *got_strips, *prepared)
    tile, strip_coefs, start_strips = split_refs(rest, 5, 4 * n, 3 * n)
    got_start, got_start_strips = exchange((start_a, start_b), start_strips, kinds)
    *begun, final = pl.pallas_call(
        adjoint_ahead_kernel,
        out_shape=(
            tile_shape,
            shape(OWN, 2, SUBLANES, LANES),
            saved_shape,
            strip_shape,
            shape(*final.shape),
        ),
        in_specs=[vmem()] * 6,
        out_specs=(vmem(),) * 4 + (hbm,),
        scratch_shapes=[pltpu.SemaphoreType.DMA],
        input_output_aliases={0: 0},
        compiler_params=params(),
        name="ahead",
    )(start, *tile[1:], final)
    cells = layers * OWN * count_x * LANES * count_y
    summed, _, _ = pl.pallas_call(
        functools.partial(adjoint_kernel, kinds, 0.5 / (tail_count * cells)),
        out_shape=(
            shape(1, number + LANES),
            tile_shape,
            shape(OWN, 2, SUBLANES, LANES),
        ),
        in_specs=[vmem()] * (2 + 3 * n + 4 + 4 + 4 * n + 3),
        out_specs=(vmem(),) * 3,
        input_output_aliases={2 + 3 * n: 1, 3 + 3 * n: 2},
        scratch_shapes=[pltpu.VMEM((INNER, 2, SUBLANES, LANES), jnp.float32)] * (2 * n)
        + [pltpu.VMEM((OWN * layers, LANES), jnp.float32)],
        compiler_params=params(),
        name="adjoint",
    )(
        *got_start,
        *got_start_strips,
        *begun,
        *tile[1:],
        *strip_coefs,
        objective,
        wells,
        split,
    )
    gradient, objective = total_over(summed, AXES)
    return final.reshape(initial.shape), gradient.reshape(-1), objective.reshape(-1)


def solution(mesh):
    in_specs = (
        P(("groups", "sa"), None, "gx", "gy"),
        P(("groups", "sa"), None, "gx", "gy"),
        P(("groups", "sa"), None, "gx", "gy"),
        P(("groups", "sa"), None, "gx", "gy"),
        P("groups", "gx", "gy"),
        P("groups"),
        P("groups", None),
        P("groups"),
        P(("groups", "sa")),
    )
    out_specs = (P(("groups", "sa"), None, "gx", "gy"), P("groups"), P("groups"))
    return jax.shard_map(local, mesh=mesh, in_specs=in_specs, out_specs=out_specs, check_vma=False)
```

```python
import functools

import jax
import jax.numpy as jnp
from jax import lax
from jax.experimental import pallas as pl
from jax.experimental.pallas import tpu as pltpu
from jax.sharding import PartitionSpec as P

ITERS = 16
KAPPA = 0.1
VERT = 0.05
LANES = 128
SUBLANES = 8
DEPTH = ITERS
OWN = 2 * DEPTH
EXT = OWN + 2 * DEPTH
WIDE = 2 * DEPTH
GROUPS = LANES // WIDE
INNER = EXT // GROUPS
JOIN = ITERS // 2
CHUNK = 4096
VMEM_LIMIT = 24 * 1024 * 1024


def vmem():
    return pl.BlockSpec(memory_space=pltpu.VMEM)


def params():
    return pltpu.CompilerParams(vmem_limit_bytes=VMEM_LIMIT)


def sub_id():
    return lax.broadcasted_iota(jnp.int32, (SUBLANES, LANES), 0)


def lane_id():
    return lax.broadcasted_iota(jnp.int32, (SUBLANES, LANES), 1)


def wrap(shift):
    return shift % LANES if isinstance(shift, int) else lax.rem(shift, LANES)


def lane_roll(value, shift):
    if isinstance(shift, int) and shift % LANES == 0:
        return value
    return pltpu.roll(value, wrap(shift), 1)


def pick(flag, yes, no):
    if isinstance(flag, bool):
        return yes if flag else no
    return jnp.where(flag, yes, no)


def odd_tile():
    return lax.rem(lax.axis_index("gx"), 2)


def lacks_b():
    x = lax.axis_index("gx")
    return (x == 0) | (x == lax.axis_size("gx") - 1)


def strip_kinds(count):
    return (None,) if count == 2 else (True, False)


def is_right(kind):
    return lax.axis_index("gy") == 0 if kind is None else kind


def planes(ref, row, half, rows):
    return ref[pl.ds(half * rows + row, SUBLANES, stride=2 * rows), :]


def copy_all(pairs, sems):
    copies = [pltpu.make_async_copy(*pair, sems.at[k]) for k, pair in enumerate(pairs)]
    for copy in copies:
        copy.start()
    for copy in copies:
        copy.wait()


def rims_kernel(initial, retard, velx, vely, out_a, out_b, sems):
    odd = odd_tile()
    pairs = []
    for field, ref in enumerate((initial, retard, velx, vely)):
        for out, base in ((out_a, DEPTH * (1 - odd)), (out_b, DEPTH * odd)):
            source = ref.at[:, :, pl.ds(pl.multiple_of(base, DEPTH), DEPTH), :]
            pairs.append((source, out.at[field]))
    copy_all(pairs, sems)


def edge_offset(kind):
    return DEPTH * (1 - lax.axis_index("gy")) if kind is None else (0 if kind else DEPTH)


def strip_pack_kernel(kinds, *refs):
    ins, (own, *copied), outs, (sems,) = split_refs(refs, 7, 4, 3 * len(kinds), 1)
    pairs = [(ref, own.at[field]) for field, ref in enumerate(ins[:4])]
    copy_all(pairs + list(zip(ins[4:], copied)), sems)
    odd = odd_tile()
    slot = lane_id() // DEPTH
    for number, kind in enumerate(kinds):
        to_y, to_a, to_b = outs[3 * number : 3 * number + 3]
        offset = edge_offset(kind)

        def put(packed, field, row, half, target):
            moved = lane_roll(planes(own.at[field], row, half, OWN), DEPTH * target + offset)
            return moved if packed is None else jnp.where(slot == target, moved, packed)

        for half in range(2):
            for i in range(INNER):
                packed = None
                for field in range(4):
                    for j in range(2):
                        target = 4 * (field // 2) + 2 * j + field % 2
                        packed = put(packed, field, INNER * j + i, half, target)
                to_y[i, half] = packed
            for out, base in ((to_a, DEPTH * (1 - odd)), (to_b, DEPTH * odd)):
                for i in range(INNER // 2):
                    packed = None
                    for field in range(4):
                        for upper in range(2):
                            row = base + INNER // 2 * upper + i
                            target = 4 * upper + field
                            target = slot_b(odd, target) if out is to_b else target
                            packed = put(packed, field, row, half, target)
                    out[i, half] = packed


def over_chunks(number, chunk):
    if number == CHUNK:
        chunk(0, 0)
    else:
        lax.fori_loop(0, number // CHUNK, chunk, 0)


def coefficients(retard, velx, vely):
    spread = KAPPA * retard
    from_x = retard * velx + spread
    from_y = retard * vely + spread
    keep = 1.0 - (from_x + from_y + (2.0 + 2.0 * VERT / KAPPA) * spread)
    return keep, from_x, from_y, spread


def store_tile(refs, row, half, raw, source=None):
    state, retard, velx, vely = raw
    keep, from_x, from_y, spread = coefficients(retard, velx, vely)
    from_y = jnp.where(lane_id() == 0, 0.0, from_y)
    for ref, value in zip(refs, (state, keep, from_x, from_y, spread)):
        ref[row, half] = value


def source_kernel(kinds, wells, controls, profile, own, *refs):
    n = len(kinds)
    sources, tile, edges, (saved, split), (acc, acc_low) = split_refs(refs, 1 + n, 5, 1, 2, 2)
    for x in range(OWN):
        for half in range(2):
            raw = [planes(own.at[field], x, half, OWN) for field in range(4)]
            store_tile(tile, DEPTH + x, half, raw)
    first_j = lane_id() // WIDE == 1
    for field in range(4):
        for i in range(INNER):
            for half in range(2):
                moved = [
                    lane_roll(planes(own.at[field], INNER * j + i, half, OWN), WIDE * (j + 1) + DEPTH)
                    for j in range(2)
                ]
                edges[0][field, i, half] = jnp.where(first_j, *moved)

    x_index, y_index = lax.axis_index("gx"), lax.axis_index("gy")
    all_x, all_blocks = OWN * lax.axis_size("gx"), lax.axis_size("gy")
    layers = 4
    per_block = EXT * layers
    r = lax.broadcasted_iota(jnp.int32, (per_block, 1), 0)
    x = x_index * OWN - DEPTH + r // layers
    ids = []
    for block in [y_index] + [
        1 - y_index if kind is None else (y_index + 1 if kind else y_index - 1) for kind in kinds
    ]:
        inside = (x >= 0) & (x < all_x) & (block >= 0) & (block < all_blocks)
        ids.append(jnp.where(inside, ((r % layers) * all_x + x) * all_blocks + block, -1))
    ids = jnp.concatenate(ids, axis=0)
    acc[...] = jnp.zeros_like(acc)
    acc_low[...] = jnp.zeros_like(acc_low)

    def chunk(c, carry):
        span = pl.ds(c * CHUNK if isinstance(c, int) else pl.multiple_of(c * CHUNK, CHUNK), CHUNK)
        part = profile[span, :]
        high = part.astype(jnp.bfloat16)
        low = (part - high.astype(jnp.float32)).astype(jnp.bfloat16)
        rate = controls[:, span]
        rate_high = rate.astype(jnp.bfloat16).astype(jnp.float32)
        hit = ids == wells[:, span]
        hot_high = jnp.where(hit, rate_high, 0.0).astype(jnp.bfloat16)
        hot_low = jnp.where(hit, rate - rate_high, 0.0).astype(jnp.bfloat16)
        split_part = jnp.concatenate([high, low], axis=1)
        split[span, :] = split_part
        acc[...] += jnp.dot(hot_high, split_part, preferred_element_type=jnp.float32)
        acc_low[...] += jnp.dot(hot_low, high, preferred_element_type=jnp.float32)
        return carry

    over_chunks(wells.shape[1], chunk)
    acc_low[...] += acc[:, :LANES] + acc[:, LANES:]
    upper = sub_id() % 2 == 1
    group = lane_id() // WIDE

    def both(first, half):
        low_layer = jnp.broadcast_to(acc_low[pl.ds(first + half, 1), :], (SUBLANES, LANES))
        high_layer = jnp.broadcast_to(acc_low[pl.ds(first + 2 + half, 1), :], (SUBLANES, LANES))
        return jnp.where(upper, high_layer, low_layer)

    masks = Masks(kinds)
    for number in range(n):
        for i in range(INNER):
            for half in range(2):
                packed = None
                for j in range(GROUPS):
                    e = j * INNER + i
                    here = both(e * layers, half)
                    if number == 0:
                        sources[0][e, half] = here
                    beside = both((number + 1) * per_block + e * layers, half)
                    mixed = jnp.where(masks.own_edge[number], here, beside)
                    moved = lane_roll(mixed, WIDE * j + DEPTH)
                    packed = moved if packed is None else jnp.where(group == j, moved, packed)
                sources[1 + number][i, half] = packed
    for x in range(OWN):
        for half in range(2):
            tile[0][DEPTH + x, half] += sources[0][DEPTH + x, half]
    ahead(functools.partial(forward_step, masks, (*tile, sources[0]), sourced=True), tile[0], saved)


class Masks:
    def __init__(self, kinds):
        lane = lane_id()
        self.first, self.last = lane == 0, lane == LANES - 1
        self.group = lane // WIDE
        upper = sub_id() % 2 == 1
        self.below = jnp.where(upper, VERT / KAPPA, 0.0)
        self.above = jnp.where(upper, 0.0, VERT / KAPPA)
        self.right = [is_right(kind) for kind in kinds]
        half, eighth, sixteenth = lane % WIDE // DEPTH, lane // DEPTH, lane // JOIN
        self.rim = [half == pick(right, 1, 0) for right in self.right]
        self.not_rim = [half == pick(right, 0, 1) for right in self.right]
        self.own_edge = [eighth != pick(right, 0, LANES // DEPTH - 1) for right in self.right]
        self.outer = [sixteenth == pick(right, LANES // JOIN - 1, 0) for right in self.right]

    def vertical(self, pair):
        low = (VERT / KAPPA) * pair[1] + self.below * pltpu.roll(pair[1], 1, 0)
        high = (VERT / KAPPA) * pair[0] + self.above * pltpu.roll(pair[0], SUBLANES - 1, 0)
        return low, high

    def outer_from(self, strips, e, half, value):
        j, i = divmod(e, INNER)
        for strip, outer in zip(strips, self.outer):
            value = jnp.where(outer, lane_roll(strip[i, half], LANES - DEPTH - WIDE * j), value)
        return value

    def join(self, tile, strips, first, last):
        for e in range(first, last + 1):
            j, i = divmod(e, INNER)
            for h in range(2):
                value = self.outer_from(strips, e, h, tile[e, h])
                tile[e, h] = value
                moved = lane_roll(value, WIDE * j + DEPTH)
                for strip, own in zip(strips, self.not_rim):
                    strip[i, h] = jnp.where((self.group == j) & own, moved, strip[i, h])


def slot_b(odd, slot):
    return lax.rem(slot + 6 - 4 * odd, LANES // DEPTH)


def places(odd):
    return DEPTH * (2 - odd), DEPTH * (1 + odd), 3 * DEPTH * (1 - odd), 3 * DEPTH * odd


def merge_strip(masks, number, odd, slot, middle, own_a, own_b, rim_y, rim_a, rim_b):
    first_a = places(odd)[2]
    inner = (masks.group == 1) | (masks.group == 2)
    own = jnp.where(masks.group == 3 * (1 - odd), own_a, own_b)
    own = jnp.where(inner, middle, own)
    rim = jnp.where(lane_id() // DEPTH == slot, rim_a, rim_b)
    rim = lane_roll(rim, 2 * first_a + pick(masks.right[number], DEPTH, 0) + LANES - DEPTH * slot)
    return jnp.where(masks.rim[number], jnp.where(inner, rim_y, rim), own)


def forward_step(masks, tile, first, last, lower=None, upper=None, sourced=True):
    state, keep, from_x, from_y, spread, source = tile
    before = lower or [state[first - 1, h] for h in range(2)]
    here = [state[first, h] for h in range(2)]
    for e in range(first, last + 1):
        after = upper if upper and e == last else [state[e + 1, h] for h in range(2)]
        upright = masks.vertical(here)
        for h in range(2):
            y_high = jnp.where(masks.last, 0.0, lane_roll(here[h], LANES - 1))
            value = (
                keep[e, h] * here[h]
                + from_x[e, h] * before[h]
                + from_y[e, h] * lane_roll(here[h], 1)
                + spread[e, h] * (after[h] + y_high + upright[h])
            )
            state[e, h] = value + source[e, h] if sourced else value
        before, here = here, after


def forward_strips(masks, strips, sourced):
    for strip, keep, from_x, from_y, spread, source in strips:
        old = [strip[0, h] for h in range(2)]
        here = old
        before = [lane_roll(strip[INNER - 1, h], WIDE) for h in range(2)]
        for i in range(INNER):
            if i < INNER - 1:
                after = [strip[i + 1, h] for h in range(2)]
            else:
                after = [lane_roll(value, LANES - WIDE) for value in old]
            upright = masks.vertical(here)
            for h in range(2):
                value = (
                    keep[i, h] * here[h]
                    + from_x[i, h] * before[h]
                    + from_y[i, h] * lane_roll(here[h], 1)
                    + spread[i, h] * (after[h] + lane_roll(here[h], LANES - 1) + upright[h])
                )
                strip[i, h] = value + source[i, h] if sourced else value
            before, here = here, after


def scaled(refs, e, value=None):
    state, _, from_x, from_y, spread, _ = refs
    value = value or [state[e, h] for h in range(2)]
    return (
        value,
        [from_x[e, h] * value[h] for h in range(2)],
        [from_y[e, h] * value[h] for h in range(2)],
        [spread[e, h] * value[h] for h in range(2)],
    )


def adjoint_step(masks, tile, first, last, lower=None, upper=None):
    state, keep, from_x, from_y, spread, total = tile
    before, here = scaled(tile, first - 1, lower), scaled(tile, first)
    for e in range(first, last + 1):
        after = scaled(tile, e + 1, upper if e == last else None)
        value, _, by_y, by_spread = here
        upright = masks.vertical(by_spread)
        for h in range(2):
            y_low = jnp.where(masks.first, 0.0, lane_roll(by_spread[h], 1))
            fresh = (
                keep[e, h] * value[h]
                + (after[1][h] + before[3][h])
                + (y_low + lane_roll(by_y[h], LANES - 1))
                + upright[h]
            )
            state[e, h] = fresh
            if DEPTH <= e < DEPTH + OWN:
                total[e - DEPTH, h] += fresh
        before, here = here, after


def adjoint_strips(masks, strips):
    for refs in strips:
        strip, keep, from_x, from_y, spread, total = refs
        here = scaled(refs, 0)
        wrapped = [lane_roll(value, LANES - WIDE) for value in here[1]]
        last_row = scaled(refs, INNER - 1)
        before = (None, None, None, [lane_roll(value, WIDE) for value in last_row[3]])
        for i in range(INNER):
            after = scaled(refs, i + 1) if i < INNER - 1 else (None, wrapped, None, None)
            value, _, by_y, by_spread = here
            upright = masks.vertical(by_spread)
            for h in range(2):
                fresh = (
                    keep[i, h] * value[h]
                    + (after[1][h] + before[3][h])
                    + (lane_roll(by_spread[h], 1) + lane_roll(by_y[h], LANES - 1))
                    + upright[h]
                )
                strip[i, h] = fresh
                total[i, h] += fresh
            before, here = here, after


def ahead(step, state, saved):
    for t in range(JOIN):
        low, high = DEPTH + 1 + t, DEPTH + OWN - 2 - t
        for h in range(2):
            saved[t, h] = state[low, h]
            saved[t, 2 + h] = state[high, h]
        step(low, high)


def sweep(step, strip_step, join, saved):
    for t in range(ITERS):
        sourced = t < ITERS - 1
        if t == JOIN:
            join(t, EXT - 1 - t)
        if t < JOIN:
            step(t + 1, DEPTH + t, sourced, upper=[saved[t, h] for h in range(2)])
            step(DEPTH + OWN - 1 - t, EXT - 2 - t, sourced, lower=[saved[t, 2 + h] for h in range(2)])
        else:
            step(t + 1, EXT - 2 - t, sourced)
        strip_step(sourced)


def split_refs(refs, *counts):
    out = []
    for count in counts:
        out.append(refs[:count])
        refs = refs[count:]
    return out


def forward_kernel(kinds, tail_count, *refs):
    n = len(kinds)
    ins, got_strips, sources, tile, (edges, saved), outs, strips, out_strips, states = split_refs(
        refs, 4, 3 * n, 1 + n, 5, 2, 5 + 5, 4 * n, 3 * n, n
    )
    monitor, ranking, got_a, got_b = ins
    final, start_a, start_b, objective, start, *tile = outs
    odd = odd_tile()
    masks = Masks(kinds)
    state = tile[0]
    _, _, at_a, at_b = places(odd)
    present = jnp.where(lacks_b(), 0.0, 1.0)
    present_lanes = jnp.where(masks.group == 3 * odd, present, 1.0)
    for x in range(DEPTH):
        for h in range(2):
            raw_a = [planes(got_a.at[field], x, h, DEPTH) for field in range(4)]
            raw_b = [planes(got_b.at[field], x, h, DEPTH) for field in range(4)]
            raw_b[:2] = [value * present for value in raw_b[:2]]
            store_tile(tile, at_a + x, h, raw_a)
            store_tile(tile, at_b + x, h, raw_b)
            i = x
            upper = i // (INNER // 2)
            for k in range(n):
                got = got_strips[3 * k : 3 * k + 3]
                side = pick(masks.right[k], DEPTH, 0)
                raw = [
                    merge_strip(
                        masks,
                        k,
                        odd,
                        4 * upper + field,
                        edges[field, i, h],
                        lane_roll(raw_a[field], 2 * at_a + DEPTH),
                        lane_roll(raw_b[field], 2 * at_b + DEPTH),
                        lane_roll(
                            got[0][i, h], LANES + WIDE + side - 64 * (field // 2) - DEPTH * (field % 2)
                        ),
                        got[1][i % (INNER // 2), h],
                        got[2][i % (INNER // 2), h],
                    )
                    for field in range(4)
                ]
                raw[:2] = [value * present_lanes for value in raw[:2]]
                mine = (states[k], *strips[4 * k : 4 * k + 4])
                for ref, value in zip(mine, (raw[0] + sources[1 + k][i, h], *coefficients(*raw[1:]))):
                    ref[i, h] = value
    for e in (*range(DEPTH), *range(DEPTH + OWN, EXT)):
        for h in range(2):
            state[e, h] += sources[0][e, h]
    strip_refs = [(states[k], *strips[4 * k : 4 * k + 4], sources[1 + k]) for k in range(n)]
    strip_states = [strip[0] for strip in strip_refs]

    def step(first, last, sourced, **beside):
        forward_step(masks, (*tile, sources[0]), first, last, sourced=sourced, **beside)

    sweep(
        step,
        functools.partial(forward_strips, masks, strip_refs),
        functools.partial(masks.join, state, strip_states),
        saved,
    )

    sample = sub_id() // 2
    tail = jnp.zeros((SUBLANES, LANES), jnp.float32)
    for s in range(4):
        tail = jnp.where(sample == s, jnp.where(ranking[s] < tail_count, 1.0, 0.0), tail)
    upper = sub_id() % 2 == 1
    sums = [jnp.zeros((SUBLANES, LANES), jnp.float32) for _ in range(4)]
    for x in range(OWN):
        for h in range(2):
            fresh = masks.outer_from(strip_states, DEPTH + x, h, state[DEPTH + x, h])
            final[pl.ds(h * OWN + x, SUBLANES, stride=2 * OWN), :] = fresh
            low = jnp.broadcast_to(monitor[pl.ds(h * OWN + x, 1), :], (SUBLANES, LANES))
            high = jnp.broadcast_to(monitor[pl.ds((2 + h) * OWN + x, 1), :], (SUBLANES, LANES))
            weighted = tail * jnp.where(upper, high, low) * fresh
            start[DEPTH + x, h] = weighted * (1.0 / (tail_count * ITERS))
            sums[x % 4] = sums[x % 4] + weighted * fresh
    objective[...] = (sums[0] + sums[1]) + (sums[2] + sums[3])

    base_a, base_b, _, _ = places(odd)
    for x in range(DEPTH):
        for h in range(2):
            start_a[x, h] = start[base_a + x, h]
            start_b[x, h] = start[base_b + x, h]
    slot = lane_id() // DEPTH
    for k, kind in enumerate(kinds):
        to_y, to_a, to_b = out_strips[3 * k : 3 * k + 3]
        offset = edge_offset(kind)

        def put(packed, row, h, target):
            moved = lane_roll(start[row, h], DEPTH * target + offset)
            return moved if packed is None else jnp.where(slot == target, moved, packed)

        for i in range(INNER // 2):
            packed = None
            for upper_half in range(2):
                for j in range(2):
                    for h in range(2):
                        row = DEPTH + INNER * j + INNER // 2 * upper_half + i
                        packed = put(packed, row, h, 4 * upper_half + 2 * j + h)
            to_y[i] = packed
        for out, base in ((to_a, base_a), (to_b, base_b)):
            for i in range(INNER // 4):
                packed = None
                for quarter in range(4):
                    for h in range(2):
                        target = 2 * quarter + h
                        target = slot_b(odd, target) if out is to_b else target
                        packed = put(packed, base + INNER // 4 * quarter + i, h, target)
                out[i] = packed


def adjoint_ahead_kernel(*refs):
    coefs, (final, state, total, saved, edges, final_out, sem) = refs[1:5], refs[5:]
    leave = pltpu.make_async_copy(final, final_out, sem)
    leave.start()
    masks = Masks(())
    total[...] = jnp.zeros_like(total)
    first_j = masks.group == 1
    for i in range(INNER):
        for h in range(2):
            moved = [
                lane_roll(state[DEPTH + INNER * j + i, h], WIDE * (j + 1) + DEPTH) for j in range(2)
            ]
            edges[i, h] = jnp.where(first_j, *moved)
    ahead(functools.partial(adjoint_step, masks, (state, *coefs, total)), state, saved)
    leave.wait()


def adjoint_kernel(kinds, scale, *refs):
    n = len(kinds)
    parts, part_strips, (_, _, saved, edges), coefs, strip_coefs, rest, outs, strips, (rows,) = split_refs(
        refs, 2, 3 * n, 4, 4, 4 * n, 3, 3, 2 * n, 1
    )
    objective, wells, profile = rest
    out, state, total = outs
    odd = odd_tile()
    masks = Masks(kinds)
    whole = jnp.sum(jnp.sum(objective[...], axis=0, keepdims=True), axis=1, keepdims=True)
    out[:, wells.shape[1] :] = jnp.broadcast_to(whole * scale, (1, LANES))
    at = places(odd)[2:]
    for part, first in zip(parts, at):
        for x in range(DEPTH):
            for h in range(2):
                state[first + x, h] = part[x, h]
    strip_refs = []
    for k in range(n):
        strip, strip_total = strips[2 * k : 2 * k + 2]
        got_y, got_a, got_b = part_strips[3 * k : 3 * k + 3]
        side = pick(masks.right[k], DEPTH, 0)
        for i in range(INNER):
            eighth, quarter = divmod(i, INNER // 2)[0], divmod(i, INNER // 4)[0]
            for h in range(2):
                moved = [
                    lane_roll(part[i, h], 2 * first + DEPTH) for part, first in zip(parts, at)
                ]
                beside = merge_strip(
                    masks,
                    k,
                    odd,
                    2 * quarter + h,
                    edges[i, h],
                    moved[0],
                    moved[1],
                    lane_roll(got_y[i % (INNER // 2)], LANES + WIDE + side - 64 * eighth - DEPTH * h),
                    got_a[i % (INNER // 4)],
                    got_b[i % (INNER // 4)],
                )
                strip[i, h] = beside
        strip_refs.append((strip, *strip_coefs[4 * k : 4 * k + 4], strip_total))
        strip_total[...] = jnp.zeros_like(strip_total)

    def step(first, last, _, **beside):
        adjoint_step(masks, (state, *coefs, total), first, last, **beside)

    sweep(
        step,
        lambda _: adjoint_strips(masks, strip_refs),
        functools.partial(masks.join, state, [refs[0] for refs in strip_refs]),
        saved,
    )
    totals = [refs[-1] for refs in strip_refs]
    for x in range(OWN):
        for h in range(2):
            value = masks.outer_from(totals, DEPTH + x, h, total[x, h])
            value = value + pltpu.roll(value, 4, 0)
            value = value + pltpu.roll(value, 2, 0)
            rows[pl.ds((2 * x + h) * 2, 2), :] = value[:2]
    count = rows.shape[0]
    r = lax.broadcasted_iota(jnp.int32, (count, 1), 0)
    layer = (r % 2) * 2 + (r // 2) % 2
    x = lax.axis_index("gx") * OWN + r // 4
    ids = (layer * (OWN * lax.axis_size("gx")) + x) * lax.axis_size("gy") + lax.axis_index("gy")
    field = rows[...]
    high = field.astype(jnp.bfloat16)
    low = (field - high.astype(jnp.float32)).astype(jnp.bfloat16)
    both = jnp.concatenate([high, low], axis=0)
    contract = (((1,), (1,)), ((), ()))
    controls = wells.shape[1]

    def chunk(c, carry):
        span = pl.ds(c * CHUNK if isinstance(c, int) else pl.multiple_of(c * CHUNK, CHUNK), CHUNK)
        share_high, share_low = profile[span, :LANES], profile[span, LANES:]
        first = lax.dot_general(both, share_high, contract, preferred_element_type=jnp.float32)
        second = lax.dot_general(high, share_low, contract, preferred_element_type=jnp.float32)
        product = first[:count] + first[count:] + second
        chosen = jnp.where(ids == wells[:, span], product, 0.0)
        out[:, span] = jnp.sum(chosen, axis=0, keepdims=True)
        return carry

    over_chunks(controls, chunk)


def shape(*dims):
    return jax.ShapeDtypeStruct(dims, jnp.float32)


def same(x, count):
    return x


def partner_a(x, count):
    return x ^ 1


def partner_b(x, count):
    other = x + 1 if x % 2 else x - 1
    return other if 0 <= other < count else None


AXES = ("gx", "gy", "sa")


def swap_pairs(partner, kind, count_x, count_y, count_s):
    pairs = []
    for x in range(count_x):
        for y in range(count_y):
            for s in range(count_s):
                from_x, from_s = partner(x, count_x), s
                from_y = y if kind == "tile" else 1 - y if kind is None else (y + 1 if kind else y - 1)
                if from_x is None:
                    from_x, from_y, from_s = x, y, s ^ 1
                if 0 <= from_y < count_y:
                    pairs.append(
                        ((from_x * count_y + from_y) * count_s + from_s, (x * count_y + y) * count_s + s)
                    )
    return pairs


def exchange(tiles, strips, kinds):
    counts = [lax.axis_size(axis) for axis in AXES]
    got = [
        lax.ppermute(tile, AXES, swap_pairs(partner, "tile", *counts))
        for tile, partner in zip(tiles, (partner_a, partner_b))
    ]
    got_strips = []
    for k, kind in enumerate(kinds):
        for strip, partner in zip(strips[3 * k : 3 * k + 3], (same, partner_a, partner_b)):
            got_strips.append(lax.ppermute(strip, AXES, swap_pairs(partner, kind, *counts)))
    return got, got_strips


def add_kernel(value, *refs):
    got, (gradient, objective) = refs[:-2], refs[-2:]
    total = value[...] + got[0][...]
    if len(got) == 3:
        total = total + (got[1][...] + got[2][...])
    number = gradient.shape[1]
    gradient[...] = total[:, :number]
    objective[...] = total[:, number : number + 1]


def total_over(value, axes):
    count = 1
    for axis in axes:
        count *= lax.axis_size(axis)
    bit = 1
    while bit < count:
        bits = [bit] if 2 * bit >= count else [bit, 2 * bit, 3 * bit]
        got = [lax.ppermute(value, axes, [(i, i ^ b) for i in range(count)]) for b in bits]
        bit *= 4
        if bit >= count:
            break
        value = value + got[0]
        if len(got) == 3:
            value = value + (got[1] + got[2])
    return pl.pallas_call(
        add_kernel,
        out_shape=(shape(1, value.shape[1] - LANES), shape(1, 1)),
        in_specs=[vmem()] * (1 + len(got)),
        out_specs=(vmem(), vmem()),
        compiler_params=params(),
        name="total",
    )(value, *got)


def local(initial, retard, velx, vely, monitor, controls, profile, wells, ranking):
    samples, layers, width_x, width_y = initial.shape
    count_x, count_y = lax.axis_size("gx"), lax.axis_size("gy")
    assert (samples, layers, width_x, width_y) == (4, 4, OWN, LANES)
    assert count_x % 2 == 0 and lax.axis_size("sa") == 2
    number = controls.shape[0]
    assert number % CHUNK == 0
    kinds = strip_kinds(count_y)
    n = len(kinds)
    half_tile = shape(4, samples, layers, DEPTH, LANES)
    hbm = pl.BlockSpec(memory_space=pltpu.HBM)
    smem = pl.BlockSpec(memory_space=pltpu.SMEM)
    tail_count = samples * lax.axis_size("sa") // 2
    any_space = pl.BlockSpec(memory_space=pl.ANY)
    fields = (initial, retard, velx, vely)

    def in_hbm(values):
        return [pltpu.with_memory_space_constraint(value, pltpu.HBM) for value in values]

    sent = pl.pallas_call(
        rims_kernel,
        out_shape=(half_tile, half_tile),
        in_specs=[hbm] * 4,
        out_specs=(any_space, any_space),
        scratch_shapes=[pltpu.SemaphoreType.DMA((8,))],
        compiler_params=params(),
        name="rims",
    )(*in_hbm(fields))
    own, monitor, controls, wells, *sent_strips = pl.pallas_call(
        functools.partial(strip_pack_kernel, kinds),
        out_shape=(
            shape(4, samples * layers * OWN, LANES),
            shape(layers * OWN, LANES),
            shape(1, number),
            jax.ShapeDtypeStruct((1, number), jnp.int32),
        )
        + (
            shape(INNER, 2, SUBLANES, LANES),
            shape(INNER // 2, 2, SUBLANES, LANES),
            shape(INNER // 2, 2, SUBLANES, LANES),
        )
        * n,
        in_specs=[hbm] * 7,
        out_specs=(vmem(),) * (4 + 3 * n),
        scratch_shapes=[pltpu.SemaphoreType.DMA((7,))],
        compiler_params=params(),
        name="strips",
    )(
        *in_hbm(value.reshape(-1, LANES) for value in (*fields, monitor)),
        *in_hbm(value.reshape(1, -1) for value in (controls, wells)),
    )
    got, got_strips = exchange(sent, sent_strips, kinds)
    tile_shape = shape(EXT, 2, SUBLANES, LANES)
    strip_shape = shape(INNER, 2, SUBLANES, LANES)
    saved_shape = shape(JOIN, 4, SUBLANES, LANES)
    blocks = (1 + n) * EXT * layers
    *prepared, split = pl.pallas_call(
        functools.partial(source_kernel, kinds),
        out_shape=(tile_shape,)
        + (strip_shape,) * n
        + (tile_shape,) * 5
        + (
            shape(4, INNER, 2, SUBLANES, LANES),
            saved_shape,
            jax.ShapeDtypeStruct((number, 2 * LANES), jnp.bfloat16),
        ),
        in_specs=[vmem()] * 4,
        out_specs=(vmem(),) * (1 + n + 5 + 3),
        scratch_shapes=[
            pltpu.VMEM((blocks, 2 * LANES), jnp.float32),
            pltpu.VMEM((blocks, LANES), jnp.float32),
        ],
        compiler_params=params(),
        name="source",
    )(wells, controls, profile, own)
    got = [part.reshape(4, -1, LANES) for part in got]
    half_start = shape(DEPTH, 2, SUBLANES, LANES)
    first_tile = 4 + 3 * n + 1 + n
    final, start_a, start_b, objective, start, *rest = pl.pallas_call(
        functools.partial(forward_kernel, kinds, tail_count),
        out_shape=(
            shape(samples * layers * OWN, LANES),
            half_start,
            half_start,
            shape(SUBLANES, LANES),
            tile_shape,
        )
        + (tile_shape,) * 5
        + (strip_shape,) * (4 * n)
        + (
            shape(INNER // 2, SUBLANES, LANES),
            shape(INNER // 4, SUBLANES, LANES),
            shape(INNER // 4, SUBLANES, LANES),
        )
        * n,
        in_specs=[vmem(), smem] + [vmem()] * (2 + 3 * n + 1 + n + 5 + 2),
        out_specs=(vmem(),) * (5 + 5 + 4 * n + 3 * n),
        scratch_shapes=[pltpu.VMEM((INNER, 2, SUBLANES, LANES), jnp.float32)] * n,
        input_output_aliases={first_tile + k: 5 + k for k in range(5)},
        compiler_params=params(),
        name="forward",
    )(monitor, ranking, *got, *got_strips, *prepared)
    tile, strip_coefs, start_strips = split_refs(rest, 5, 4 * n, 3 * n)
    got_start, got_start_strips = exchange((start_a, start_b), start_strips, kinds)
    *begun, final = pl.pallas_call(
        adjoint_ahead_kernel,
        out_shape=(
            tile_shape,
            shape(OWN, 2, SUBLANES, LANES),
            saved_shape,
            strip_shape,
            shape(*final.shape),
        ),
        in_specs=[vmem()] * 6,
        out_specs=(vmem(),) * 4 + (hbm,),
        scratch_shapes=[pltpu.SemaphoreType.DMA],
        input_output_aliases={0: 0},
        compiler_params=params(),
        name="ahead",
    )(start, *tile[1:], final)
    cells = layers * OWN * count_x * LANES * count_y
    summed, _, _ = pl.pallas_call(
        functools.partial(adjoint_kernel, kinds, 0.5 / (tail_count * cells)),
        out_shape=(
            shape(1, number + LANES),
            tile_shape,
            shape(OWN, 2, SUBLANES, LANES),
        ),
        in_specs=[vmem()] * (2 + 3 * n + 4 + 4 + 4 * n + 3),
        out_specs=(vmem(),) * 3,
        input_output_aliases={2 + 3 * n: 1, 3 + 3 * n: 2},
        scratch_shapes=[pltpu.VMEM((INNER, 2, SUBLANES, LANES), jnp.float32)] * (2 * n)
        + [pltpu.VMEM((OWN * layers, LANES), jnp.float32)],
        compiler_params=params(),
        name="adjoint",
    )(
        *got_start,
        *got_start_strips,
        *begun,
        *tile[1:],
        *strip_coefs,
        objective,
        wells,
        split,
    )
    gradient, objective = total_over(summed, AXES)
    return final.reshape(initial.shape), gradient.reshape(-1), objective.reshape(-1)


def solution(mesh):
    in_specs = (
        P(("groups", "sa"), None, "gx", "gy"),
        P(("groups", "sa"), None, "gx", "gy"),
        P(("groups", "sa"), None, "gx", "gy"),
        P(("groups", "sa"), None, "gx", "gy"),
        P("groups", "gx", "gy"),
        P("groups"),
        P("groups", None),
        P("groups"),
        P(("groups", "sa")),
    )
    out_specs = (P(("groups", "sa"), None, "gx", "gy"), P("groups"), P("groups"))
    return jax.shard_map(local, mesh=mesh, in_specs=in_specs, out_specs=out_specs, check_vma=False)
```
